128 devices in a mesh: feat: 32 (over y_hi, z, x), dp: 4 (over y_lo, core).
Axes of the slice: x: 4, y: 4 (y_hi: 2, y_lo: 2; y = y_hi * 2 + y_lo), z: 4, core: 2. Of those that a mesh axis runs over, the one named last changes fastest.
Arguments:
- tokens: bfloat16 [1024, 65536], P('dp', 'feat'), may hold values from -6 to 6
- weights: bfloat16 [9, 256, 256, 256], P(None, 'feat'), may hold values from -0.125 to 0.125
- order: int32 [8], replicated, may hold values from 0 to 7, each once
- mask: int32 [8, 256], P(None, 'feat'), may hold values 0 or 1
- low_u: bfloat16 [65536, 128], P('feat'), may hold values from -0.0234375 to 0.0234375
- low_v: bfloat16 [128, 65536], P(None, 'feat'), may hold values from -0.5 to 0.5
- cotangent: bfloat16 [1024, 65536], P('dp', 'feat'), may hold values from -6 to 6
Outputs:
- output: bfloat16 [1024, 65536], P('dp', 'feat')
- grad_tokens: bfloat16 [1024, 65536], P('dp', 'feat')
- grad_weights: bfloat16 [9, 256, 256, 256], P(None, 'feat', 'dp')
- grad_u: bfloat16 [65536, 128], P(('feat', 'dp'))
- grad_v: bfloat16 [128, 65536], P(None, ('feat', 'dp'))
The draws below stay inside these ranges and needn't reach their ends.
All inputs are finite; a program needn't handle non-finite values. No bound on the sum of `mask` on one device may be relied on, other than what follows from the above.
Results may differ from the reference program's by a relative error of at most 0.0065.
Values may be sent and summed in bfloat16 or wider, within the bound.
No kernel may reach another device: no remote copies, remote signals or barrier semaphores. Data moves between devices by JAX's collectives and lax.ppermute only.
A program may use at most 192 MiB of HBM per device.

```python
import jax
import jax.numpy as jnp
from jax import lax

B = 256
LEVELS = 8
R = 128
TOK_DEV = 256
NB = 256
W = 65536
TOKENS = 1024
N_DP = 4


def place_ends(values, own_key, low, largest):
    shape = values.shape
    place = [jax.random.randint(jax.random.fold_in(own_key, axis), (), 0, shape[axis]) for axis in range(len(shape))]
    values = values.at[tuple(place)].set(low)
    longest = shape.index(max(shape))
    place[longest] = (place[longest] + 1) % shape[longest]
    return values.at[tuple(place)].set(largest)


def block_levels(key, extent, split, smallest, high):
    factor_of, own = 1.0, jax.random.fold_in(key, 6)
    for axis_at, blocks in split:
        steps = jnp.exp(jax.random.uniform(jax.random.fold_in(own, axis_at), (blocks,), jnp.float32, smallest / len(split), high / len(split)))
        factor_of = factor_of * jnp.repeat(steps, extent[axis_at] // blocks).reshape([-1 if axis == axis_at else 1 for axis in range(len(extent))])
    return factor_of


def normal_values(own_key, shape, spread, most, shards=(), kind=jnp.bfloat16):
    values = spread * jax.random.normal(own_key, shape, jnp.float32)
    if shards:
        values = values * block_levels(own_key, shape, shards, -0.22, 0.18)
    return jnp.clip(values, -most, most).astype(kind)


def setup_inputs(seed: int = 0) -> dict:
    seeds = jax.random.split(jax.random.key(seed), 8)
    return {
        "tokens": normal_values(seeds[0], (TOKENS, W), 1.0, 6.0, ((0, 4), (1, 32))),
        "weights": normal_values(seeds[1], (LEVELS + 1, NB, B, B), (B * (LEVELS + 1)) ** -0.5, 0.125, ((1, 32),)),
        "order": jax.random.permutation(seeds[2], LEVELS).astype(jnp.int32),
        "mask": place_ends((jax.random.randint(seeds[3], (LEVELS, NB), 0, 4) < 3).astype(jnp.int32), jax.random.fold_in(seeds[3], 1), 0, 1),
        "low_u": normal_values(seeds[4], (W, R), W ** -0.5, 0.0234375, ((0, 32),)),
        "low_v": normal_values(seeds[5], (R, W), R ** -0.5, 0.5, ((1, 32),)),
        "cotangent": normal_values(seeds[6], (TOKENS, W), 1.0, 6.0, ((0, 4), (1, 32))),
    }


def gelu_parts(value):
    cdf = 0.5 * (1.0 + lax.erf(value * 0.7071067811865476))
    slope = cdf + value * jnp.exp(-0.5 * value * value) * 0.3989422804014327
    return value * cdf, slope


def group_sum(parts):
    return jnp.sum(parts, axis=0)


def reference(tokens, weights, order, mask, low_u, low_v, cotangent):
    rows = tokens.shape[0]
    blocks = tokens.reshape(rows, NB, B)
    index = jnp.arange(NB, dtype=jnp.int32)

    def partner(arr, level, axis):
        offset = jnp.left_shift(jnp.int32(1), order[level].astype(jnp.int32))
        return jnp.take(arr, jnp.bitwise_xor(index, offset).astype(jnp.int32), axis=axis)

    blocks_f = blocks.astype(jnp.float32)
    mixed = jnp.einsum("tlb,lbc->tlc", blocks_f, weights[0].astype(jnp.float32))
    for level in range(LEVELS):
        gate = mask[level].astype(jnp.float32)[None, :, None]
        moved = partner(blocks_f, level, 1)
        mixed = mixed + jnp.einsum("tlb,lbc->tlc", moved, weights[level + 1].astype(jnp.float32)) * gate
    coeff_b = jnp.dot(tokens, low_u, preferred_element_type=jnp.float32).astype(jnp.bfloat16)
    pre = mixed.reshape(rows, W) + jnp.dot(coeff_b, low_v, preferred_element_type=jnp.float32)
    act, slope = gelu_parts(pre)
    output = act.astype(jnp.bfloat16)
    delta = (cotangent.astype(jnp.float32) * slope).astype(jnp.bfloat16)
    d_blocks = delta.reshape(rows, NB, B).astype(jnp.float32)
    back = jnp.einsum("tlc,lbc->tlb", d_blocks, weights[0].astype(jnp.float32))
    for level in range(LEVELS):
        gate = mask[level].astype(jnp.float32)[None, :, None]
        term = jnp.einsum("tlc,lbc->tlb", d_blocks, weights[level + 1].astype(jnp.float32)) * gate
        back = back + partner(term, level, 1)
    back_coeff = jnp.dot(delta, low_v.T, preferred_element_type=jnp.float32).astype(jnp.bfloat16)
    grad_tokens = (back.reshape(rows, W) + jnp.dot(back_coeff, low_u.T, preferred_element_type=jnp.float32)).astype(jnp.bfloat16)
    x_groups = blocks_f.reshape(N_DP, TOK_DEV, NB, B)
    d_groups = d_blocks.reshape(N_DP, TOK_DEV, NB, B)
    grads = [group_sum(jnp.einsum("gtlb,gtlc->glbc", x_groups, d_groups))]
    for level in range(LEVELS):
        gate = mask[level].astype(jnp.float32)[None, :, None, None]
        moved = partner(x_groups, level, 2)
        grads.append(group_sum(jnp.einsum("gtlb,gtlc->glbc", moved, d_groups) * gate))
    grad_weights = jnp.stack(grads).astype(jnp.bfloat16)
    tok_groups = tokens.astype(jnp.float32).reshape(N_DP, TOK_DEV, W)
    delta_groups = delta.astype(jnp.float32).reshape(N_DP, TOK_DEV, W)
    bc_groups = back_coeff.astype(jnp.float32).reshape(N_DP, TOK_DEV, R)
    cf_groups = coeff_b.astype(jnp.float32).reshape(N_DP, TOK_DEV, R)
    grad_u = group_sum(jnp.einsum("gtf,gtr->gfr", tok_groups, bc_groups)).astype(jnp.bfloat16)
    grad_v = group_sum(jnp.einsum("gtr,gtf->grf", cf_groups, delta_groups)).astype(jnp.bfloat16)
    return (output, grad_tokens, grad_weights, grad_u, grad_v)
```

```python
import jax
import jax.numpy as jnp
from jax import lax
from jax.experimental import pallas as pl
from jax.experimental.pallas import tpu as pltpu
from jax.sharding import PartitionSpec as P

F32 = jnp.float32
BF16 = jnp.bfloat16
T = 256
D = 2048
B = 256
R = 128
NB = 8
YLO, CORE = 8, 9
VMEM = 40 * 1024 * 1024


def nn(a, b):
    return jnp.dot(a, b, preferred_element_type=F32)


def nt(a, b):
    return lax.dot_general(a, b, (((1,), (1,)), ((), ())), preferred_element_type=F32)


def tn(a, b):
    return lax.dot_general(a, b, (((0,), (0,)), ((), ())), preferred_element_type=F32)


def gelu_parts(value):
    cdf = 0.5 * (1.0 + lax.erf(value * 0.7071067811865476))
    slope = cdf + value * jnp.exp(-0.5 * value * value) * 0.3989422804014327
    return (value * cdf, slope)


def gate(info, mask, bit, block):
    return mask[info[bit] - 1, block].astype(F32)


def call(body, grid, in_specs, out_specs, out_shape, flops, data, name, scratch=()):
    return pl.pallas_call(
        body,
        grid_spec=pltpu.PrefetchScalarGridSpec(
            num_scalar_prefetch=2,
            grid=(grid,),
            in_specs=in_specs,
            out_specs=out_specs,
            scratch_shapes=list(scratch),
        ),
        out_shape=out_shape,
        compiler_params=pltpu.CompilerParams(
            dimension_semantics=("arbitrary",), vmem_limit_bytes=VMEM
        ),
        cost_estimate=pl.CostEstimate(flops=flops, bytes_accessed=data, transcendentals=0),
        name=name,
    )


def sds(shape, dtype):
    return jax.ShapeDtypeStruct(shape, dtype)


def col(width=B, at=lambda i, info: i):
    return pl.BlockSpec((T, width), lambda i, info, mask: (0, at(i, info)))


def whole(shape):
    return pl.BlockSpec(shape, lambda i, info, mask: (0,) * len(shape))


def weight(bit):
    if bit is None:
        return pl.BlockSpec((1, 1, B, B), lambda i, info, mask: (0, i, 0, 0))
    return pl.BlockSpec((1, 1, B, B), lambda i, info, mask: (info[bit], i, 0, 0))


def prolog_body(info, mask, x, u, cpart, xs):
    @pl.when(pl.program_id(0) == 0)
    def _():
        cpart[...] = jnp.zeros_like(cpart)

    cpart[...] += nn(x[...], u[...])
    xs[...] = jnp.where(info[YLO] == 0, x[:, 128:], x[:, :128])


def prolog(info, mask, x, low_u):
    return call(
        prolog_body,
        NB,
        [col(), pl.BlockSpec((B, R), lambda i, info, mask: (i, 0))],
        [whole((T, R)), col(128)],
        [sds((T, R), F32), sds((T, D // 2), BF16)],
        2 * T * D * R,
        3 << 20,
        "prolog",
    )(info, mask, x, low_u)


def near_mix_body(info, mask, *refs):
    i = pl.program_id(0)
    xs, ws, mixed = refs[:7], refs[7:14], refs[14]
    total = nn(xs[0][...], ws[0][0, 0])
    for k, bit in enumerate((0, 1, 2, 3, 5, 7)):
        total += nn(xs[k + 1][...], ws[k + 1][0, 0]) * gate(info, mask, bit, i)
    mixed[...] = total


def near_mix(info, mask, x, p3, p5, p7, weights):
    return call(
        near_mix_body,
        NB,
        [col()]
        + [col(at=lambda i, info, o=o: i ^ o) for o in (1, 2, 4)]
        + [col()] * 3
        + [weight(b) for b in (None, 0, 1, 2, 3, 5, 7)],
        col(),
        sds((T, D), F32),
        14 * T * D * B,
        14 << 20,
        "near_mix",
    )(info, mask, x, x, x, x, p3, p5, p7, *([weights] * 7))


def middle_body(info, mask, mixed, p4, p6, w3, w4, w5, w6, *refs):
    coeff, low_v, cot, out, delta, t3, t4, t5, t6, bpart = refs
    i = pl.program_id(0)
    pre = mixed[...] + nn(coeff[...], low_v[...])
    pre += nn(p4[...], w4[0, 0]) * gate(info, mask, 4, i)
    pre += nn(p6[...], w6[0, 0]) * gate(info, mask, 6, i)
    act, slope = gelu_parts(pre)
    out[...] = act.astype(BF16)
    d = (cot[...].astype(F32) * slope).astype(BF16)
    delta[:, pl.ds(pl.multiple_of(i * B, B), B)] = d

    @pl.when(i == 0)
    def _():
        bpart[...] = jnp.zeros_like(bpart)
        delta[:, D:] = coeff[...]

    bpart[...] += nt(d, low_v[...])
    for bit, t, w in ((3, t3, w3), (4, t4, w4), (5, t5, w5), (6, t6, w6)):
        t[...] = (nt(d, w[0, 0]) * gate(info, mask, bit, i)).astype(BF16)


def middle(info, mask, mixed, p4, p6, weights, coeff, low_v, cot):
    return call(
        middle_body,
        NB,
        [col()] * 3
        + [weight(b) for b in range(3, 7)]
        + [whole((T, R)), pl.BlockSpec((R, B), lambda i, info, mask: (0, i)), col()],
        [col(), whole((T, D + R))] + [col()] * 4 + [whole((T, R))],
        [sds((T, D), BF16), sds((T, D + R), BF16)]
        + [sds((T, D), BF16)] * 4
        + [sds((T, R), F32)],
        12 * T * D * B,
        18 << 20,
        "middle",
    )(info, mask, mixed, p4, p6, *([weights] * 4), coeff, low_v, cot)


def far_grads_body(info, mask, p3, p4, p5, p6, delta, keep, send, acc):
    i = pl.program_id(0)
    core = info[CORE]
    for k, p in enumerate((p3, p4, p5, p6)):
        acc[...] = tn(p[...], delta[...]) * gate(info, mask, 3 + k, i)
        for half in range(2):
            mine = pl.ds(pl.multiple_of(128 * half + 64 * core, 64), 64)
            other = pl.ds(pl.multiple_of(128 * half + 64 * (1 - core), 64), 64)
            keep[half, k, 0] = acc[mine, :]
            send[half, k, 0] = acc[other, :].astype(BF16)


def far_grads(info, mask, partners, delta):
    spec = pl.BlockSpec((2, 4, 1, 64, B), lambda i, info, mask: (0, 0, i, 0, 0))
    return call(
        far_grads_body,
        NB,
        [col()] * 5,
        [spec, spec],
        [sds((2, 4, NB, 64, B), F32), sds((2, 4, NB, 64, B), BF16)],
        8 * T * D * B,
        12 << 20,
        "far_grads",
        [pltpu.VMEM((B, B), F32)],
    )(info, mask, *partners[:4], delta)


def hi_term_body(info, mask, dn, w, t):
    t[...] = (nt(dn[...], w[0, 0]) * gate(info, mask, 7, pl.program_id(0))).astype(BF16)


def hi_term(info, mask, dn, weights):
    return call(
        hi_term_body,
        NB,
        [col(), weight(7)],
        col(),
        sds((T, D), BF16),
        2 * T * D * B,
        3 << 20,
        "hi_term",
    )(info, mask, dn, weights)


def local_back_body(info, mask, delta, w0, w1, w2, w4, back):
    i = pl.program_id(0)

    @pl.when(i == 0)
    def _():
        back[...] = jnp.zeros_like(back)

    d = delta[...]

    def add(block, value):
        at = pl.ds(pl.multiple_of(block * B, B), B)
        back[:, at] += value

    add(i, nt(d, w0[0, 0]))
    for bit, w in enumerate((w1, w2, w4)):
        add(i ^ (1 << bit), nt(d, w[0, 0]) * gate(info, mask, bit, i))


def local_back(info, mask, delta, weights):
    return call(
        local_back_body,
        NB,
        [col(), weight(None)] + [weight(b) for b in range(3)],
        whole((T, D)),
        sds((T, D), F32),
        8 * T * D * B,
        8 << 20,
        "local_back",
    )(info, mask, delta, *([weights] * 4))


def near_grads_body(info, mask, x0, x1, x2, x4, p7, n0, n1, n2, n4, n7, delta, dn, keep, send, acc):
    i = pl.program_id(0)
    core = info[CORE]
    mine = pl.ds(pl.multiple_of(64 * core, 64), 64)
    other = pl.ds(pl.multiple_of(64 * (1 - core), 64), 64)
    pairs = ((x0, n0, None), (x1, n1, 0), (x2, n2, 1), (x4, n4, 2), (p7, n7, 7))
    for k, (x, n, bit) in enumerate(pairs):
        g = tn(x[...], delta[...]) + tn(n[...], dn[...])
        if bit is not None:
            g = g * gate(info, mask, bit, i)
        acc[...] = g
        keep[k, 0] = acc[mine, :]
        send[k, 0] = acc[other, :].astype(BF16)


def near_grads(info, mask, x, p7, xn, hn, delta, dn):
    own = [col(128, lambda i, info, o=o: 2 * (i ^ o) + info[YLO]) for o in (0, 1, 2, 4, 0)]
    got = [col(128, lambda i, info, o=o: i ^ o) for o in (0, 1, 2, 4, 0)]
    spec = pl.BlockSpec((5, 1, 64, B), lambda i, info, mask: (0, i, 0, 0))
    return call(
        near_grads_body,
        NB,
        own + got + [col(), col()],
        [spec, spec],
        [sds((5, NB, 64, B), F32), sds((5, NB, 64, B), BF16)],
        10 * T * D * B,
        12 << 20,
        "near_grads",
        [pltpu.VMEM((128, B), F32)],
    )(info, mask, x, x, x, x, p7, xn, xn, xn, xn, hn, delta, dn)


def grad_tokens_body(info, mask, back, sx, sz, t7, bc, u, out):
    total = back[...] + nt(bc[...], u[...])
    for t in (sx, sz, t7):
        total += t[...].astype(F32)
    out[...] = total.astype(BF16)


def grad_tokens_sum(info, mask, back, terms, bc, low_u):
    return call(
        grad_tokens_body,
        NB,
        [col()] * 4 + [whole((T, R)), pl.BlockSpec((B, R), lambda i, info, mask: (i, 0))],
        col(),
        sds((T, D), BF16),
        2 * T * D * R,
        9 << 20,
        "grad_tokens",
    )(info, mask, back, *terms, bc, low_u)


def assemble_body(info, mask, near_keep, near_got, far_keep, far_got, out):
    k = pl.program_id(0)
    far = jnp.logical_and(k >= 4, k < 8)

    @pl.when(far)
    def _():
        out[...] = (far_keep[...] + far_got[...].astype(F32)).astype(BF16)

    @pl.when(jnp.logical_not(far))
    def _():
        out[...] = (near_keep[...] + near_got[...].astype(F32)).astype(BF16)


def assemble(info, mask, near_keep, near_got, far_keep, far_got):
    shape = (1, NB, 64, B)

    def near(k, info, mask):
        return (jnp.where(k < 4, k, jnp.where(k == 8, 4, 3)), 0, 0, 0)

    def far(k, info, mask):
        return (jnp.clip(k - 4, 0, 3), 0, 0, 0)

    def place(k, info, mask):
        return (jnp.where(k == 0, 0, info[jnp.maximum(k - 1, 0)]), 0, 0, 0)

    return call(
        assemble_body,
        9,
        [pl.BlockSpec(shape, near)] * 2 + [pl.BlockSpec(shape, far)] * 2,
        pl.BlockSpec(shape, place),
        sds((9, NB, 64, B), BF16),
        0,
        10 << 20,
        "assemble",
    )(info, mask, near_keep, near_got, far_keep, far_got)


def swap(value, axis, offset):
    sizes = 1
    for name in axis if isinstance(axis, tuple) else (axis,):
        sizes *= lax.axis_size(name)
    return lax.ppermute(value, axis, [(i, i ^ offset) for i in range(sizes)])


def sum_feat(value, offsets):
    for offset in offsets:
        value = value + swap(value, "feat", offset)
    return value


def merge(own, got):
    return (own.astype(F32) + got.astype(F32)).astype(BF16)


def pick(arr, index, axis=0):
    return lax.dynamic_index_in_dim(arr, index, axis, keepdims=False)


def per_device(x, weights, order, mask, low_u, low_v, cot):
    dp = lax.axis_index("dp").astype(jnp.int32)
    ylo, core = dp // 2, dp % 2
    both = ("feat", "dp")
    levels = jnp.arange(8, dtype=jnp.int32)
    slots = 1 + jnp.sum(jnp.where(order[None, :] == levels[:, None], levels[None, :], 0), 1)
    info = jnp.concatenate([slots, jnp.stack([ylo, core])]).astype(jnp.int32)

    cpart, xs = prolog(info, mask, x, low_u)
    p3, p5, p7 = swap(x, "feat", 1), swap(x, "feat", 4), swap(x, "feat", 16)
    c = sum_feat(cpart, (3, 12))
    c, p3, p5, p7, xs = lax.optimization_barrier((c, p3, p5, p7, xs))
    p4, p6 = swap(p3, "feat", 3), swap(p5, "feat", 12)
    xn = swap(xs, "dp", 2)
    hn = swap(xs, both, 66)
    partners = [p3, p4, p5, p6, p7]
    coeff = sum_feat(c, (1, 4, 16)).astype(BF16)
    coeff, xn, hn = lax.optimization_barrier((coeff, xn, hn))
    mixed = near_mix(info, mask, x, p3, p5, p7, weights)
    out, delta, t3, t4, t5, t6, bpart = middle(
        info, mask, mixed, p4, p6, weights, coeff, low_v, cot
    )
    dn = swap(delta, "dp", 2)
    r4, r6 = swap(t4, "feat", 3), swap(t6, "feat", 12)
    b = sum_feat(bpart, (1, 4, 16))
    b, r4, r6, dn, t3, t5 = lax.optimization_barrier((b, r4, r6, dn, t3, t5))
    sx, sz = swap(merge(t3, r4), "feat", 1), swap(merge(t5, r6), "feat", 4)
    t7 = swap(hi_term(info, mask, dn, weights), both, 66)
    bc = sum_feat(b, (3, 12)).astype(BF16)

    far_keep, far_send = far_grads(info, mask, partners, delta)
    far_got = swap(far_send, "dp", 1)
    back = local_back(info, mask, delta, weights)
    far_sum_send = (pick(far_keep, 1 - ylo) + pick(far_got, 1 - ylo).astype(F32)).astype(BF16)
    far_keep2 = pick(far_keep, ylo) + pick(far_got, ylo).astype(F32)
    far_got2 = swap(far_sum_send, "dp", 2)
    near_keep, near_send = near_grads(info, mask, x, partners[4], xn, hn, delta, dn)
    near_got = swap(near_send, "dp", 1)

    half = D // 2
    gv = tn(delta[:, D:], lax.dynamic_slice(delta, (0, ylo * half), (T, half)))
    gv = gv + tn(dn[:, D:], lax.dynamic_slice(dn, (0, ylo * half), (T, half)))
    gv_send = lax.dynamic_slice(gv, (0, (1 - core) * (half // 2)), (R, half // 2)).astype(BF16)
    gv_keep = lax.dynamic_slice(gv, (0, core * (half // 2)), (R, half // 2))
    grad_v = (gv_keep + swap(gv_send, "dp", 1).astype(F32)).astype(BF16)

    gu = tn(x, bc).reshape(4, D // 4, R)
    gu_total = pick(gu, dp)
    gu_send = [pick(gu, dp ^ m).astype(BF16) for m in (1, 2, 3)]
    gu_send, sx, sz, t7, far_got2 = lax.optimization_barrier((gu_send, sx, sz, t7, far_got2))
    for m in (1, 2, 3):
        gu_total = gu_total + swap(gu_send[m - 1], "dp", m).astype(F32)
    grad_u = gu_total.astype(BF16)

    grad_x = grad_tokens_sum(info, mask, back, [sx, sz, t7], bc, low_u)
    grad_w = assemble(info, mask, near_keep, near_got, far_keep2, far_got2)
    return out, grad_x, grad_w, grad_u, grad_v


def solution(mesh):
    return jax.shard_map(
        per_device,
        mesh=mesh,
        in_specs=(
            P("dp", "feat"),
            P(None, "feat", None, None),
            P(),
            P(None, "feat"),
            P("feat", None),
            P(None, "feat"),
            P("dp", "feat"),
        ),
        out_specs=(
            P("dp", "feat"),
            P("dp", "feat"),
            P(None, "feat", "dp", None),
            P(("feat", "dp"), None),
            P(None, ("feat", "dp")),
        ),
        check_vma=False,
    )
```

```python
import jax
import jax.numpy as jnp
from jax import lax
from jax.experimental import pallas as pl
from jax.experimental.pallas import tpu as pltpu
from jax.sharding import PartitionSpec as P

F32 = jnp.float32
BF16 = jnp.bfloat16
T = 256
D = 2048
B = 256
R = 128
NB = 8
STEPS = 4
W2 = 2 * B
YLO, CORE, DP = 8, 9, 10
LIMIT = 52 << 20


def nn(a, b):
    return jnp.dot(a, b, preferred_element_type=F32)


def nt(a, b):
    return lax.dot_general(a, b, (((1,), (1,)), ((), ())), preferred_element_type=F32)


def tn(a, b):
    return lax.dot_general(a, b, (((0,), (0,)), ((), ())), preferred_element_type=F32)


def gelu_parts(value):
    cdf = 0.5 * (1.0 + lax.erf(value * 0.7071067811865476))
    slope = cdf + value * jnp.exp(-0.5 * value * value) * 0.3989422804014327
    return (value * cdf, slope)


def gate(info, mask, bit, block):
    return mask[info[bit] - 1, block].astype(F32)


def call(body, in_specs, out_specs, out_shape, flops, data, name, grid=STEPS, aliases={}):
    return pl.pallas_call(
        body,
        grid_spec=pltpu.PrefetchScalarGridSpec(
            num_scalar_prefetch=2, grid=(grid,), in_specs=in_specs, out_specs=out_specs
        ),
        out_shape=out_shape,
        input_output_aliases=aliases,
        compiler_params=pltpu.CompilerParams(
            dimension_semantics=("arbitrary",), vmem_limit_bytes=LIMIT
        ),
        cost_estimate=pl.CostEstimate(flops=flops, bytes_accessed=data, transcendentals=0),
        name=name,
    )


def sds(shape, dtype):
    return jax.ShapeDtypeStruct(shape, dtype)


def col(width=W2, at=lambda i, info: i):
    return pl.BlockSpec((T, width), lambda i, info, mask: (0, at(i, info)))


def whole(shape):
    return pl.BlockSpec(shape, lambda i, info, mask: (0,) * len(shape))


def weight(bit):
    if bit is None:
        return pl.BlockSpec((1, 2, B, B), lambda i, info, mask: (0, i, 0, 0))
    return pl.BlockSpec((1, 2, B, B), lambda i, info, mask: (info[bit], i, 0, 0))


def blk(ref, j):
    return ref[:, j * B : (j + 1) * B]


OWN = [col(), col(at=lambda i, info: i ^ 1), col(at=lambda i, info: i ^ 2)]


def prolog_body(info, mask, x, u, cpart, xs):
    @pl.when(pl.program_id(0) == 0)
    def _():
        cpart[...] = jnp.zeros_like(cpart)

    cpart[...] += nn(x[...], u[...])
    for j in range(2):
        b = blk(x, j)
        xs[:, j * 128 : (j + 1) * 128] = jnp.where(info[YLO] == 0, b[:, 128:], b[:, :128])


def prolog(info, mask, x, low_u):
    return call(
        prolog_body,
        [col(), pl.BlockSpec((W2, R), lambda i, info, mask: (i, 0))],
        [whole((T, R)), col(B)],
        [sds((T, R), F32), sds((T, D // 2), BF16)],
        2 * T * D * R,
        3 << 20,
        "prolog",
    )(info, mask, x, low_u)


def near_mix_body(info, mask, xa, xb, xc, p3, p5, p7, w, w0, w1, w2, w3, w5, w7, mixed):
    i = pl.program_id(0)
    for j in range(2):
        total = nn(blk(xa, j), w[0, j])
        for x, k, v, bit in (
            (xa, 1 - j, w0, 0),
            (xb, j, w1, 1),
            (xc, j, w2, 2),
            (p3, j, w3, 3),
            (p5, j, w5, 5),
            (p7, j, w7, 7),
        ):
            total += nn(blk(x, k), v[0, j]) * gate(info, mask, bit, 2 * i + j)
        mixed[:, j * B : (j + 1) * B] = total


def near_mix(info, mask, x, p3, p5, p7, weights):
    return call(
        near_mix_body,
        OWN + [col()] * 3 + [weight(b) for b in (None, 0, 1, 2, 3, 5, 7)],
        col(),
        sds((T, D), F32),
        14 * T * D * B,
        14 << 20,
        "near_mix",
    )(info, mask, x, x, x, p3, p5, p7, *([weights] * 7))


def middle_body(info, mask, mixed, p4, p6, w3, w4, w5, w6, *refs):
    coeff, low_v, cot, out, delta, t3, t4, t5, t6, bpart = refs
    i = pl.program_id(0)

    @pl.when(i == 0)
    def _():
        bpart[...] = jnp.zeros_like(bpart)
        delta[:, D:] = coeff[...]

    for j in range(2):
        cols = slice(j * B, (j + 1) * B)
        pre = mixed[:, cols] + nn(coeff[...], low_v[:, cols])
        pre += nn(p4[:, cols], w4[0, j]) * gate(info, mask, 4, 2 * i + j)
        pre += nn(p6[:, cols], w6[0, j]) * gate(info, mask, 6, 2 * i + j)
        act, slope = gelu_parts(pre)
        out[:, cols] = act.astype(BF16)
        d = (cot[:, cols].astype(F32) * slope).astype(BF16)
        delta[:, pl.ds(pl.multiple_of((2 * i + j) * B, B), B)] = d
        bpart[...] += nt(d, low_v[:, cols])
        for bit, t, w in ((4, t4, w4), (6, t6, w6), (3, t3, w3), (5, t5, w5)):
            t[:, cols] = (nt(d, w[0, j]) * gate(info, mask, bit, 2 * i + j)).astype(BF16)


def middle(info, mask, mixed, p4, p6, weights, coeff, low_v, cot):
    return call(
        middle_body,
        [col()] * 3
        + [weight(b) for b in range(3, 7)]
        + [whole((T, R)), pl.BlockSpec((R, W2), lambda i, info, mask: (0, i)), col()],
        [col(), whole((T, D + R))] + [col()] * 4 + [whole((T, R))],
        [sds((T, D), BF16), sds((T, D + R), BF16)]
        + [sds((T, D), BF16)] * 4
        + [sds((T, R), F32)],
        12 * T * D * B,
        18 << 20,
        "middle",
    )(info, mask, mixed, p4, p6, *([weights] * 4), coeff, low_v, cot)


def far_grads_body(info, mask, p3, p4, p5, p6, delta, keep, send):
    i = pl.program_id(0)
    first = info[CORE] == 0
    for j in range(2):
        d = blk(delta, j)
        for k, p in enumerate((p3, p4, p5, p6)):
            g = tn(blk(p, j), d) * gate(info, mask, 3 + k, 2 * i + j)
            for half in range(2):
                lo, hi = g[128 * half : 128 * half + 64], g[128 * half + 64 : 128 * half + 128]
                keep[half, k, j] = jnp.where(first, lo, hi)
                send[half, k, j] = jnp.where(first, hi, lo).astype(BF16)


def far_grads(info, mask, partners, delta):
    spec = pl.BlockSpec((2, 4, 2, 64, B), lambda i, info, mask: (0, 0, i, 0, 0))
    return call(
        far_grads_body,
        [col()] * 5,
        [spec, spec],
        [sds((2, 4, NB, 64, B), F32), sds((2, 4, NB, 64, B), BF16)],
        8 * T * D * B,
        12 << 20,
        "far_grads",
    )(info, mask, *partners, delta)


def second_body(info, mask, t3, r4, t5, r6, dn, w, sx, sz, hi):
    sx[...] = (t3[...].astype(F32) + r4[...].astype(F32)).astype(BF16)
    sz[...] = (t5[...].astype(F32) + r6[...].astype(F32)).astype(BF16)
    for j in range(2):
        g = gate(info, mask, 7, 2 * pl.program_id(0) + j)
        hi[:, j * B : (j + 1) * B] = (nt(blk(dn, j), w[0, j]) * g).astype(BF16)


def second(info, mask, t3, r4, t5, r6, dn, weights):
    return call(
        second_body,
        [col()] * 5 + [weight(7)],
        [col()] * 3,
        [sds((T, D), BF16)] * 3,
        2 * T * D * B,
        9 << 20,
        "second",
    )(info, mask, t3, r4, t5, r6, dn, weights)


def local_back_body(info, mask, delta, bc, u, w, w0, w1, w2, back):
    i = pl.program_id(0)

    @pl.when(i == 0)
    def _():
        back[...] = jnp.zeros_like(back)

    def place(step, j):
        return pl.ds(pl.multiple_of(step * W2 + j * B, B), B)

    low = nt(bc[...], u[...])
    for j in range(2):
        d, e = blk(delta, j), blk(delta, 1 - j)
        back[:, place(i, j)] += (
            nt(d, w[0, j]) + nt(e, w0[0, 1 - j]) * gate(info, mask, 0, 2 * i + 1 - j) + blk(low, j)
        )
        back[:, place(i ^ 1, j)] += nt(d, w1[0, j]) * gate(info, mask, 1, 2 * i + j)
        back[:, place(i ^ 2, j)] += nt(d, w2[0, j]) * gate(info, mask, 2, 2 * i + j)


def local_back(info, mask, delta, bc, low_u, weights):
    return call(
        local_back_body,
        [col(), whole((T, R)), pl.BlockSpec((W2, R), lambda i, info, mask: (i, 0))]
        + [weight(b) for b in (None, 0, 1, 2)],
        whole((T, D)),
        sds((T, D), F32),
        8 * T * D * B,
        8 << 20,
        "local_back",
    )(info, mask, delta, bc, low_u, *([weights] * 4))


def near_grads_body(info, mask, xa, xb, xc, p7, na, nb, nc, n7, delta, dn, co, cn, *outs):
    keep, send, vkeep, vsend = outs
    i = pl.program_id(0)
    first = info[CORE] == 0

    def half(ref, j):
        return ref[:, pl.ds(pl.multiple_of(j * B + info[YLO] * 128, 128), 128)]

    def part(ref, j):
        return ref[:, j * 128 : (j + 1) * 128]

    for j in range(2):
        own = [half(xa, j), half(xa, 1 - j), half(xb, j), half(xc, j), half(p7, j)]
        got = [part(na, j), part(na, 1 - j), part(nb, j), part(nc, j), part(n7, j)]
        g = tn(jnp.concatenate(own, 1), blk(delta, j)) + tn(jnp.concatenate(got, 1), blk(dn, j))
        for k, bit in enumerate((None, 0, 1, 2, 7)):
            h = g[128 * k : 128 * (k + 1)]
            if bit is not None:
                h = h * gate(info, mask, bit, 2 * i + j)
            keep[k, j] = jnp.where(first, h[:64], h[64:])
            send[k, j] = jnp.where(first, h[64:], h[:64]).astype(BF16)

    @pl.when(i // 2 == info[YLO])
    def _():
        v = tn(co[...], delta[...]) + tn(cn[...], dn[...])

        @pl.when(i == info[DP])
        def _():
            vkeep[...] = v

        @pl.when(i != info[DP])
        def _():
            vsend[...] = v.astype(BF16)


def near_grads(info, mask, x, p7, xn, hn, delta, dn):
    got = [col(B), col(B, lambda i, info: i ^ 1), col(B, lambda i, info: i ^ 2), col(B)]
    spec = pl.BlockSpec((5, 2, 64, B), lambda i, info, mask: (0, i, 0, 0))
    last = col(R, lambda i, info: D // R)
    return call(
        near_grads_body,
        OWN + [col()] + got + [col(), col(), last, last],
        [spec, spec, whole((R, W2)), whole((R, W2))],
        [
            sds((5, NB, 64, B), F32),
            sds((5, NB, 64, B), BF16),
            sds((R, W2), F32),
            sds((R, W2), BF16),
        ],
        10 * T * D * B,
        12 << 20,
        "near_grads",
    )(info, mask, x, x, x, p7, xn, xn, xn, hn, delta, dn, delta, dn)


def grad_u_body(info, mask, x, bc, keep, send):
    i = pl.program_id(0)
    g = tn(x[...], bc[...])

    @pl.when(i % 2 == info[CORE])
    def _():
        keep[i // 2] = g

    @pl.when(i % 2 != info[CORE])
    def _():
        send[i // 2] = g.astype(BF16)


def grad_u_parts(info, mask, x, bc):
    shape = (2, W2, R)
    return call(
        grad_u_body,
        [col(), whole((T, R))],
        [whole(shape)] * 2,
        [sds(shape, F32), sds(shape, BF16)],
        2 * T * D * R,
        2 << 20,
        "grad_u",
    )(info, mask, x, bc)


def grad_u_halves_body(info, mask, keep, got, mine, other):
    y = info[YLO]
    mine[...] = keep[y] + got[y].astype(F32)
    other[...] = (keep[1 - y] + got[1 - y].astype(F32)).astype(BF16)


def grad_u_halves(info, mask, keep, got):
    return call(
        grad_u_halves_body,
        [whole((2, W2, R))] * 2,
        [whole((W2, R))] * 2,
        [sds((W2, R), F32), sds((W2, R), BF16)],
        0,
        1 << 20,
        "grad_u_halves",
        1,
    )(info, mask, keep, got)


def grad_tokens_body(info, mask, back, sx, sz, t7, out):
    total = back[...]
    for t in (sx, sz, t7):
        total += t[...].astype(F32)
    out[...] = total.astype(BF16)


def grad_tokens_sum(info, mask, back, terms):
    return call(
        grad_tokens_body,
        [col()] * 4,
        col(),
        sds((T, D), BF16),
        4 * T * D,
        6 << 20,
        "grad_tokens",
    )(info, mask, back, *terms)


def assemble_body(info, mask, keep, got, *out):
    out[-1][...] = (keep[...] + got[...].astype(F32)).astype(BF16)


def assemble(info, mask, keep, got, bits, before=None):
    shape = (1, NB, 64, B)

    def source(k, info, mask):
        return (k, 0, 0, 0)

    def place(k, info, mask):
        at = 0 if bits[0] is None else info[bits[0]]
        for n, bit in enumerate(bits[1:], 1):
            at = jnp.where(k == n, info[bit], at)
        return (at, 0, 0, 0)

    more = [] if before is None else [before]
    return call(
        assemble_body,
        [pl.BlockSpec(shape, source)] * 2 + [pl.BlockSpec(memory_space=pl.ANY)] * len(more),
        pl.BlockSpec(shape, place),
        sds((9, NB, 64, B), BF16),
        0,
        len(bits) << 20,
        "assemble",
        len(bits),
        {4: 0} if more else {},
    )(info, mask, keep, got, *more)


def swap(value, axis, offset):
    sizes = 1
    for name in axis if isinstance(axis, tuple) else (axis,):
        sizes *= lax.axis_size(name)
    return lax.ppermute(value, axis, [(i, i ^ offset) for i in range(sizes)])


def sum_feat(value, offsets):
    for offset in offsets:
        value = value + swap(value, "feat", offset)
    return value


def beside(order, part, *args):
    shapes = jax.eval_shape(part, *args)

    def nothing(*args):
        return jax.tree.map(lambda s: jnp.zeros(s.shape, s.dtype), shapes)

    return lax.cond(order[0] >= 0, part, nothing, *args)


def pick(arr, index, axis=0):
    return lax.dynamic_index_in_dim(arr, index, axis, keepdims=False)


def per_device(x, weights, order, mask, low_u, low_v, cot):
    dp = lax.axis_index("dp").astype(jnp.int32)
    ylo, core = dp // 2, dp % 2
    both = ("feat", "dp")
    levels = jnp.arange(8, dtype=jnp.int32)
    slots = 1 + jnp.sum(jnp.where(order[None, :] == levels[:, None], levels[None, :], 0), 1)
    info = jnp.concatenate([slots, jnp.stack([ylo, core, dp])]).astype(jnp.int32)

    cpart, xs = prolog(info, mask, x, low_u)
    p3, p5, p7 = swap(x, "feat", 1), swap(x, "feat", 4), swap(x, "feat", 16)
    c = sum_feat(cpart, (3, 12))
    c, p3, p5, p7, xs = lax.optimization_barrier((c, p3, p5, p7, xs))
    p4, p6 = swap(p3, "feat", 3), swap(p5, "feat", 12)
    xn = swap(xs, "dp", 2)
    hn = swap(xs, both, 66)
    coeff = sum_feat(c, (1, 4, 16)).astype(BF16)
    mixed = near_mix(info, mask, x, p3, p5, p7, weights)
    coeff, xn, hn, mixed = lax.optimization_barrier((coeff, xn, hn, mixed))
    out, delta, t3, t4, t5, t6, bpart = middle(
        info, mask, mixed, p4, p6, weights, coeff, low_v, cot
    )

    dn = swap(delta, "dp", 2)
    r4, r6 = swap(t4, "feat", 3), swap(t6, "feat", 12)

    def beside_first(p3, p4, p5, p6, delta, bpart):
        b = sum_feat(bpart, (1, 4, 16))
        keep, send = far_grads(info, mask, (p3, p4, p5, p6), delta)
        got = swap(send, "dp", 1)
        away = pick(keep, 1 - ylo) + pick(got, 1 - ylo).astype(F32)
        return b, pick(keep, ylo) + pick(got, ylo).astype(F32), away.astype(BF16)

    b, far_keep, far_send = beside(order, beside_first, p3, p4, p5, p6, delta, bpart)
    r4, r6, dn, b, far_send = lax.optimization_barrier((r4, r6, dn, b, far_send))

    sx, sz, hi = second(info, mask, t3, r4, t5, r6, dn, weights)
    sx, sz, hi, b, far_send = lax.optimization_barrier((sx, sz, hi, b, far_send))
    sx, sz, t7 = swap(sx, "feat", 1), swap(sz, "feat", 4), swap(hi, both, 66)
    far_got = swap(far_send, "dp", 2)

    def beside_second(b, x, p7, xn, hn, delta, dn, low_u, weights):
        bc = sum_feat(b, (3, 12)).astype(BF16)
        keep, send, v_keep, v_send = near_grads(info, mask, x, p7, xn, hn, delta, dn)
        bc, send, v_send = lax.optimization_barrier((bc, send, v_send))
        got = swap(send, "dp", 1)
        back = local_back(info, mask, delta, bc, low_u, weights)
        gu_keep, gu_send = grad_u_parts(info, mask, x, bc)
        gu_send, got, v_send = lax.optimization_barrier((gu_send, got, v_send))
        gu_got = swap(gu_send, "dp", 1)
        gu_keep, gu_send = grad_u_halves(info, mask, gu_keep, gu_got)
        gu_send, v_send = lax.optimization_barrier((gu_send, v_send))
        gu_got = swap(gu_send, "dp", 2)
        grad_u = (gu_keep + gu_got.astype(F32)).astype(BF16)
        v_send, grad_u = lax.optimization_barrier((v_send, grad_u))
        grad_v = (v_keep + swap(v_send, "dp", 1).astype(F32)).astype(BF16)
        grad_w = assemble(info, mask, keep, got, (None, 0, 1, 2, 7))
        return back, grad_w, grad_u, grad_v

    back, grad_w, grad_u, grad_v = beside(
        order, beside_second, b, x, p7, xn, hn, delta, dn, low_u, weights
    )
    grad_x = grad_tokens_sum(info, mask, back, [sx, sz, t7])
    grad_w = assemble(info, mask, far_keep, far_got, (3, 4, 5, 6), grad_w)
    return out, grad_x, grad_w, grad_u, grad_v


def solution(mesh):
    return jax.shard_map(
        per_device,
        mesh=mesh,
        in_specs=(
            P("dp", "feat"),
            P(None, "feat", None, None),
            P(),
            P(None, "feat"),
            P("feat", None),
            P(None, "feat"),
            P("dp", "feat"),
        ),
        out_specs=(
            P("dp", "feat"),
            P("dp", "feat"),
            P(None, "feat", "dp", None),
            P(("feat", "dp"), None),
            P(None, ("feat", "dp")),
        ),
        check_vma=False,
    )
```

```python
import jax
import jax.numpy as jnp
from jax import lax
from jax.experimental import pallas as pl
from jax.experimental.pallas import tpu as pltpu
from jax.sharding import PartitionSpec as P

F32 = jnp.float32
BF16 = jnp.bfloat16
T = 256
D = 2048
B = 256
R = 128
NB = 8
STEPS = 4
W2 = 2 * B
YLO, CORE, DP = 8, 9, 10
LIMIT = 52 << 20


def nn(a, b):
    return jnp.dot(a, b, preferred_element_type=F32)


def nt(a, b):
    return lax.dot_general(a, b, (((1,), (1,)), ((), ())), preferred_element_type=F32)


def tn(a, b):
    return lax.dot_general(a, b, (((0,), (0,)), ((), ())), preferred_element_type=F32)


def gelu_parts(value):
    cdf = 0.5 * (1.0 + lax.erf(value * 0.7071067811865476))
    slope = cdf + value * jnp.exp(-0.5 * value * value) * 0.3989422804014327
    return (value * cdf, slope)


def gate(info, mask, bit, block):
    return mask[info[bit] - 1, block].astype(F32)


def call(body, in_specs, out_specs, out_shape, flops, data, name, grid=STEPS, aliases=None):
    return pl.pallas_call(
        body,
        grid_spec=pltpu.PrefetchScalarGridSpec(
            num_scalar_prefetch=2, grid=(grid,), in_specs=in_specs, out_specs=out_specs
        ),
        out_shape=out_shape,
        input_output_aliases=aliases or {},
        compiler_params=pltpu.CompilerParams(
            dimension_semantics=("arbitrary",), vmem_limit_bytes=LIMIT
        ),
        cost_estimate=pl.CostEstimate(flops=flops, bytes_accessed=data, transcendentals=0),
        name=name,
    )


def sds(shape, dtype):
    return jax.ShapeDtypeStruct(shape, dtype)


def col(width=W2, at=lambda i, info: i):
    return pl.BlockSpec((T, width), lambda i, info, mask: (0, at(i, info)))


def whole(shape):
    return pl.BlockSpec(shape, lambda i, info, mask: (0,) * len(shape))


def weight(bit):
    if bit is None:
        return pl.BlockSpec((1, 2, B, B), lambda i, info, mask: (0, i, 0, 0))
    return pl.BlockSpec((1, 2, B, B), lambda i, info, mask: (info[bit], i, 0, 0))


def blk(ref, j):
    return ref[:, j * B : (j + 1) * B]


OWN = [col(), col(at=lambda i, info: i ^ 1), col(at=lambda i, info: i ^ 2)]


def prolog_body(info, mask, x, u, cpart, xs):
    @pl.when(pl.program_id(0) == 0)
    def _():
        cpart[...] = jnp.zeros_like(cpart)

    cpart[...] += nn(x[...], u[...])
    for j in range(2):
        b = blk(x, j)
        xs[:, j * 128 : (j + 1) * 128] = jnp.where(info[YLO] == 0, b[:, 128:], b[:, :128])


def prolog(info, mask, x, low_u):
    return call(
        prolog_body,
        [col(), pl.BlockSpec((W2, R), lambda i, info, mask: (i, 0))],
        [whole((T, R)), col(B)],
        [sds((T, R), F32), sds((T, D // 2), BF16)],
        2 * T * D * R,
        3 << 20,
        "prolog",
    )(info, mask, x, low_u)


def near_mix_body(info, mask, xa, xb, xc, p3, p5, p7, w, w0, w1, w2, w3, w5, w7, mixed):
    i = pl.program_id(0)
    for j in range(2):
        total = nn(blk(xa, j), w[0, j])
        for x, k, v, bit in (
            (xa, 1 - j, w0, 0),
            (xb, j, w1, 1),
            (xc, j, w2, 2),
            (p3, j, w3, 3),
            (p5, j, w5, 5),
            (p7, j, w7, 7),
        ):
            total += nn(blk(x, k), v[0, j]) * gate(info, mask, bit, 2 * i + j)
        mixed[:, j * B : (j + 1) * B] = total


def near_mix(info, mask, x, p3, p5, p7, weights):
    return call(
        near_mix_body,
        OWN + [col()] * 3 + [weight(b) for b in (None, 0, 1, 2, 3, 5, 7)],
        col(),
        sds((T, D), F32),
        14 * T * D * B,
        14 << 20,
        "near_mix",
    )(info, mask, x, x, x, p3, p5, p7, *([weights] * 7))


def middle_body(info, mask, mixed, p4, p6, w3, w4, w5, w6, *refs):
    coeff, low_v, cot, out, delta, t3, t4, t5, t6, bpart = refs
    i = pl.program_id(0)

    @pl.when(i == 0)
    def _():
        bpart[...] = jnp.zeros_like(bpart)
        delta[:, D:] = coeff[...]

    for j in range(2):
        cols = slice(j * B, (j + 1) * B)
        pre = mixed[:, cols] + nn(coeff[...], low_v[:, cols])
        pre += nn(p4[:, cols], w4[0, j]) * gate(info, mask, 4, 2 * i + j)
        pre += nn(p6[:, cols], w6[0, j]) * gate(info, mask, 6, 2 * i + j)
        act, slope = gelu_parts(pre)
        out[:, cols] = act.astype(BF16)
        d = (cot[:, cols].astype(F32) * slope).astype(BF16)
        delta[:, pl.ds(pl.multiple_of((2 * i + j) * B, B), B)] = d
        bpart[...] += nt(d, low_v[:, cols])
        for bit, t, w in ((4, t4, w4), (6, t6, w6), (3, t3, w3), (5, t5, w5)):
            t[:, cols] = (nt(d, w[0, j]) * gate(info, mask, bit, 2 * i + j)).astype(BF16)


def middle(info, mask, mixed, p4, p6, weights, coeff, low_v, cot):
    return call(
        middle_body,
        [col()] * 3
        + [weight(b) for b in range(3, 7)]
        + [whole((T, R)), pl.BlockSpec((R, W2), lambda i, info, mask: (0, i)), col()],
        [col(), whole((T, D + R))] + [col()] * 4 + [whole((T, R))],
        [sds((T, D), BF16), sds((T, D + R), BF16)]
        + [sds((T, D), BF16)] * 4
        + [sds((T, R), F32)],
        12 * T * D * B,
        18 << 20,
        "middle",
    )(info, mask, mixed, p4, p6, *([weights] * 4), coeff, low_v, cot)


def far_grads_body(info, mask, p3, p4, p5, p6, delta, keep, send):
    i = pl.program_id(0)
    first = info[CORE] == 0
    for j in range(2):
        d = blk(delta, j)
        for k, p in enumerate((p3, p4, p5, p6)):
            g = tn(blk(p, j), d) * gate(info, mask, 3 + k, 2 * i + j)
            for half in range(2):
                lo, hi = g[128 * half : 128 * half + 64], g[128 * half + 64 : 128 * half + 128]
                keep[half, k, j] = jnp.where(first, lo, hi)
                send[half, k, j] = jnp.where(first, hi, lo).astype(BF16)


def far_grads(info, mask, partners, delta):
    spec = pl.BlockSpec((2, 4, 2, 64, B), lambda i, info, mask: (0, 0, i, 0, 0))
    return call(
        far_grads_body,
        [col()] * 5,
        [spec, spec],
        [sds((2, 4, NB, 64, B), F32), sds((2, 4, NB, 64, B), BF16)],
        8 * T * D * B,
        12 << 20,
        "far_grads",
    )(info, mask, *partners, delta)


def second_body(info, mask, t3, r4, t5, r6, dn, w, sx, sz, hi):
    sx[...] = t3[...] + r4[...]
    sz[...] = t5[...] + r6[...]
    for j in range(2):
        g = gate(info, mask, 7, 2 * pl.program_id(0) + j)
        hi[:, j * B : (j + 1) * B] = (nt(blk(dn, j), w[0, j]) * g).astype(BF16)


def second(info, mask, t3, r4, t5, r6, dn, weights):
    return call(
        second_body,
        [col()] * 5 + [weight(7)],
        [col()] * 3,
        [sds((T, D), BF16)] * 3,
        2 * T * D * B,
        9 << 20,
        "second",
    )(info, mask, t3, r4, t5, r6, dn, weights)


def local_back_body(info, mask, delta, w, w0, w1, w2, back):
    i = pl.program_id(0)

    @pl.when(i == 0)
    def _():
        back[...] = jnp.zeros_like(back)

    def place(step, j):
        return pl.ds(pl.multiple_of(step * W2 + j * B, B), B)

    for j in range(2):
        d, e = blk(delta, j), blk(delta, 1 - j)
        back[:, place(i, j)] += (
            nt(d, w[0, j]) + nt(e, w0[0, 1 - j]) * gate(info, mask, 0, 2 * i + 1 - j)
        )
        back[:, place(i ^ 1, j)] += nt(d, w1[0, j]) * gate(info, mask, 1, 2 * i + j)
        back[:, place(i ^ 2, j)] += nt(d, w2[0, j]) * gate(info, mask, 2, 2 * i + j)


def local_back(info, mask, delta, weights):
    return call(
        local_back_body,
        [col()] + [weight(b) for b in (None, 0, 1, 2)],
        whole((T, D)),
        sds((T, D), F32),
        8 * T * D * B,
        8 << 20,
        "local_back",
    )(info, mask, delta, *([weights] * 4))


def near_grads_body(info, mask, xa, xb, xc, p7, na, nb, nc, n7, delta, dn, co, cn, *outs):
    keep, send, vkeep, vsend = outs
    i = pl.program_id(0)
    first = info[CORE] == 0

    def half(ref, j):
        return ref[:, pl.ds(pl.multiple_of(j * B + info[YLO] * 128, 128), 128)]

    def part(ref, j):
        return ref[:, j * 128 : (j + 1) * 128]

    for j in range(2):
        own = [half(xa, j), half(xa, 1 - j), half(xb, j), half(xc, j), half(p7, j)]
        got = [part(na, j), part(na, 1 - j), part(nb, j), part(nc, j), part(n7, j)]
        g = tn(jnp.concatenate(own, 1), blk(delta, j)) + tn(jnp.concatenate(got, 1), blk(dn, j))
        for k, bit in enumerate((None, 0, 1, 2, 7)):
            h = g[128 * k : 128 * (k + 1)]
            if bit is not None:
                h = h * gate(info, mask, bit, 2 * i + j)
            keep[k, j] = jnp.where(first, h[:64], h[64:])
            send[k, j] = jnp.where(first, h[64:], h[:64]).astype(BF16)

    @pl.when(i // 2 == info[YLO])
    def _():
        v = tn(co[...], delta[...]) + tn(cn[...], dn[...])

        @pl.when(i == info[DP])
        def _():
            vkeep[...] = v

        @pl.when(i != info[DP])
        def _():
            for k in range(W2 // R):
                vsend[k * R : (k + 1) * R] = v[:, k * R : (k + 1) * R].astype(BF16)


def near_grads(info, mask, x, p7, xn, hn, delta, dn):
    got = [col(B), col(B, lambda i, info: i ^ 1), col(B, lambda i, info: i ^ 2), col(B)]
    spec = pl.BlockSpec((5, 2, 64, B), lambda i, info, mask: (0, i, 0, 0))
    last = col(R, lambda i, info: D // R)
    return call(
        near_grads_body,
        OWN + [col()] + got + [col(), col(), last, last],
        [spec, spec, whole((R, W2)), whole((W2, R))],
        [
            sds((5, NB, 64, B), F32),
            sds((5, NB, 64, B), BF16),
            sds((R, W2), F32),
            sds((W2, R), BF16),
        ],
        10 * T * D * B,
        12 << 20,
        "near_grads",
    )(info, mask, x, x, x, p7, xn, xn, xn, hn, delta, dn, delta, dn)


def grad_u_body(info, mask, x, bc, v, keep, send):
    i = pl.program_id(0)
    g = tn(x[...], bc[...])

    @pl.when(i % 2 == info[CORE])
    def _():
        keep[i // 2] = g

    @pl.when(i % 2 != info[CORE])
    def _():
        send[i // 2] = g.astype(BF16)

    @pl.when(i == 0)
    def _():
        send[2] = v[...]


def grad_u_parts(info, mask, x, bc, v_send):
    return call(
        grad_u_body,
        [col(), whole((T, R)), whole((W2, R))],
        [whole((2, W2, R)), whole((3, W2, R))],
        [sds((2, W2, R), F32), sds((3, W2, R), BF16)],
        2 * T * D * R,
        2 << 20,
        "grad_u",
    )(info, mask, x, bc, v_send)


def grad_u_halves_body(info, mask, keep, got, v_keep, mine, other, grad_v):
    y = info[YLO]
    mine[...] = keep[y] + got[y].astype(F32)
    other[...] = (keep[1 - y] + got[1 - y].astype(F32)).astype(BF16)
    for k in range(W2 // R):
        at = slice(k * R, (k + 1) * R)
        grad_v[:, at] = (v_keep[:, at] + got[2, at].astype(F32)).astype(BF16)


def grad_u_halves(info, mask, keep, got, v_keep):
    return call(
        grad_u_halves_body,
        [whole((2, W2, R)), whole((3, W2, R)), whole((R, W2))],
        [whole((W2, R)), whole((W2, R)), whole((R, W2))],
        [sds((W2, R), F32), sds((W2, R), BF16), sds((R, W2), BF16)],
        0,
        1 << 20,
        "grad_u_halves",
        1,
    )(info, mask, keep, got, v_keep)


def last_body(info, mask, back, sx, sz, t7, bc, u, keep, near, got, before, out, grad_w):
    total = back[...] + nt(bc[...], u[...])
    for t in (sx, sz, t7):
        total += t[...].astype(F32)
    out[...] = total.astype(BF16)
    grad_w[...] = (keep[0] + near[0].astype(F32) + got[...].astype(F32)).astype(BF16)


def last(info, mask, back, terms, bc, low_u, keep, near, got, grad_w):
    half = pl.BlockSpec((1, 1, NB, 64, B), lambda i, info, mask: (info[YLO], i, 0, 0, 0))
    part = (1, NB, 64, B)
    return call(
        last_body,
        [col()] * 4
        + [whole((T, R)), pl.BlockSpec((W2, R), lambda i, info, mask: (i, 0)), half, half]
        + [pl.BlockSpec(part, lambda i, info, mask: (i, 0, 0, 0)), pl.BlockSpec(memory_space=pl.ANY)],
        [col(), pl.BlockSpec(part, lambda i, info, mask: (info[3 + i], 0, 0, 0))],
        [sds((T, D), BF16), sds((9, NB, 64, B), BF16)],
        2 * T * D * R,
        12 << 20,
        "last",
        aliases={11: 1},
    )(info, mask, back, *terms, bc, low_u, keep, near, got, grad_w)


def assemble_body(info, mask, keep, got, out):
    out[...] = (keep[...] + got[...].astype(F32)).astype(BF16)


def assemble(info, mask, keep, got):
    shape = (1, NB, 64, B)

    def place(k, info, mask):
        at = jnp.where(k == 4, info[7], info[jnp.clip(k - 1, 0, 2)])
        return (jnp.where(k == 0, 0, at), 0, 0, 0)

    return call(
        assemble_body,
        [pl.BlockSpec(shape, lambda k, info, mask: (k, 0, 0, 0))] * 2,
        pl.BlockSpec(shape, place),
        sds((9, NB, 64, B), BF16),
        0,
        6 << 20,
        "assemble",
        5,
    )(info, mask, keep, got)


def swap(value, axis, offset):
    sizes = 1
    for name in axis if isinstance(axis, tuple) else (axis,):
        sizes *= lax.axis_size(name)
    return lax.ppermute(value, axis, [(i, i ^ offset) for i in range(sizes)])


def sum_feat(value, offsets):
    for offset in offsets:
        value = value + swap(value, "feat", offset)
    return value


def beside(order, part, *args):
    shapes = jax.eval_shape(part, *args)

    def nothing(*args):
        return jax.tree.map(lambda s: jnp.zeros(s.shape, s.dtype), shapes)

    return lax.cond(order[0] >= 0, part, nothing, *args)


def pick(arr, index, axis=0):
    return lax.dynamic_index_in_dim(arr, index, axis, keepdims=False)


def per_device(x, weights, order, mask, low_u, low_v, cot):
    dp = lax.axis_index("dp").astype(jnp.int32)
    ylo, core = dp // 2, dp % 2
    both = ("feat", "dp")
    levels = jnp.arange(8, dtype=jnp.int32)
    slots = 1 + jnp.sum(jnp.where(order[None, :] == levels[:, None], levels[None, :], 0), 1)
    info = jnp.concatenate([slots, jnp.stack([ylo, core, dp])]).astype(jnp.int32)

    cpart, xs = prolog(info, mask, x, low_u)
    p3, p5, p7 = swap(x, "feat", 1), swap(x, "feat", 4), swap(x, "feat", 16)
    c = sum_feat(cpart, (3, 12))
    c, p3, p5, p7, xs = lax.optimization_barrier((c, p3, p5, p7, xs))
    p4, p6 = swap(p3, "feat", 3), swap(p5, "feat", 12)
    xn = swap(xs, "dp", 2)
    hn = swap(xs, both, 66)
    coeff = sum_feat(c, (1, 4, 16)).astype(BF16)
    mixed = near_mix(info, mask, x, p3, p5, p7, weights)
    coeff, xn, hn, mixed = lax.optimization_barrier((coeff, xn, hn, mixed))
    out, delta, t3, t4, t5, t6, bpart = middle(
        info, mask, mixed, p4, p6, weights, coeff, low_v, cot
    )

    dn = swap(delta, "dp", 2)
    r4, r6 = swap(t4, "feat", 3), swap(t6, "feat", 12)

    def beside_first(p3, p4, p5, p6, delta, bpart):
        b = sum_feat(bpart, (1,))
        b, delta = lax.optimization_barrier((b, delta))
        keep, send = far_grads(info, mask, (p3, p4, p5, p6), delta)
        got = swap(send, "dp", 1)
        away = pick(keep, 1 - ylo) + pick(got, 1 - ylo).astype(F32)
        return sum_feat(b, (4, 16)), keep, got, away.astype(BF16)

    b, far_keep, far_near, far_send = beside(order, beside_first, p3, p4, p5, p6, delta, bpart)
    r4, r6, dn, b, far_send = lax.optimization_barrier((r4, r6, dn, b, far_send))

    sx, sz, hi = second(info, mask, t3, r4, t5, r6, dn, weights)
    sx, sz, hi, b, far_send = lax.optimization_barrier((sx, sz, hi, b, far_send))
    sx, sz, t7 = swap(sx, "feat", 1), swap(sz, "feat", 4), swap(hi, both, 66)
    far_got = swap(far_send, "dp", 2)

    def beside_second(b, x, p7, xn, hn, delta, dn, weights):
        back = local_back(info, mask, delta, weights)
        b, back = lax.optimization_barrier((sum_feat(b, (3,)), back))
        bc = sum_feat(b, (12,)).astype(BF16)
        keep, send, v_keep, v_send = near_grads(info, mask, x, p7, xn, hn, delta, dn)
        bc, send, v_send = lax.optimization_barrier((bc, send, v_send))
        got = swap(send, "dp", 1)
        gu_keep, gu_send = grad_u_parts(info, mask, x, bc, v_send)
        gu_send, got = lax.optimization_barrier((gu_send, got))
        gu_got = swap(gu_send, "dp", 1)
        gu_keep, gu_send, grad_v = grad_u_halves(info, mask, gu_keep, gu_got, v_keep)
        gu_send, got = lax.optimization_barrier((gu_send, got))
        grad_u = (gu_keep + swap(gu_send, "dp", 2).astype(F32)).astype(BF16)
        return back, bc, assemble(info, mask, keep, got), grad_u, grad_v

    back, bc, grad_w, grad_u, grad_v = beside(
        order, beside_second, b, x, p7, xn, hn, delta, dn, weights
    )
    grad_x, grad_w = last(
        info, mask, back, [sx, sz, t7], bc, low_u, far_keep, far_near, far_got, grad_w
    )
    return out, grad_x, grad_w, grad_u, grad_v


def solution(mesh):
    return jax.shard_map(
        per_device,
        mesh=mesh,
        in_specs=(
            P("dp", "feat"),
            P(None, "feat", None, None),
            P(),
            P(None, "feat"),
            P("feat", None),
            P(None, "feat"),
            P("dp", "feat"),
        ),
        out_specs=(
            P("dp", "feat"),
            P("dp", "feat"),
            P(None, "feat", "dp", None),
            P(("feat", "dp"), None),
            P(None, ("feat", "dp")),
        ),
        check_vma=False,
    )
```

```python
import jax
import jax.numpy as jnp
from jax import lax
from jax.experimental import pallas as pl
from jax.experimental.pallas import tpu as pltpu
from jax.sharding import PartitionSpec as P

F32 = jnp.float32
BF16 = jnp.bfloat16
T = 256
D = 2048
B = 256
R = 128
NB = 8
STEPS = 4
W2 = 2 * B
MID, FAR, SEC = 4, 4, 4
YLO, CORE, DP = 8, 9, 10
LIMIT = 52 << 20


def nn(a, b):
    return jnp.dot(a, b, preferred_element_type=F32)


def nt(a, b):
    return lax.dot_general(a, b, (((1,), (1,)), ((), ())), preferred_element_type=F32)


def tn(a, b):
    return lax.dot_general(a, b, (((0,), (0,)), ((), ())), preferred_element_type=F32)


def gelu_parts(value):
    cdf = 0.5 * (1.0 + lax.erf(value * 0.7071067811865476))
    slope = cdf + value * jnp.exp(-0.5 * value * value) * 0.3989422804014327
    return (value * cdf, slope)


def gate(info, mask, bit, block):
    return mask[info[bit] - 1, block].astype(F32)


def call(body, in_specs, out_specs, out_shape, flops, data, name, grid=STEPS, aliases=None):
    return pl.pallas_call(
        body,
        grid_spec=pltpu.PrefetchScalarGridSpec(
            num_scalar_prefetch=2, grid=(grid,), in_specs=in_specs, out_specs=out_specs
        ),
        out_shape=out_shape,
        input_output_aliases=aliases or {},
        compiler_params=pltpu.CompilerParams(
            dimension_semantics=("arbitrary",), vmem_limit_bytes=LIMIT
        ),
        cost_estimate=pl.CostEstimate(flops=flops, bytes_accessed=data, transcendentals=0),
        name=name,
    )


def sds(shape, dtype):
    return jax.ShapeDtypeStruct(shape, dtype)


def col(width=W2, at=lambda i, info: i):
    return pl.BlockSpec((T, width), lambda i, info, mask: (0, at(i, info)))


def whole(shape):
    return pl.BlockSpec(shape, lambda i, info, mask: (0,) * len(shape))


def weight(bit, blocks=2):
    if bit is None:
        return pl.BlockSpec((1, blocks, B, B), lambda i, info, mask: (0, i, 0, 0))
    return pl.BlockSpec((1, blocks, B, B), lambda i, info, mask: (info[bit], i, 0, 0))


def blk(ref, j):
    return ref[:, j * B : (j + 1) * B]


OWN = [col(), col(at=lambda i, info: i ^ 1), col(at=lambda i, info: i ^ 2)]


def prolog_body(info, mask, x, u, cpart, xs):
    @pl.when(pl.program_id(0) == 0)
    def _():
        cpart[...] = jnp.zeros_like(cpart)

    cpart[...] += nn(x[...], u[...])
    for j in range(2):
        b = blk(x, j)
        xs[:, j * 128 : (j + 1) * 128] = jnp.where(info[YLO] == 0, b[:, 128:], b[:, :128])


def prolog(info, mask, x, low_u):
    return call(
        prolog_body,
        [col(), pl.BlockSpec((W2, R), lambda i, info, mask: (i, 0))],
        [whole((T, R)), col(B)],
        [sds((T, R), F32), sds((T, D // 2), BF16)],
        2 * T * D * R,
        3 << 20,
        "prolog",
    )(info, mask, x, low_u)


def near_mix_body(info, mask, xa, xb, xc, p3, p5, p7, w, w0, w1, w2, w3, w5, w7, mixed):
    i = pl.program_id(0)
    for j in range(2):
        total = nn(blk(xa, j), w[0, j])
        for x, k, v, bit in (
            (xa, 1 - j, w0, 0),
            (xb, j, w1, 1),
            (xc, j, w2, 2),
            (p3, j, w3, 3),
            (p5, j, w5, 5),
            (p7, j, w7, 7),
        ):
            total += nn(blk(x, k), v[0, j]) * gate(info, mask, bit, 2 * i + j)
        mixed[:, j * B : (j + 1) * B] = total


def near_mix(info, mask, x, p3, p5, p7, weights):
    return call(
        near_mix_body,
        OWN + [col()] * 3 + [weight(b) for b in (None, 0, 1, 2, 3, 5, 7)],
        col(),
        sds((T, D), F32),
        14 * T * D * B,
        14 << 20,
        "near_mix",
    )(info, mask, x, x, x, p3, p5, p7, *([weights] * 7))


def middle_body(info, mask, mixed, p4, p6, w3, w4, w5, w6, *refs):
    coeff, low_v, cot, out, delta, t3, t4, t5, t6, bpart = refs
    i = pl.program_id(0)

    @pl.when(i == 0)
    def _():
        bpart[...] = jnp.zeros_like(bpart)
        delta[:, D:] = coeff[...]

    for j in range(MID):
        cols = slice(j * B, (j + 1) * B)
        pre = mixed[:, cols] + nn(coeff[...], low_v[:, cols])
        pre += nn(p4[:, cols], w4[0, j]) * gate(info, mask, 4, MID * i + j)
        pre += nn(p6[:, cols], w6[0, j]) * gate(info, mask, 6, MID * i + j)
        act, slope = gelu_parts(pre)
        out[:, cols] = act.astype(BF16)
        d = (cot[:, cols].astype(F32) * slope).astype(BF16)
        delta[:, pl.ds(pl.multiple_of((MID * i + j) * B, B), B)] = d
        bpart[...] += nt(d, low_v[:, cols])
        for bit, t, w in ((4, t4, w4), (6, t6, w6), (3, t3, w3), (5, t5, w5)):
            t[:, cols] = (nt(d, w[0, j]) * gate(info, mask, bit, MID * i + j)).astype(BF16)


def middle(info, mask, mixed, p4, p6, weights, coeff, low_v, cot):
    return call(
        middle_body,
        [col(MID * B)] * 3
        + [weight(b, MID) for b in range(3, 7)]
        + [whole((T, R)), pl.BlockSpec((R, MID * B), lambda i, info, mask: (0, i)), col(MID * B)],
        [col(MID * B), whole((T, D + R))] + [col(MID * B)] * 4 + [whole((T, R))],
        [sds((T, D), BF16), sds((T, D + R), BF16)]
        + [sds((T, D), BF16)] * 4
        + [sds((T, R), F32)],
        12 * T * D * B,
        18 << 20,
        "middle",
        NB // MID,
    )(info, mask, mixed, p4, p6, *([weights] * 4), coeff, low_v, cot)


def far_grads_body(info, mask, p3, p4, p5, p6, delta, keep, send):
    i = pl.program_id(0)
    first = info[CORE] == 0
    for j in range(FAR):
        d = blk(delta, j)
        for k, p in enumerate((p3, p4, p5, p6)):
            g = tn(blk(p, j), d) * gate(info, mask, 3 + k, FAR * i + j)
            for half in range(2):
                lo, hi = g[128 * half : 128 * half + 64], g[128 * half + 64 : 128 * half + 128]
                keep[half, k, j] = jnp.where(first, lo, hi)
                send[half, k, j] = jnp.where(first, hi, lo).astype(BF16)


def far_grads(info, mask, partners, delta):
    spec = pl.BlockSpec((2, 4, FAR, 64, B), lambda i, info, mask: (0, 0, i, 0, 0))
    return call(
        far_grads_body,
        [col(FAR * B)] * 5,
        [spec, spec],
        [sds((2, 4, NB, 64, B), F32), sds((2, 4, NB, 64, B), BF16)],
        8 * T * D * B,
        12 << 20,
        "far_grads",
        NB // FAR,
    )(info, mask, *partners, delta)


def second_body(info, mask, t3, r4, t5, r6, dn, w, sx, sz, hi):
    sx[...] = t3[...] + r4[...]
    sz[...] = t5[...] + r6[...]
    for j in range(SEC):
        g = gate(info, mask, 7, SEC * pl.program_id(0) + j)
        hi[:, j * B : (j + 1) * B] = (nt(blk(dn, j), w[0, j]) * g).astype(BF16)


def second(info, mask, t3, r4, t5, r6, dn, weights):
    return call(
        second_body,
        [col(SEC * B)] * 5 + [weight(7, SEC)],
        [col(SEC * B)] * 3,
        [sds((T, D), BF16)] * 3,
        2 * T * D * B,
        9 << 20,
        "second",
        NB // SEC,
    )(info, mask, t3, r4, t5, r6, dn, weights)


def local_back_body(info, mask, delta, w, w0, w1, w2, back):
    i = pl.program_id(0)

    @pl.when(i == 0)
    def _():
        back[...] = jnp.zeros_like(back)

    def place(step, j):
        return pl.ds(pl.multiple_of(step * W2 + j * B, B), B)

    for j in range(2):
        d, e = blk(delta, j), blk(delta, 1 - j)
        back[:, place(i, j)] += (
            nt(d, w[0, j]) + nt(e, w0[0, 1 - j]) * gate(info, mask, 0, 2 * i + 1 - j)
        )
        back[:, place(i ^ 1, j)] += nt(d, w1[0, j]) * gate(info, mask, 1, 2 * i + j)
        back[:, place(i ^ 2, j)] += nt(d, w2[0, j]) * gate(info, mask, 2, 2 * i + j)


def local_back(info, mask, delta, weights):
    return call(
        local_back_body,
        [col()] + [weight(b) for b in (None, 0, 1, 2)],
        whole((T, D)),
        sds((T, D), F32),
        8 * T * D * B,
        8 << 20,
        "local_back",
    )(info, mask, delta, *([weights] * 4))


def near_grads_body(info, mask, xa, xb, xc, p7, na, nb, nc, n7, delta, dn, co, cn, *outs):
    keep, send, vkeep, vsend = outs
    i = pl.program_id(0)
    first = info[CORE] == 0

    def half(ref, j):
        return ref[:, pl.ds(pl.multiple_of(j * B + info[YLO] * 128, 128), 128)]

    def part(ref, j):
        return ref[:, j * 128 : (j + 1) * 128]

    for j in range(2):
        own = [half(xa, j), half(xa, 1 - j), half(xb, j), half(xc, j), half(p7, j)]
        got = [part(na, j), part(na, 1 - j), part(nb, j), part(nc, j), part(n7, j)]
        g = tn(jnp.concatenate(own, 1), blk(delta, j)) + tn(jnp.concatenate(got, 1), blk(dn, j))
        for k, bit in enumerate((None, 0, 1, 2, 7)):
            h = g[128 * k : 128 * (k + 1)]
            if bit is not None:
                h = h * gate(info, mask, bit, 2 * i + j)
            keep[k, j] = jnp.where(first, h[:64], h[64:])
            send[k, j] = jnp.where(first, h[64:], h[:64]).astype(BF16)

    @pl.when(i // 2 == info[YLO])
    def _():
        v = tn(co[...], delta[...]) + tn(cn[...], dn[...])

        @pl.when(i == info[DP])
        def _():
            vkeep[...] = v

        @pl.when(i != info[DP])
        def _():
            for k in range(W2 // R):
                vsend[k * R : (k + 1) * R] = v[:, k * R : (k + 1) * R].astype(BF16)


def near_grads(info, mask, x, p7, xn, hn, delta, dn):
    got = [col(B), col(B, lambda i, info: i ^ 1), col(B, lambda i, info: i ^ 2), col(B)]
    spec = pl.BlockSpec((5, 2, 64, B), lambda i, info, mask: (0, i, 0, 0))
    last = col(R, lambda i, info: D // R)
    return call(
        near_grads_body,
        OWN + [col()] + got + [col(), col(), last, last],
        [spec, spec, whole((R, W2)), whole((W2, R))],
        [
            sds((5, NB, 64, B), F32),
            sds((5, NB, 64, B), BF16),
            sds((R, W2), F32),
            sds((W2, R), BF16),
        ],
        10 * T * D * B,
        12 << 20,
        "near_grads",
    )(info, mask, x, x, x, p7, xn, xn, xn, hn, delta, dn, delta, dn)


def grad_u_body(info, mask, x, bc, v, keep, send):
    i = pl.program_id(0)
    g = tn(x[...], bc[...])

    @pl.when(i % 2 == info[CORE])
    def _():
        keep[i // 2] = g

    @pl.when(i % 2 != info[CORE])
    def _():
        send[i // 2] = g.astype(BF16)

    @pl.when(i == 0)
    def _():
        send[2] = v[...]


def grad_u_parts(info, mask, x, bc, v_send):
    return call(
        grad_u_body,
        [col(), whole((T, R)), whole((W2, R))],
        [whole((2, W2, R)), whole((3, W2, R))],
        [sds((2, W2, R), F32), sds((3, W2, R), BF16)],
        2 * T * D * R,
        2 << 20,
        "grad_u",
    )(info, mask, x, bc, v_send)


def grad_u_halves_body(info, mask, keep, got, v_keep, mine, other, grad_v):
    y = info[YLO]
    mine[...] = keep[y] + got[y].astype(F32)
    other[...] = (keep[1 - y] + got[1 - y].astype(F32)).astype(BF16)
    for k in range(W2 // R):
        at = slice(k * R, (k + 1) * R)
        grad_v[:, at] = (v_keep[:, at] + got[2, at].astype(F32)).astype(BF16)


def grad_u_halves(info, mask, keep, got, v_keep):
    return call(
        grad_u_halves_body,
        [whole((2, W2, R)), whole((3, W2, R)), whole((R, W2))],
        [whole((W2, R)), whole((W2, R)), whole((R, W2))],
        [sds((W2, R), F32), sds((W2, R), BF16), sds((R, W2), BF16)],
        0,
        1 << 20,
        "grad_u_halves",
        1,
    )(info, mask, keep, got, v_keep)


def last_body(info, mask, back, sx, sz, t7, bc, u, keep, near, got, before, out, grad_w):
    total = back[...] + nt(bc[...], u[...])
    for t in (sx, sz, t7):
        total += t[...].astype(F32)
    out[...] = total.astype(BF16)
    grad_w[...] = (keep[0] + near[0].astype(F32) + got[...].astype(F32)).astype(BF16)


def last(info, mask, back, terms, bc, low_u, keep, near, got, grad_w):
    half = pl.BlockSpec((1, 1, NB, 64, B), lambda i, info, mask: (info[YLO], i, 0, 0, 0))
    part = (1, NB, 64, B)
    return call(
        last_body,
        [col()] * 4
        + [whole((T, R)), pl.BlockSpec((W2, R), lambda i, info, mask: (i, 0)), half, half]
        + [pl.BlockSpec(part, lambda i, info, mask: (i, 0, 0, 0)), pl.BlockSpec(memory_space=pl.ANY)],
        [col(), pl.BlockSpec(part, lambda i, info, mask: (info[3 + i], 0, 0, 0))],
        [sds((T, D), BF16), sds((9, NB, 64, B), BF16)],
        2 * T * D * R,
        12 << 20,
        "last",
        aliases={11: 1},
    )(info, mask, back, *terms, bc, low_u, keep, near, got, grad_w)


def assemble_body(info, mask, keep, got, out):
    out[...] = (keep[...] + got[...].astype(F32)).astype(BF16)


def assemble(info, mask, keep, got):
    shape = (1, NB, 64, B)

    def place(k, info, mask):
        at = jnp.where(k == 4, info[7], info[jnp.clip(k - 1, 0, 2)])
        return (jnp.where(k == 0, 0, at), 0, 0, 0)

    return call(
        assemble_body,
        [pl.BlockSpec(shape, lambda k, info, mask: (k, 0, 0, 0))] * 2,
        pl.BlockSpec(shape, place),
        sds((9, NB, 64, B), BF16),
        0,
        6 << 20,
        "assemble",
        5,
    )(info, mask, keep, got)


def swap(value, axis, offset):
    sizes = 1
    for name in axis if isinstance(axis, tuple) else (axis,):
        sizes *= lax.axis_size(name)
    return lax.ppermute(value, axis, [(i, i ^ offset) for i in range(sizes)])


def sum_feat(value, offsets):
    for offset in offsets:
        value = value + swap(value, "feat", offset)
    return value


def beside(order, part, *args):
    shapes = jax.eval_shape(part, *args)

    def nothing(*args):
        return jax.tree.map(lambda s: jnp.zeros(s.shape, s.dtype), shapes)

    return lax.cond(order[0] >= 0, part, nothing, *args)


def pick(arr, index, axis=0):
    return lax.dynamic_index_in_dim(arr, index, axis, keepdims=False)


def per_device(x, weights, order, mask, low_u, low_v, cot):
    dp = lax.axis_index("dp").astype(jnp.int32)
    ylo, core = dp // 2, dp % 2
    both = ("feat", "dp")
    levels = jnp.arange(8, dtype=jnp.int32)
    slots = 1 + jnp.sum(jnp.where(order[None, :] == levels[:, None], levels[None, :], 0), 1)
    info = jnp.concatenate([slots, jnp.stack([ylo, core, dp])]).astype(jnp.int32)

    cpart, xs = prolog(info, mask, x, low_u)
    p3, p5, p7 = swap(x, "feat", 1), swap(x, "feat", 4), swap(x, "feat", 16)
    c = sum_feat(cpart, (3, 12))
    c, p3, p5, p7, xs = lax.optimization_barrier((c, p3, p5, p7, xs))
    p4, p6 = swap(p3, "feat", 3), swap(p5, "feat", 12)
    xn = swap(xs, "dp", 2)
    hn = swap(xs, both, 66)
    coeff = sum_feat(c, (1, 4, 16)).astype(BF16)
    mixed = near_mix(info, mask, x, p3, p5, p7, weights)
    coeff, xn, hn, mixed = lax.optimization_barrier((coeff, xn, hn, mixed))
    out, delta, t3, t4, t5, t6, bpart = middle(
        info, mask, mixed, p4, p6, weights, coeff, low_v, cot
    )

    dn = swap(delta, "dp", 2)
    r4, r6 = swap(t4, "feat", 3), swap(t6, "feat", 12)

    b = sum_feat(bpart, (1,))

    def beside_first(p3, p4, p5, p6, delta, b, weights):
        back = local_back(info, mask, delta, weights)
        b, back, delta = lax.optimization_barrier((sum_feat(b, (4,)), back, delta))
        keep, send = far_grads(info, mask, (p3, p4, p5, p6), delta)
        b, send = lax.optimization_barrier((sum_feat(b, (16,)), send))
        got = swap(send, "dp", 1)
        away = pick(keep, 1 - ylo) + pick(got, 1 - ylo).astype(F32)
        return sum_feat(b, (3,)), back, keep, got, away.astype(BF16)

    b, back, far_keep, far_near, far_send = beside(
        order, beside_first, p3, p4, p5, p6, delta, b, weights
    )
    r4, r6, dn, b, far_send = lax.optimization_barrier((r4, r6, dn, b, far_send))

    sx, sz, hi = second(info, mask, t3, r4, t5, r6, dn, weights)
    sx, sz, hi, b, far_send = lax.optimization_barrier((sx, sz, hi, b, far_send))
    sx, sz, t7 = swap(sx, "feat", 1), swap(sz, "feat", 4), swap(hi, both, 66)
    far_got = swap(far_send, "dp", 2)

    def beside_second(b, x, p7, xn, hn, delta, dn):
        bc = sum_feat(b, (12,)).astype(BF16)
        keep, send, v_keep, v_send = near_grads(info, mask, x, p7, xn, hn, delta, dn)
        bc, send, v_send = lax.optimization_barrier((bc, send, v_send))
        got = swap(send, "dp", 1)
        gu_keep, gu_send = grad_u_parts(info, mask, x, bc, v_send)
        gu_send, got = lax.optimization_barrier((gu_send, got))
        gu_got = swap(gu_send, "dp", 1)
        gu_keep, gu_send, grad_v = grad_u_halves(info, mask, gu_keep, gu_got, v_keep)
        gu_send, got = lax.optimization_barrier((gu_send, got))
        grad_u = (gu_keep + swap(gu_send, "dp", 2).astype(F32)).astype(BF16)
        return bc, assemble(info, mask, keep, got), grad_u, grad_v

    bc, grad_w, grad_u, grad_v = beside(order, beside_second, b, x, p7, xn, hn, delta, dn)
    grad_x, grad_w = last(
        info, mask, back, [sx, sz, t7], bc, low_u, far_keep, far_near, far_got, grad_w
    )
    return out, grad_x, grad_w, grad_u, grad_v


def solution(mesh):
    return jax.shard_map(
        per_device,
        mesh=mesh,
        in_specs=(
            P("dp", "feat"),
            P(None, "feat", None, None),
            P(),
            P(None, "feat"),
            P("feat", None),
            P(None, "feat"),
            P("dp", "feat"),
        ),
        out_specs=(
            P("dp", "feat"),
            P("dp", "feat"),
            P(None, "feat", "dp", None),
            P(("feat", "dp"), None),
            P(None, ("feat", "dp")),
        ),
        check_vma=False,
    )
```

```python
import jax
import jax.numpy as jnp
from jax import lax
from jax.experimental import pallas as pl
from jax.experimental.pallas import tpu as pltpu
from jax.sharding import PartitionSpec as P

F32 = jnp.float32
BF16 = jnp.bfloat16
T = 256
D = 2048
B = 256
R = 128
NB = 8
STEPS = 4
W2 = 2 * B
MID, FAR, SEC = 4, 4, 4
YLO, CORE, DP = 8, 9, 10
LIMIT = 52 << 20


def nn(a, b):
    return jnp.dot(a, b, preferred_element_type=F32)


def nt(a, b):
    return lax.dot_general(a, b, (((1,), (1,)), ((), ())), preferred_element_type=F32)


def tn(a, b):
    return lax.dot_general(a, b, (((0,), (0,)), ((), ())), preferred_element_type=F32)


def gelu_parts(value):
    cdf = 0.5 * (1.0 + lax.erf(value * 0.7071067811865476))
    slope = cdf + value * jnp.exp(-0.5 * value * value) * 0.3989422804014327
    return (value * cdf, slope)


def gate(info, mask, bit, block):
    return mask[info[bit] - 1, block].astype(F32)


def call(body, in_specs, out_specs, out_shape, flops, data, name, grid=STEPS, aliases=None):
    return pl.pallas_call(
        body,
        grid_spec=pltpu.PrefetchScalarGridSpec(
            num_scalar_prefetch=2, grid=(grid,), in_specs=in_specs, out_specs=out_specs
        ),
        out_shape=out_shape,
        input_output_aliases=aliases or {},
        compiler_params=pltpu.CompilerParams(
            dimension_semantics=("arbitrary",), vmem_limit_bytes=LIMIT
        ),
        cost_estimate=pl.CostEstimate(flops=flops, bytes_accessed=data, transcendentals=0),
        name=name,
    )


def sds(shape, dtype):
    return jax.ShapeDtypeStruct(shape, dtype)


def col(width=W2, at=lambda i, info: i):
    return pl.BlockSpec((T, width), lambda i, info, mask: (0, at(i, info)))


def whole(shape):
    return pl.BlockSpec(shape, lambda i, info, mask: (0,) * len(shape))


def weight(bit, blocks=2):
    if bit is None:
        return pl.BlockSpec((1, blocks, B, B), lambda i, info, mask: (0, i, 0, 0))
    return pl.BlockSpec((1, blocks, B, B), lambda i, info, mask: (info[bit], i, 0, 0))


def blk(ref, j):
    return ref[:, j * B : (j + 1) * B]


OWN = [col(), col(at=lambda i, info: i ^ 1), col(at=lambda i, info: i ^ 2)]


def prolog_body(info, mask, x, u, cpart, xs):
    @pl.when(pl.program_id(0) == 0)
    def _():
        cpart[...] = jnp.zeros_like(cpart)

    cpart[...] += nn(x[...], u[...])
    for j in range(2):
        b = blk(x, j)
        xs[:, j * 128 : (j + 1) * 128] = jnp.where(info[YLO] == 0, b[:, 128:], b[:, :128])


def prolog(info, mask, x, low_u):
    return call(
        prolog_body,
        [col(), pl.BlockSpec((W2, R), lambda i, info, mask: (i, 0))],
        [whole((T, R)), col(B)],
        [sds((T, R), F32), sds((T, D // 2), BF16)],
        2 * T * D * R,
        3 << 20,
        "prolog",
    )(info, mask, x, low_u)


def near_mix_body(info, mask, xa, xb, xc, p3, p5, p7, w, w0, w1, w2, w3, w5, w7, mixed):
    i = pl.program_id(0)
    for j in range(2):
        total = nn(blk(xa, j), w[0, j])
        for x, k, v, bit in (
            (xa, 1 - j, w0, 0),
            (xb, j, w1, 1),
            (xc, j, w2, 2),
            (p3, j, w3, 3),
            (p5, j, w5, 5),
            (p7, j, w7, 7),
        ):
            total += nn(blk(x, k), v[0, j]) * gate(info, mask, bit, 2 * i + j)
        mixed[:, j * B : (j + 1) * B] = total


def near_mix(info, mask, x, p3, p5, p7, weights):
    return call(
        near_mix_body,
        OWN + [col()] * 3 + [weight(b) for b in (None, 0, 1, 2, 3, 5, 7)],
        col(),
        sds((T, D), F32),
        14 * T * D * B,
        14 << 20,
        "near_mix",
    )(info, mask, x, x, x, p3, p5, p7, *([weights] * 7))


def middle_body(info, mask, mixed, p4, p6, w3, w4, w5, w6, *refs):
    coeff, low_v, cot, out, delta, t3, t4, t5, t6, bpart = refs
    i = pl.program_id(0)

    @pl.when(i == 0)
    def _():
        bpart[...] = jnp.zeros_like(bpart)
        delta[:, D:] = coeff[...]

    for j in range(MID):
        cols = slice(j * B, (j + 1) * B)
        pre = mixed[:, cols] + nn(coeff[...], low_v[:, cols])
        pre += nn(p4[:, cols], w4[0, j]) * gate(info, mask, 4, MID * i + j)
        pre += nn(p6[:, cols], w6[0, j]) * gate(info, mask, 6, MID * i + j)
        act, slope = gelu_parts(pre)
        out[:, cols] = act.astype(BF16)
        d = (cot[:, cols].astype(F32) * slope).astype(BF16)
        delta[:, pl.ds(pl.multiple_of((MID * i + j) * B, B), B)] = d
        bpart[...] += nt(d, low_v[:, cols])
        for bit, t, w in ((4, t4, w4), (6, t6, w6), (3, t3, w3), (5, t5, w5)):
            t[:, cols] = (nt(d, w[0, j]) * gate(info, mask, bit, MID * i + j)).astype(BF16)


def middle(info, mask, mixed, p4, p6, weights, coeff, low_v, cot):
    return call(
        middle_body,
        [col(MID * B)] * 3
        + [weight(b, MID) for b in range(3, 7)]
        + [whole((T, R)), pl.BlockSpec((R, MID * B), lambda i, info, mask: (0, i)), col(MID * B)],
        [col(MID * B), whole((T, D + R))] + [col(MID * B)] * 4 + [whole((T, R))],
        [sds((T, D), BF16), sds((T, D + R), BF16)]
        + [sds((T, D), BF16)] * 4
        + [sds((T, R), F32)],
        12 * T * D * B,
        18 << 20,
        "middle",
        NB // MID,
    )(info, mask, mixed, p4, p6, *([weights] * 4), coeff, low_v, cot)


def far_grads_body(info, mask, p3, p4, p5, p6, delta, keep, send):
    i = pl.program_id(0)
    first = info[CORE] == 0
    for j in range(FAR):
        d = blk(delta, j)
        for k, p in enumerate((p3, p4, p5, p6)):
            g = tn(blk(p, j), d) * gate(info, mask, 3 + k, FAR * i + j)
            for half in range(2):
                lo, hi = g[128 * half : 128 * half + 64], g[128 * half + 64 : 128 * half + 128]
                keep[half, k, j] = jnp.where(first, lo, hi)
                send[half, k, j] = jnp.where(first, hi, lo).astype(BF16)


def far_grads(info, mask, partners, delta):
    spec = pl.BlockSpec((2, 4, FAR, 64, B), lambda i, info, mask: (0, 0, i, 0, 0))
    return call(
        far_grads_body,
        [col(FAR * B)] * 5,
        [spec, spec],
        [sds((2, 4, NB, 64, B), F32), sds((2, 4, NB, 64, B), BF16)],
        8 * T * D * B,
        12 << 20,
        "far_grads",
        NB // FAR,
    )(info, mask, *partners, delta)


def second_body(info, mask, t3, r4, t5, r6, dn, w, sx, sz, hi):
    sx[...] = t3[...] + r4[...]
    sz[...] = t5[...] + r6[...]
    for j in range(SEC):
        g = gate(info, mask, 7, SEC * pl.program_id(0) + j)
        hi[:, j * B : (j + 1) * B] = (nt(blk(dn, j), w[0, j]) * g).astype(BF16)


def second(info, mask, t3, r4, t5, r6, dn, weights):
    return call(
        second_body,
        [col(SEC * B)] * 5 + [weight(7, SEC)],
        [col(SEC * B)] * 3,
        [sds((T, D), BF16)] * 3,
        2 * T * D * B,
        9 << 20,
        "second",
        NB // SEC,
    )(info, mask, t3, r4, t5, r6, dn, weights)


def local_back_body(info, mask, delta, w, w0, w1, w2, back):
    i = pl.program_id(0)

    @pl.when(i == 0)
    def _():
        back[...] = jnp.zeros_like(back)

    def place(step, j):
        return pl.ds(pl.multiple_of(step * W2 + j * B, B), B)

    for j in range(2):
        d, e = blk(delta, j), blk(delta, 1 - j)
        back[:, place(i, j)] += (
            nt(d, w[0, j]) + nt(e, w0[0, 1 - j]) * gate(info, mask, 0, 2 * i + 1 - j)
        )
        back[:, place(i ^ 1, j)] += nt(d, w1[0, j]) * gate(info, mask, 1, 2 * i + j)
        back[:, place(i ^ 2, j)] += nt(d, w2[0, j]) * gate(info, mask, 2, 2 * i + j)


def local_back(info, mask, delta, weights):
    return call(
        local_back_body,
        [col()] + [weight(b) for b in (None, 0, 1, 2)],
        whole((T, D)),
        sds((T, D), F32),
        8 * T * D * B,
        8 << 20,
        "local_back",
    )(info, mask, delta, *([weights] * 4))


def near_grads_body(info, mask, xa, xb, xc, p7, na, nb, nc, n7, delta, dn, co, cn, *outs):
    keep, send, vkeep, vsend = outs
    i = pl.program_id(0)
    first = info[CORE] == 0

    def half(ref, j):
        return ref[:, pl.ds(pl.multiple_of(j * B + info[YLO] * 128, 128), 128)]

    def part(ref, j):
        return ref[:, j * 128 : (j + 1) * 128]

    for j in range(2):
        own = [half(xa, j), half(xa, 1 - j), half(xb, j), half(xc, j), half(p7, j)]
        got = [part(na, j), part(na, 1 - j), part(nb, j), part(nc, j), part(n7, j)]
        g = tn(jnp.concatenate(own, 1), blk(delta, j)) + tn(jnp.concatenate(got, 1), blk(dn, j))
        for k, bit in enumerate((None, 0, 1, 2, 7)):
            h = g[128 * k : 128 * (k + 1)]
            if bit is not None:
                h = h * gate(info, mask, bit, 2 * i + j)
            keep[k, j] = jnp.where(first, h[:64], h[64:])
            send[k, j] = jnp.where(first, h[64:], h[:64]).astype(BF16)

    @pl.when(i // 2 == info[YLO])
    def _():
        v = tn(co[...], delta[...]) + tn(cn[...], dn[...])

        @pl.when(i == info[DP])
        def _():
            vkeep[...] = v

        @pl.when(i != info[DP])
        def _():
            for k in range(W2 // R):
                vsend[k * R : (k + 1) * R] = v[:, k * R : (k + 1) * R].astype(BF16)


def near_grads(info, mask, x, p7, xn, hn, delta, dn):
    got = [col(B), col(B, lambda i, info: i ^ 1), col(B, lambda i, info: i ^ 2), col(B)]
    spec = pl.BlockSpec((5, 2, 64, B), lambda i, info, mask: (0, i, 0, 0))
    last = col(R, lambda i, info: D // R)
    return call(
        near_grads_body,
        OWN + [col()] + got + [col(), col(), last, last],
        [spec, spec, whole((R, W2)), whole((W2, R))],
        [
            sds((5, NB, 64, B), F32),
            sds((5, NB, 64, B), BF16),
            sds((R, W2), F32),
            sds((W2, R), BF16),
        ],
        10 * T * D * B,
        12 << 20,
        "near_grads",
    )(info, mask, x, x, x, p7, xn, xn, xn, hn, delta, dn, delta, dn)


def grad_u_body(info, mask, x, bc, v, keep, send):
    i = pl.program_id(0)
    g = tn(x[...], bc[...])

    @pl.when(i % 2 == info[CORE])
    def _():
        keep[i // 2] = g

    @pl.when(i % 2 != info[CORE])
    def _():
        send[i // 2] = g.astype(BF16)

    @pl.when(i == 0)
    def _():
        send[2] = v[...]


def grad_u_parts(info, mask, x, bc, v_send):
    return call(
        grad_u_body,
        [col(), whole((T, R)), whole((W2, R))],
        [whole((2, W2, R)), whole((3, W2, R))],
        [sds((2, W2, R), F32), sds((3, W2, R), BF16)],
        2 * T * D * R,
        2 << 20,
        "grad_u",
    )(info, mask, x, bc, v_send)


def grad_u_halves_body(info, mask, keep, got, v_keep, mine, other, grad_v):
    y = info[YLO]
    mine[...] = keep[y] + got[y].astype(F32)
    other[...] = (keep[1 - y] + got[1 - y].astype(F32)).astype(BF16)
    for k in range(W2 // R):
        at = slice(k * R, (k + 1) * R)
        grad_v[:, at] = (v_keep[:, at] + got[2, at].astype(F32)).astype(BF16)


def grad_u_halves(info, mask, keep, got, v_keep):
    return call(
        grad_u_halves_body,
        [whole((2, W2, R)), whole((3, W2, R)), whole((R, W2))],
        [whole((W2, R)), whole((W2, R)), whole((R, W2))],
        [sds((W2, R), F32), sds((W2, R), BF16), sds((R, W2), BF16)],
        0,
        1 << 20,
        "grad_u_halves",
        1,
    )(info, mask, keep, got, v_keep)


def last_body(info, mask, back, sx, sz, t7, bc, u, keep, near, got, before, out, grad_w):
    total = back[...] + nt(bc[...], u[...])
    for t in (sx, sz, t7):
        total += t[...].astype(F32)
    out[...] = total.astype(BF16)
    grad_w[...] = (keep[0] + near[0].astype(F32) + got[...].astype(F32)).astype(BF16)


def last(info, mask, back, terms, bc, low_u, keep, near, got, grad_w):
    half = pl.BlockSpec((1, 1, NB, 64, B), lambda i, info, mask: (info[YLO], i, 0, 0, 0))
    part = (1, NB, 64, B)
    return call(
        last_body,
        [col()] * 4
        + [whole((T, R)), pl.BlockSpec((W2, R), lambda i, info, mask: (i, 0)), half, half]
        + [pl.BlockSpec(part, lambda i, info, mask: (i, 0, 0, 0)), pl.BlockSpec(memory_space=pl.ANY)],
        [col(), pl.BlockSpec(part, lambda i, info, mask: (info[3 + i], 0, 0, 0))],
        [sds((T, D), BF16), sds((9, NB, 64, B), BF16)],
        2 * T * D * R,
        12 << 20,
        "last",
        aliases={11: 1},
    )(info, mask, back, *terms, bc, low_u, keep, near, got, grad_w)


def assemble_body(info, mask, keep, got, out):
    out[...] = (keep[...] + got[...].astype(F32)).astype(BF16)


def assemble(info, mask, keep, got):
    shape = (1, NB, 64, B)

    def place(k, info, mask):
        at = jnp.where(k == 4, info[7], info[jnp.clip(k - 1, 0, 2)])
        return (jnp.where(k == 0, 0, at), 0, 0, 0)

    return call(
        assemble_body,
        [pl.BlockSpec(shape, lambda k, info, mask: (k, 0, 0, 0))] * 2,
        pl.BlockSpec(shape, place),
        sds((9, NB, 64, B), BF16),
        0,
        6 << 20,
        "assemble",
        5,
    )(info, mask, keep, got)


def swap(value, axis, offset):
    sizes = 1
    for name in axis if isinstance(axis, tuple) else (axis,):
        sizes *= lax.axis_size(name)
    return lax.ppermute(value, axis, [(i, i ^ offset) for i in range(sizes)])


def sum_feat(value, offsets):
    for offset in offsets:
        value = value + swap(value, "feat", offset)
    return value


def beside(order, part, *args):
    shapes = jax.eval_shape(part, *args)

    def nothing(*args):
        return jax.tree.map(lambda s: jnp.zeros(s.shape, s.dtype), shapes)

    return lax.cond(order[0] >= 0, part, nothing, *args)


def pick(arr, index, axis=0):
    return lax.dynamic_index_in_dim(arr, index, axis, keepdims=False)


def per_device(x, weights, order, mask, low_u, low_v, cot):
    dp = lax.axis_index("dp").astype(jnp.int32)
    ylo, core = dp // 2, dp % 2
    both = ("feat", "dp")
    levels = jnp.arange(8, dtype=jnp.int32)
    slots = 1 + jnp.sum(jnp.where(order[None, :] == levels[:, None], levels[None, :], 0), 1)
    info = jnp.concatenate([slots, jnp.stack([ylo, core, dp])]).astype(jnp.int32)

    cpart, xs = prolog(info, mask, x, low_u)
    p3, p5, p7 = swap(x, "feat", 1), swap(x, "feat", 4), swap(x, "feat", 16)
    c = sum_feat(cpart, (3, 12))
    c, p3, p5, xs = lax.optimization_barrier((c, p3, p5, xs))
    p4, p6 = swap(p3, "feat", 3), swap(p5, "feat", 12)
    xn = swap(xs, "dp", 2)
    hn = swap(xs, both, 66)
    coeff = sum_feat(c, (1, 4, 16)).astype(BF16)
    mixed = near_mix(info, mask, x, p3, p5, p7, weights)
    coeff, xn, hn, mixed = lax.optimization_barrier((coeff, xn, hn, mixed))
    out, delta, t3, t4, t5, t6, bpart = middle(
        info, mask, mixed, p4, p6, weights, coeff, low_v, cot
    )

    dn = swap(delta, "dp", 2)
    r4, r6 = swap(t4, "feat", 3), swap(t6, "feat", 12)

    far_keep, far_send = far_grads(info, mask, (p3, p4, p5, p6), delta)
    b = sum_feat(bpart, (1,))

    def beside_first(keep, send, delta, b, weights):
        got = swap(send, "dp", 1)
        back = local_back(info, mask, delta, weights)
        away = pick(keep, 1 - ylo) + pick(got, 1 - ylo).astype(F32)
        return sum_feat(b, (4,)), back, got, away.astype(BF16)

    b, back, far_near, far_send = beside(
        order, beside_first, far_keep, far_send, delta, b, weights
    )
    r4, r6, dn, b, far_send = lax.optimization_barrier((r4, r6, dn, b, far_send))

    sx, sz, hi = second(info, mask, t3, r4, t5, r6, dn, weights)
    b = sum_feat(b, (16,))
    sx, sz, hi, b, far_send = lax.optimization_barrier((sx, sz, hi, b, far_send))
    sx, sz, t7 = swap(sx, "feat", 1), swap(sz, "feat", 4), swap(hi, both, 66)
    far_got = swap(far_send, "dp", 2)

    def beside_second(b, x, p7, xn, hn, delta, dn):
        b, dn = lax.optimization_barrier((b, dn))
        b = sum_feat(b, (3,))
        keep, send, v_keep, v_send = near_grads(info, mask, x, p7, xn, hn, delta, dn)
        b, send, v_send = lax.optimization_barrier((b, send, v_send))
        bc = sum_feat(b, (12,)).astype(BF16)
        bc, send, v_send = lax.optimization_barrier((bc, send, v_send))
        got = swap(send, "dp", 1)
        gu_keep, gu_send = grad_u_parts(info, mask, x, bc, v_send)
        gu_send, got = lax.optimization_barrier((gu_send, got))
        gu_got = swap(gu_send, "dp", 1)
        gu_keep, gu_send, grad_v = grad_u_halves(info, mask, gu_keep, gu_got, v_keep)
        gu_send, got = lax.optimization_barrier((gu_send, got))
        grad_u = (gu_keep + swap(gu_send, "dp", 2).astype(F32)).astype(BF16)
        return bc, assemble(info, mask, keep, got), grad_u, grad_v

    bc, grad_w, grad_u, grad_v = beside(order, beside_second, b, x, p7, xn, hn, delta, dn)
    grad_x, grad_w = last(
        info, mask, back, [sx, sz, t7], bc, low_u, far_keep, far_near, far_got, grad_w
    )
    return out, grad_x, grad_w, grad_u, grad_v


def solution(mesh):
    return jax.shard_map(
        per_device,
        mesh=mesh,
        in_specs=(
            P("dp", "feat"),
            P(None, "feat", None, None),
            P(),
            P(None, "feat"),
            P("feat", None),
            P(None, "feat"),
            P("dp", "feat"),
        ),
        out_specs=(
            P("dp", "feat"),
            P("dp", "feat"),
            P(None, "feat", "dp", None),
            P(("feat", "dp"), None),
            P(None, ("feat", "dp")),
        ),
        check_vma=False,
    )
```

```python
import jax
import jax.numpy as jnp
from jax import lax
from jax.experimental import pallas as pl
from jax.experimental.pallas import tpu as pltpu
from jax.sharding import PartitionSpec as P

F32 = jnp.float32
BF16 = jnp.bfloat16
T = 256
D = 2048
B = 256
R = 128
NB = 8
STEPS = 4
W2 = 2 * B
MID, FAR, SEC = 4, 4, 4
YLO, CORE, DP = 8, 9, 10
LIMIT = 60 << 20


def nn(a, b):
    return jnp.dot(a, b, preferred_element_type=F32)


def nt(a, b):
    return lax.dot_general(a, b, (((1,), (1,)), ((), ())), preferred_element_type=F32)


def tn(a, b):
    return lax.dot_general(a, b, (((0,), (0,)), ((), ())), preferred_element_type=F32)


def gelu_parts(value):
    cdf = 0.5 * (1.0 + lax.erf(value * 0.7071067811865476))
    slope = cdf + value * jnp.exp(-0.5 * value * value) * 0.3989422804014327
    return (value * cdf, slope)


def gate(info, mask, bit, block):
    return mask[info[bit] - 1, block].astype(F32)


def call(body, in_specs, out_specs, out_shape, flops, data, name, grid=STEPS, aliases=None):
    return pl.pallas_call(
        body,
        grid_spec=pltpu.PrefetchScalarGridSpec(
            num_scalar_prefetch=2, grid=(grid,), in_specs=in_specs, out_specs=out_specs
        ),
        out_shape=out_shape,
        input_output_aliases=aliases or {},
        compiler_params=pltpu.CompilerParams(
            dimension_semantics=("arbitrary",), vmem_limit_bytes=LIMIT
        ),
        cost_estimate=pl.CostEstimate(flops=flops, bytes_accessed=data, transcendentals=0),
        name=name,
    )


def sds(shape, dtype):
    return jax.ShapeDtypeStruct(shape, dtype)


def col(width=W2, at=lambda i, info: i):
    return pl.BlockSpec((T, width), lambda i, info, mask: (0, at(i, info)))


def whole(shape):
    return pl.BlockSpec(shape, lambda i, info, mask: (0,) * len(shape))


def weight(bit, blocks=2):
    if bit is None:
        return pl.BlockSpec((1, blocks, B, B), lambda i, info, mask: (0, i, 0, 0))
    return pl.BlockSpec((1, blocks, B, B), lambda i, info, mask: (info[bit], i, 0, 0))


def blk(ref, j):
    return ref[:, j * B : (j + 1) * B]


OWN = [col(), col(at=lambda i, info: i ^ 1), col(at=lambda i, info: i ^ 2)]


def prolog_body(info, mask, x, u, cpart, xs):
    @pl.when(pl.program_id(0) == 0)
    def _():
        cpart[...] = jnp.zeros_like(cpart)

    cpart[...] += nn(x[...], u[...])
    for j in range(2):
        b = blk(x, j)
        xs[:, j * 128 : (j + 1) * 128] = jnp.where(info[YLO] == 0, b[:, 128:], b[:, :128])


def prolog(info, mask, x, low_u):
    return call(
        prolog_body,
        [col(), pl.BlockSpec((W2, R), lambda i, info, mask: (i, 0))],
        [whole((T, R)), col(B)],
        [sds((T, R), F32), sds((T, D // 2), BF16)],
        2 * T * D * R,
        3 << 20,
        "prolog",
    )(info, mask, x, low_u)


def near_mix_body(info, mask, xa, xb, xc, p3, p5, p7, w, w0, w1, w2, w3, w5, w7, mixed):
    i = pl.program_id(0)
    for j in range(2):
        total = nn(blk(xa, j), w[0, j])
        for x, k, v, bit in (
            (xa, 1 - j, w0, 0),
            (xb, j, w1, 1),
            (xc, j, w2, 2),
            (p3, j, w3, 3),
            (p5, j, w5, 5),
            (p7, j, w7, 7),
        ):
            total += nn(blk(x, k), v[0, j]) * gate(info, mask, bit, 2 * i + j)
        mixed[:, j * B : (j + 1) * B] = total


def near_mix(info, mask, x, p3, p5, p7, weights):
    return call(
        near_mix_body,
        OWN + [col()] * 3 + [weight(b) for b in (None, 0, 1, 2, 3, 5, 7)],
        col(),
        sds((T, D), F32),
        14 * T * D * B,
        14 << 20,
        "near_mix",
    )(info, mask, x, x, x, p3, p5, p7, *([weights] * 7))


def middle_body(info, mask, mixed, p4, p6, w3, w4, w5, w6, *refs):
    coeff, low_v, cot, out, delta, t3, t4, t5, t6, bpart = refs
    i = pl.program_id(0)

    @pl.when(i == 0)
    def _():
        bpart[...] = jnp.zeros_like(bpart)
        delta[:, D:] = coeff[...]

    for j in range(MID):
        cols = slice(j * B, (j + 1) * B)
        pre = mixed[:, cols] + nn(coeff[...], low_v[:, cols])
        pre += nn(p4[:, cols], w4[0, j]) * gate(info, mask, 4, MID * i + j)
        pre += nn(p6[:, cols], w6[0, j]) * gate(info, mask, 6, MID * i + j)
        act, slope = gelu_parts(pre)
        out[:, cols] = act.astype(BF16)
        d = (cot[:, cols].astype(F32) * slope).astype(BF16)
        delta[:, pl.ds(pl.multiple_of((MID * i + j) * B, B), B)] = d
        bpart[...] += nt(d, low_v[:, cols])
        for bit, t, w in ((4, t4, w4), (6, t6, w6), (3, t3, w3), (5, t5, w5)):
            t[:, cols] = (nt(d, w[0, j]) * gate(info, mask, bit, MID * i + j)).astype(BF16)


def middle(info, mask, mixed, p4, p6, weights, coeff, low_v, cot):
    return call(
        middle_body,
        [col(MID * B)] * 3
        + [weight(b, MID) for b in range(3, 7)]
        + [whole((T, R)), pl.BlockSpec((R, MID * B), lambda i, info, mask: (0, i)), col(MID * B)],
        [col(MID * B), whole((T, D + R))] + [col(MID * B)] * 4 + [whole((T, R))],
        [sds((T, D), BF16), sds((T, D + R), BF16)]
        + [sds((T, D), BF16)] * 4
        + [sds((T, R), F32)],
        12 * T * D * B,
        18 << 20,
        "middle",
        NB // MID,
    )(info, mask, mixed, p4, p6, *([weights] * 4), coeff, low_v, cot)


def far_grads_body(info, mask, p3, p4, p5, p6, delta, keep, send):
    i = pl.program_id(0)
    first = info[CORE] == 0
    for j in range(FAR):
        d = blk(delta, j)
        for k, p in enumerate((p3, p4, p5, p6)):
            g = tn(blk(p, j), d) * gate(info, mask, 3 + k, FAR * i + j)
            for half in range(2):
                lo, hi = g[128 * half : 128 * half + 64], g[128 * half + 64 : 128 * half + 128]
                keep[half, k, j] = jnp.where(first, lo, hi)
                send[half, k, j] = jnp.where(first, hi, lo).astype(BF16)


def far_grads(info, mask, partners, delta):
    spec = pl.BlockSpec((2, 4, FAR, 64, B), lambda i, info, mask: (0, 0, i, 0, 0))
    return call(
        far_grads_body,
        [col(FAR * B)] * 5,
        [spec, spec],
        [sds((2, 4, NB, 64, B), F32), sds((2, 4, NB, 64, B), BF16)],
        8 * T * D * B,
        12 << 20,
        "far_grads",
        NB // FAR,
    )(info, mask, *partners, delta)


def second_body(info, mask, t3, r4, t5, r6, dn, w, sx, sz, hi):
    sx[...] = t3[...] + r4[...]
    sz[...] = t5[...] + r6[...]
    for j in range(SEC):
        g = gate(info, mask, 7, SEC * pl.program_id(0) + j)
        hi[:, j * B : (j + 1) * B] = (nt(blk(dn, j), w[0, j]) * g).astype(BF16)


def second(info, mask, t3, r4, t5, r6, dn, weights):
    return call(
        second_body,
        [col(SEC * B)] * 5 + [weight(7, SEC)],
        [col(SEC * B)] * 3,
        [sds((T, D), BF16)] * 3,
        2 * T * D * B,
        9 << 20,
        "second",
        NB // SEC,
    )(info, mask, t3, r4, t5, r6, dn, weights)


def local_back_body(info, mask, delta, w, w0, w1, w2, back):
    i = pl.program_id(0)

    @pl.when(i == 0)
    def _():
        back[...] = jnp.zeros_like(back)

    def place(step, j):
        return pl.ds(pl.multiple_of(step * W2 + j * B, B), B)

    for j in range(2):
        d, e = blk(delta, j), blk(delta, 1 - j)
        back[:, place(i, j)] += (
            nt(d, w[0, j]) + nt(e, w0[0, 1 - j]) * gate(info, mask, 0, 2 * i + 1 - j)
        )
        back[:, place(i ^ 1, j)] += nt(d, w1[0, j]) * gate(info, mask, 1, 2 * i + j)
        back[:, place(i ^ 2, j)] += nt(d, w2[0, j]) * gate(info, mask, 2, 2 * i + j)


def local_back(info, mask, delta, weights):
    return call(
        local_back_body,
        [col()] + [weight(b) for b in (None, 0, 1, 2)],
        whole((T, D)),
        sds((T, D), F32),
        8 * T * D * B,
        8 << 20,
        "local_back",
    )(info, mask, delta, *([weights] * 4))


def near_grads_body(info, mask, xa, xb, xc, p7, na, nb, nc, n7, delta, dn, co, cn, *outs):
    keep, send, vkeep, vsend = outs
    i = pl.program_id(0)
    first = info[CORE] == 0

    def half(ref, j):
        return ref[:, pl.ds(pl.multiple_of(j * B + info[YLO] * 128, 128), 128)]

    def part(ref, j):
        return ref[:, j * 128 : (j + 1) * 128]

    for j in range(2):
        own = [half(xa, j), half(xa, 1 - j), half(xb, j), half(xc, j), half(p7, j)]
        got = [part(na, j), part(na, 1 - j), part(nb, j), part(nc, j), part(n7, j)]
        g = tn(jnp.concatenate(own, 1), blk(delta, j)) + tn(jnp.concatenate(got, 1), blk(dn, j))
        for k, bit in enumerate((None, 0, 1, 2, 7)):
            h = g[128 * k : 128 * (k + 1)]
            if bit is not None:
                h = h * gate(info, mask, bit, 2 * i + j)
            keep[k, j] = jnp.where(first, h[:64], h[64:])
            send[k, j] = jnp.where(first, h[64:], h[:64]).astype(BF16)

    @pl.when(i // 2 == info[YLO])
    def _():
        v = tn(co[...], delta[...]) + tn(cn[...], dn[...])

        @pl.when(i == info[DP])
        def _():
            vkeep[...] = v

        @pl.when(i != info[DP])
        def _():
            for k in range(W2 // R):
                vsend[k * R : (k + 1) * R] = v[:, k * R : (k + 1) * R].astype(BF16)


def near_grads(info, mask, x, p7, xn, hn, delta, dn):
    got = [col(B), col(B, lambda i, info: i ^ 1), col(B, lambda i, info: i ^ 2), col(B)]
    spec = pl.BlockSpec((5, 2, 64, B), lambda i, info, mask: (0, i, 0, 0))
    last = col(R, lambda i, info: D // R)
    return call(
        near_grads_body,
        OWN + [col()] + got + [col(), col(), last, last],
        [spec, spec, whole((R, W2)), whole((W2, R))],
        [
            sds((5, NB, 64, B), F32),
            sds((5, NB, 64, B), BF16),
            sds((R, W2), F32),
            sds((W2, R), BF16),
        ],
        10 * T * D * B,
        12 << 20,
        "near_grads",
    )(info, mask, x, x, x, p7, xn, xn, xn, hn, delta, dn, delta, dn)


def grad_u_body(info, mask, x, bc, v, keep, send):
    i = pl.program_id(0)
    g = tn(x[...], bc[...])

    @pl.when(i % 2 == info[CORE])
    def _():
        keep[i // 2] = g

    @pl.when(i % 2 != info[CORE])
    def _():
        send[i // 2] = g.astype(BF16)

    @pl.when(i == 0)
    def _():
        send[2] = v[...]


def grad_u_parts(info, mask, x, bc, v_send):
    return call(
        grad_u_body,
        [col(), whole((T, R)), whole((W2, R))],
        [whole((2, W2, R)), whole((3, W2, R))],
        [sds((2, W2, R), F32), sds((3, W2, R), BF16)],
        2 * T * D * R,
        2 << 20,
        "grad_u",
    )(info, mask, x, bc, v_send)


def grad_u_halves_body(info, mask, keep, got, v_keep, mine, other, grad_v):
    y = info[YLO]
    mine[...] = keep[y] + got[y].astype(F32)
    other[...] = (keep[1 - y] + got[1 - y].astype(F32)).astype(BF16)
    for k in range(W2 // R):
        at = slice(k * R, (k + 1) * R)
        grad_v[:, at] = (v_keep[:, at] + got[2, at].astype(F32)).astype(BF16)


def grad_u_halves(info, mask, keep, got, v_keep):
    return call(
        grad_u_halves_body,
        [whole((2, W2, R)), whole((3, W2, R)), whole((R, W2))],
        [whole((W2, R)), whole((W2, R)), whole((R, W2))],
        [sds((W2, R), F32), sds((W2, R), BF16), sds((R, W2), BF16)],
        0,
        1 << 20,
        "grad_u_halves",
        1,
    )(info, mask, keep, got, v_keep)


def last_body(info, mask, back, sx, sz, t7, bc, u, keep, near, got, before, out, grad_w):
    total = back[...] + nt(bc[...], u[...])
    for t in (sx, sz, t7):
        total += t[...].astype(F32)
    out[...] = total.astype(BF16)
    grad_w[...] = (keep[0] + near[0].astype(F32) + got[...].astype(F32)).astype(BF16)


def last(info, mask, back, terms, bc, low_u, keep, near, got, grad_w):
    half = pl.BlockSpec((1, 1, NB, 64, B), lambda i, info, mask: (info[YLO], i, 0, 0, 0))
    part = (1, NB, 64, B)
    return call(
        last_body,
        [col()] * 4
        + [whole((T, R)), pl.BlockSpec((W2, R), lambda i, info, mask: (i, 0)), half, half]
        + [pl.BlockSpec(part, lambda i, info, mask: (i, 0, 0, 0)), pl.BlockSpec(memory_space=pl.ANY)],
        [col(), pl.BlockSpec(part, lambda i, info, mask: (info[3 + i], 0, 0, 0))],
        [sds((T, D), BF16), sds((9, NB, 64, B), BF16)],
        2 * T * D * R,
        12 << 20,
        "last",
        aliases={11: 1},
    )(info, mask, back, *terms, bc, low_u, keep, near, got, grad_w)


def assemble_body(info, mask, keep, got, out):
    out[...] = (keep[...] + got[...].astype(F32)).astype(BF16)


def assemble(info, mask, keep, got):
    shape = (1, NB, 64, B)

    def place(k, info, mask):
        at = jnp.where(k == 4, info[7], info[jnp.clip(k - 1, 0, 2)])
        return (jnp.where(k == 0, 0, at), 0, 0, 0)

    return call(
        assemble_body,
        [pl.BlockSpec(shape, lambda k, info, mask: (k, 0, 0, 0))] * 2,
        pl.BlockSpec(shape, place),
        sds((9, NB, 64, B), BF16),
        0,
        6 << 20,
        "assemble",
        5,
    )(info, mask, keep, got)


def swap(value, axis, offset):
    sizes = 1
    for name in axis if isinstance(axis, tuple) else (axis,):
        sizes *= lax.axis_size(name)
    return lax.ppermute(value, axis, [(i, i ^ offset) for i in range(sizes)])


def sum_feat(value, offsets):
    for offset in offsets:
        value = value + swap(value, "feat", offset)
    return value


def beside(order, part, *args):
    shapes = jax.eval_shape(part, *args)

    def nothing(*args):
        return jax.tree.map(lambda s: jnp.zeros(s.shape, s.dtype), shapes)

    return lax.cond(order[0] >= 0, part, nothing, *args)


def pick(arr, index, axis=0):
    return lax.dynamic_index_in_dim(arr, index, axis, keepdims=False)


def per_device(x, weights, order, mask, low_u, low_v, cot):
    dp = lax.axis_index("dp").astype(jnp.int32)
    ylo, core = dp // 2, dp % 2
    both = ("feat", "dp")
    levels = jnp.arange(8, dtype=jnp.int32)
    slots = 1 + jnp.sum(jnp.where(order[None, :] == levels[:, None], levels[None, :], 0), 1)
    info = jnp.concatenate([slots, jnp.stack([ylo, core, dp])]).astype(jnp.int32)

    cpart, xs = prolog(info, mask, x, low_u)
    p3, p5, p7 = swap(x, "feat", 1), swap(x, "feat", 4), swap(x, "feat", 16)
    c = sum_feat(cpart, (3, 12))
    c, p3, p5, xs = lax.optimization_barrier((c, p3, p5, xs))
    p4, p6 = swap(p3, "feat", 3), swap(p5, "feat", 12)
    xn = swap(xs, "dp", 2)
    hn = swap(xs, both, 66)
    coeff = sum_feat(c, (1, 4, 16)).astype(BF16)
    mixed = near_mix(info, mask, x, p3, p5, p7, weights)
    coeff, xn, hn, mixed = lax.optimization_barrier((coeff, xn, hn, mixed))
    out, delta, t3, t4, t5, t6, bpart = middle(
        info, mask, mixed, p4, p6, weights, coeff, low_v, cot
    )

    dn = swap(delta, "dp", 2)
    r4, r6 = swap(t4, "feat", 3), swap(t6, "feat", 12)

    far_keep, far_send = far_grads(info, mask, (p3, p4, p5, p6), delta)
    b = sum_feat(bpart, (16,))

    def beside_first(keep, send, delta, b, weights):
        got = swap(send, "dp", 1)
        back = local_back(info, mask, delta, weights)
        b, back, got = lax.optimization_barrier((sum_feat(b, (1,)), back, got))
        away = pick(keep, 1 - ylo) + pick(got, 1 - ylo).astype(F32)
        return sum_feat(b, (4,)), back, got, away.astype(BF16)

    b, back, far_near, far_send = beside(
        order, beside_first, far_keep, far_send, delta, b, weights
    )
    r4, r6, dn, b, far_send = lax.optimization_barrier((r4, r6, dn, b, far_send))

    sx, sz, hi = second(info, mask, t3, r4, t5, r6, dn, weights)
    b = sum_feat(b, (3,))
    sx, sz, hi, b, far_send = lax.optimization_barrier((sx, sz, hi, b, far_send))
    sx, sz, t7 = swap(sx, "feat", 1), swap(sz, "feat", 4), swap(hi, both, 66)
    far_got = swap(far_send, "dp", 2)

    def beside_second(b, x, p7, xn, hn, delta, dn):
        b, dn = lax.optimization_barrier((b, dn))
        bc = sum_feat(b, (12,)).astype(BF16)
        keep, send, v_keep, v_send = near_grads(info, mask, x, p7, xn, hn, delta, dn)
        bc, send, v_send = lax.optimization_barrier((bc, send, v_send))
        got = swap(send, "dp", 1)
        gu_keep, gu_send = grad_u_parts(info, mask, x, bc, v_send)
        gu_send, got = lax.optimization_barrier((gu_send, got))
        gu_got = swap(gu_send, "dp", 1)
        gu_keep, gu_send, grad_v = grad_u_halves(info, mask, gu_keep, gu_got, v_keep)
        gu_send, got = lax.optimization_barrier((gu_send, got))
        grad_u = (gu_keep + swap(gu_send, "dp", 2).astype(F32)).astype(BF16)
        return bc, assemble(info, mask, keep, got), grad_u, grad_v

    bc, grad_w, grad_u, grad_v = beside(order, beside_second, b, x, p7, xn, hn, delta, dn)
    grad_x, grad_w = last(
        info, mask, back, [sx, sz, t7], bc, low_u, far_keep, far_near, far_got, grad_w
    )
    return out, grad_x, grad_w, grad_u, grad_v


def solution(mesh):
    return jax.shard_map(
        per_device,
        mesh=mesh,
        in_specs=(
            P("dp", "feat"),
            P(None, "feat", None, None),
            P(),
            P(None, "feat"),
            P("feat", None),
            P(None, "feat"),
            P("dp", "feat"),
        ),
        out_specs=(
            P("dp", "feat"),
            P("dp", "feat"),
            P(None, "feat", "dp", None),
            P(("feat", "dp"), None),
            P(None, ("feat", "dp")),
        ),
        check_vma=False,
    )
```

```python
import jax
import jax.numpy as jnp
from jax import lax
from jax.experimental import pallas as pl
from jax.experimental.pallas import tpu as pltpu
from jax.sharding import PartitionSpec as P

F32 = jnp.float32
BF16 = jnp.bfloat16
T = 256
D = 2048
B = 256
R = 128
NB = 8
STEPS = 4
W2 = 2 * B
MID, FAR, SEC = 4, 4, 4
YLO, CORE, DP = 8, 9, 10
LIMIT, LESS = 60 << 20, 52 << 20


def nn(a, b):
    return jnp.dot(a, b, preferred_element_type=F32)


def nt(a, b):
    return lax.dot_general(a, b, (((1,), (1,)), ((), ())), preferred_element_type=F32)


def tn(a, b):
    return lax.dot_general(a, b, (((0,), (0,)), ((), ())), preferred_element_type=F32)


def gelu_parts(value):
    cdf = 0.5 * (1.0 + lax.erf(value * 0.7071067811865476))
    slope = cdf + value * jnp.exp(-0.5 * value * value) * 0.3989422804014327
    return (value * cdf, slope)


def gate(info, mask, bit, block):
    return mask[info[bit] - 1, block].astype(F32)


def call(body, in_specs, out_specs, out_shape, flops, data, name, grid=STEPS, aliases=None, limit=LIMIT):
    return pl.pallas_call(
        body,
        grid_spec=pltpu.PrefetchScalarGridSpec(
            num_scalar_prefetch=2, grid=(grid,), in_specs=in_specs, out_specs=out_specs
        ),
        out_shape=out_shape,
        input_output_aliases=aliases or {},
        compiler_params=pltpu.CompilerParams(
            dimension_semantics=("arbitrary",), vmem_limit_bytes=limit
        ),
        cost_estimate=pl.CostEstimate(flops=flops, bytes_accessed=data, transcendentals=0),
        name=name,
    )


def sds(shape, dtype):
    return jax.ShapeDtypeStruct(shape, dtype)


def col(width=W2, at=lambda i, info: i):
    return pl.BlockSpec((T, width), lambda i, info, mask: (0, at(i, info)))


def whole(shape):
    return pl.BlockSpec(shape, lambda i, info, mask: (0,) * len(shape))


def weight(bit, blocks=2):
    if bit is None:
        return pl.BlockSpec((1, blocks, B, B), lambda i, info, mask: (0, i, 0, 0))
    return pl.BlockSpec((1, blocks, B, B), lambda i, info, mask: (info[bit], i, 0, 0))


def blk(ref, j):
    return ref[:, j * B : (j + 1) * B]


OWN = [col(), col(at=lambda i, info: i ^ 1), col(at=lambda i, info: i ^ 2)]


def prolog_body(info, mask, x, u, cpart, xs):
    @pl.when(pl.program_id(0) == 0)
    def _():
        cpart[...] = jnp.zeros_like(cpart)

    cpart[...] += nn(x[...], u[...])
    for j in range(2):
        b = blk(x, j)
        xs[:, j * 128 : (j + 1) * 128] = jnp.where(info[YLO] == 0, b[:, 128:], b[:, :128])


def prolog(info, mask, x, low_u):
    return call(
        prolog_body,
        [col(), pl.BlockSpec((W2, R), lambda i, info, mask: (i, 0))],
        [whole((T, R)), col(B)],
        [sds((T, R), F32), sds((T, D // 2), BF16)],
        2 * T * D * R,
        3 << 20,
        "prolog",
    )(info, mask, x, low_u)


def near_mix_body(info, mask, xa, xb, xc, p3, p5, p7, w, w0, w1, w2, w3, w5, w7, mixed):
    i = pl.program_id(0)
    for j in range(2):
        total = nn(blk(xa, j), w[0, j])
        for x, k, v, bit in (
            (xa, 1 - j, w0, 0),
            (xb, j, w1, 1),
            (xc, j, w2, 2),
            (p3, j, w3, 3),
            (p5, j, w5, 5),
            (p7, j, w7, 7),
        ):
            total += nn(blk(x, k), v[0, j]) * gate(info, mask, bit, 2 * i + j)
        mixed[:, j * B : (j + 1) * B] = total


def near_mix(info, mask, x, p3, p5, p7, weights):
    return call(
        near_mix_body,
        OWN + [col()] * 3 + [weight(b) for b in (None, 0, 1, 2, 3, 5, 7)],
        col(),
        sds((T, D), F32),
        14 * T * D * B,
        14 << 20,
        "near_mix",
    )(info, mask, x, x, x, p3, p5, p7, *([weights] * 7))


def middle_body(info, mask, mixed, p4, p6, w3, w4, w5, w6, *refs):
    coeff, low_v, cot, out, delta, t3, t4, t5, t6, bpart = refs
    i = pl.program_id(0)

    @pl.when(i == 0)
    def _():
        bpart[...] = jnp.zeros_like(bpart)
        delta[:, D:] = coeff[...]

    for j in range(MID):
        cols = slice(j * B, (j + 1) * B)
        pre = mixed[:, cols] + nn(coeff[...], low_v[:, cols])
        pre += nn(p4[:, cols], w4[0, j]) * gate(info, mask, 4, MID * i + j)
        pre += nn(p6[:, cols], w6[0, j]) * gate(info, mask, 6, MID * i + j)
        act, slope = gelu_parts(pre)
        out[:, cols] = act.astype(BF16)
        d = (cot[:, cols].astype(F32) * slope).astype(BF16)
        delta[:, pl.ds(pl.multiple_of((MID * i + j) * B, B), B)] = d
        bpart[...] += nt(d, low_v[:, cols])
        for bit, t, w in ((4, t4, w4), (6, t6, w6), (3, t3, w3), (5, t5, w5)):
            t[:, cols] = (nt(d, w[0, j]) * gate(info, mask, bit, MID * i + j)).astype(BF16)


def middle(info, mask, mixed, p4, p6, weights, coeff, low_v, cot):
    return call(
        middle_body,
        [col(MID * B)] * 3
        + [weight(b, MID) for b in range(3, 7)]
        + [whole((T, R)), pl.BlockSpec((R, MID * B), lambda i, info, mask: (0, i)), col(MID * B)],
        [col(MID * B), whole((T, D + R))] + [col(MID * B)] * 4 + [whole((T, R))],
        [sds((T, D), BF16), sds((T, D + R), BF16)]
        + [sds((T, D), BF16)] * 4
        + [sds((T, R), F32)],
        12 * T * D * B,
        18 << 20,
        "middle",
        NB // MID,
    )(info, mask, mixed, p4, p6, *([weights] * 4), coeff, low_v, cot)


def far_grads_body(info, mask, p3, p4, p5, p6, delta, keep, send):
    i = pl.program_id(0)
    first = info[CORE] == 0
    for j in range(FAR):
        d = blk(delta, j)
        for k, p in enumerate((p3, p4, p5, p6)):
            g = tn(blk(p, j), d) * gate(info, mask, 3 + k, FAR * i + j)
            for half in range(2):
                lo, hi = g[128 * half : 128 * half + 64], g[128 * half + 64 : 128 * half + 128]
                keep[half, k, j] = jnp.where(first, lo, hi)
                send[half, k, j] = jnp.where(first, hi, lo).astype(BF16)


def far_grads(info, mask, partners, delta):
    spec = pl.BlockSpec((2, 4, FAR, 64, B), lambda i, info, mask: (0, 0, i, 0, 0))
    return call(
        far_grads_body,
        [col(FAR * B)] * 5,
        [spec, spec],
        [sds((2, 4, NB, 64, B), F32), sds((2, 4, NB, 64, B), BF16)],
        8 * T * D * B,
        12 << 20,
        "far_grads",
        NB // FAR,
    )(info, mask, *partners, delta)


def second_body(info, mask, t3, r4, t5, r6, dn, w, sx, sz, hi):
    sx[...] = t3[...] + r4[...]
    sz[...] = t5[...] + r6[...]
    for j in range(SEC):
        g = gate(info, mask, 7, SEC * pl.program_id(0) + j)
        hi[:, j * B : (j + 1) * B] = (nt(blk(dn, j), w[0, j]) * g).astype(BF16)


def second(info, mask, t3, r4, t5, r6, dn, weights):
    return call(
        second_body,
        [col(SEC * B)] * 5 + [weight(7, SEC)],
        [col(SEC * B)] * 3,
        [sds((T, D), BF16)] * 3,
        2 * T * D * B,
        9 << 20,
        "second",
        NB // SEC,
    )(info, mask, t3, r4, t5, r6, dn, weights)


def local_back_body(info, mask, delta, w, w0, w1, w2, back):
    i = pl.program_id(0)

    @pl.when(i == 0)
    def _():
        back[...] = jnp.zeros_like(back)

    def place(step, j):
        return pl.ds(pl.multiple_of(step * W2 + j * B, B), B)

    for j in range(2):
        d, e = blk(delta, j), blk(delta, 1 - j)
        back[:, place(i, j)] += (
            nt(d, w[0, j]) + nt(e, w0[0, 1 - j]) * gate(info, mask, 0, 2 * i + 1 - j)
        )
        back[:, place(i ^ 1, j)] += nt(d, w1[0, j]) * gate(info, mask, 1, 2 * i + j)
        back[:, place(i ^ 2, j)] += nt(d, w2[0, j]) * gate(info, mask, 2, 2 * i + j)


def local_back(info, mask, delta, weights):
    return call(
        local_back_body,
        [col()] + [weight(b) for b in (None, 0, 1, 2)],
        whole((T, D)),
        sds((T, D), F32),
        8 * T * D * B,
        8 << 20,
        "local_back",
    )(info, mask, delta, *([weights] * 4))


def near_grads_body(info, mask, xa, xb, xc, p7, na, nb, nc, n7, delta, dn, co, cn, *outs):
    keep, send, vkeep, vsend = outs
    i = pl.program_id(0)
    first = info[CORE] == 0

    def half(ref, j):
        return ref[:, pl.ds(pl.multiple_of(j * B + info[YLO] * 128, 128), 128)]

    def part(ref, j):
        return ref[:, j * 128 : (j + 1) * 128]

    for j in range(2):
        own = [half(xa, j), half(xa, 1 - j), half(xb, j), half(xc, j), half(p7, j)]
        got = [part(na, j), part(na, 1 - j), part(nb, j), part(nc, j), part(n7, j)]
        g = tn(jnp.concatenate(own, 1), blk(delta, j)) + tn(jnp.concatenate(got, 1), blk(dn, j))
        for k, bit in enumerate((None, 0, 1, 2, 7)):
            h = g[128 * k : 128 * (k + 1)]
            if bit is not None:
                h = h * gate(info, mask, bit, 2 * i + j)
            keep[k, j] = jnp.where(first, h[:64], h[64:])
            send[k, j] = jnp.where(first, h[64:], h[:64]).astype(BF16)

    @pl.when(i // 2 == info[YLO])
    def _():
        v = tn(co[...], delta[...]) + tn(cn[...], dn[...])

        @pl.when(i == info[DP])
        def _():
            vkeep[...] = v

        @pl.when(i != info[DP])
        def _():
            for k in range(W2 // R):
                vsend[k * R : (k + 1) * R] = v[:, k * R : (k + 1) * R].astype(BF16)


def near_grads(info, mask, x, p7, xn, hn, delta, dn):
    got = [col(B), col(B, lambda i, info: i ^ 1), col(B, lambda i, info: i ^ 2), col(B)]
    spec = pl.BlockSpec((5, 2, 64, B), lambda i, info, mask: (0, i, 0, 0))
    last = col(R, lambda i, info: D // R)
    return call(
        near_grads_body,
        OWN + [col()] + got + [col(), col(), last, last],
        [spec, spec, whole((R, W2)), whole((W2, R))],
        [
            sds((5, NB, 64, B), F32),
            sds((5, NB, 64, B), BF16),
            sds((R, W2), F32),
            sds((W2, R), BF16),
        ],
        10 * T * D * B,
        12 << 20,
        "near_grads",
        limit=LESS,
    )(info, mask, x, x, x, p7, xn, xn, xn, hn, delta, dn, delta, dn)


def grad_u_body(info, mask, x, bc, v, keep, send):
    i = pl.program_id(0)
    g = tn(x[...], bc[...])

    @pl.when(i % 2 == info[CORE])
    def _():
        keep[i // 2] = g

    @pl.when(i % 2 != info[CORE])
    def _():
        send[i // 2] = g.astype(BF16)

    @pl.when(i == 0)
    def _():
        send[2] = v[...]


def grad_u_parts(info, mask, x, bc, v_send):
    return call(
        grad_u_body,
        [col(), whole((T, R)), whole((W2, R))],
        [whole((2, W2, R)), whole((3, W2, R))],
        [sds((2, W2, R), F32), sds((3, W2, R), BF16)],
        2 * T * D * R,
        2 << 20,
        "grad_u",
        limit=LESS,
    )(info, mask, x, bc, v_send)


def grad_u_halves_body(info, mask, keep, got, v_keep, mine, other, grad_v):
    y = info[YLO]
    mine[...] = keep[y] + got[y].astype(F32)
    other[...] = (keep[1 - y] + got[1 - y].astype(F32)).astype(BF16)
    for k in range(W2 // R):
        at = slice(k * R, (k + 1) * R)
        grad_v[:, at] = (v_keep[:, at] + got[2, at].astype(F32)).astype(BF16)


def grad_u_halves(info, mask, keep, got, v_keep):
    return call(
        grad_u_halves_body,
        [whole((2, W2, R)), whole((3, W2, R)), whole((R, W2))],
        [whole((W2, R)), whole((W2, R)), whole((R, W2))],
        [sds((W2, R), F32), sds((W2, R), BF16), sds((R, W2), BF16)],
        0,
        1 << 20,
        "grad_u_halves",
        1,
        limit=LESS,
    )(info, mask, keep, got, v_keep)


def last_body(info, mask, back, sx, sz, t7, bc, u, keep, near, got, before, out, grad_w):
    total = back[...] + nt(bc[...], u[...])
    for t in (sx, sz, t7):
        total += t[...].astype(F32)
    out[...] = total.astype(BF16)
    grad_w[...] = (keep[0] + near[0].astype(F32) + got[...].astype(F32)).astype(BF16)


def last(info, mask, back, terms, bc, low_u, keep, near, got, grad_w):
    half = pl.BlockSpec((1, 1, NB, 64, B), lambda i, info, mask: (info[YLO], i, 0, 0, 0))
    part = (1, NB, 64, B)
    return call(
        last_body,
        [col()] * 4
        + [whole((T, R)), pl.BlockSpec((W2, R), lambda i, info, mask: (i, 0)), half, half]
        + [pl.BlockSpec(part, lambda i, info, mask: (i, 0, 0, 0)), pl.BlockSpec(memory_space=pl.ANY)],
        [col(), pl.BlockSpec(part, lambda i, info, mask: (info[3 + i], 0, 0, 0))],
        [sds((T, D), BF16), sds((9, NB, 64, B), BF16)],
        2 * T * D * R,
        12 << 20,
        "last",
        aliases={11: 1},
    )(info, mask, back, *terms, bc, low_u, keep, near, got, grad_w)


def assemble_body(info, mask, keep, got, out):
    out[...] = (keep[...] + got[...].astype(F32)).astype(BF16)


def assemble(info, mask, keep, got):
    shape = (1, NB, 64, B)

    def place(k, info, mask):
        at = jnp.where(k == 4, info[7], info[jnp.clip(k - 1, 0, 2)])
        return (jnp.where(k == 0, 0, at), 0, 0, 0)

    return call(
        assemble_body,
        [pl.BlockSpec(shape, lambda k, info, mask: (k, 0, 0, 0))] * 2,
        pl.BlockSpec(shape, place),
        sds((9, NB, 64, B), BF16),
        0,
        6 << 20,
        "assemble",
        5,
        limit=LESS,
    )(info, mask, keep, got)


def swap(value, axis, offset):
    sizes = 1
    for name in axis if isinstance(axis, tuple) else (axis,):
        sizes *= lax.axis_size(name)
    return lax.ppermute(value, axis, [(i, i ^ offset) for i in range(sizes)])


def sum_feat(value, offsets):
    for offset in offsets:
        value = value + swap(value, "feat", offset)
    return value


def beside(order, part, *args):
    shapes = jax.eval_shape(part, *args)

    def nothing(*args):
        return jax.tree.map(lambda s: jnp.zeros(s.shape, s.dtype), shapes)

    return lax.cond(order[0] >= 0, part, nothing, *args)


def pick(arr, index, axis=0):
    return lax.dynamic_index_in_dim(arr, index, axis, keepdims=False)


def per_device(x, weights, order, mask, low_u, low_v, cot):
    dp = lax.axis_index("dp").astype(jnp.int32)
    ylo, core = dp // 2, dp % 2
    both = ("feat", "dp")
    levels = jnp.arange(8, dtype=jnp.int32)
    slots = 1 + jnp.sum(jnp.where(order[None, :] == levels[:, None], levels[None, :], 0), 1)
    info = jnp.concatenate([slots, jnp.stack([ylo, core, dp])]).astype(jnp.int32)

    cpart, xs = prolog(info, mask, x, low_u)
    p3, p5, p7 = swap(x, "feat", 1), swap(x, "feat", 4), swap(x, "feat", 16)
    c = sum_feat(cpart, (3, 12))
    c, p3, p5, xs = lax.optimization_barrier((c, p3, p5, xs))
    p4, p6 = swap(p3, "feat", 3), swap(p5, "feat", 12)
    xn = swap(xs, "dp", 2)
    coeff = sum_feat(c, (1, 4, 16)).astype(BF16)
    mixed = near_mix(info, mask, x, p3, p5, p7, weights)
    coeff, xn, mixed = lax.optimization_barrier((coeff, xn, mixed))
    out, delta, t3, t4, t5, t6, bpart = middle(
        info, mask, mixed, p4, p6, weights, coeff, low_v, cot
    )

    dn = swap(delta, "dp", 2)
    r4, r6 = swap(t4, "feat", 3), swap(t6, "feat", 12)

    hn = swap(xs, both, 66)
    far_keep, far_send = far_grads(info, mask, (p3, p4, p5, p6), delta)
    b = sum_feat(bpart, (1,))

    def beside_first(keep, send, delta, b, weights):
        got = swap(send, "dp", 1)
        back = local_back(info, mask, delta, weights)
        b, back, got = lax.optimization_barrier((b, back, got))
        away = pick(keep, 1 - ylo) + pick(got, 1 - ylo).astype(F32)
        return sum_feat(b, (4,)), back, got, away.astype(BF16)

    b, back, far_near, far_send = beside(
        order, beside_first, far_keep, far_send, delta, b, weights
    )
    r4, r6, dn, hn, b, far_send = lax.optimization_barrier((r4, r6, dn, hn, b, far_send))

    sx, sz, hi = second(info, mask, t3, r4, t5, r6, dn, weights)
    b = sum_feat(b, (16,))
    sx, sz, hi, b, far_send = lax.optimization_barrier((sx, sz, hi, b, far_send))
    sx, sz, t7 = swap(sx, "feat", 1), swap(sz, "feat", 4), swap(hi, both, 66)
    far_got = swap(far_send, "dp", 2)

    def beside_second(b, x, p7, xn, hn, delta, dn):
        b, dn = lax.optimization_barrier((b, dn))
        b = sum_feat(b, (3,))
        keep, send, v_keep, v_send = near_grads(info, mask, x, p7, xn, hn, delta, dn)
        b, send, v_send = lax.optimization_barrier((b, send, v_send))
        bc = sum_feat(b, (12,)).astype(BF16)
        bc, send, v_send = lax.optimization_barrier((bc, send, v_send))
        got = swap(send, "dp", 1)
        gu_keep, gu_send = grad_u_parts(info, mask, x, bc, v_send)
        gu_send, got = lax.optimization_barrier((gu_send, got))
        gu_got = swap(gu_send, "dp", 1)
        grad_w = assemble(info, mask, keep, got)
        return bc, grad_w, *grad_u_halves(info, mask, gu_keep, gu_got, v_keep)

    bc, grad_w, gu_keep, gu_send, grad_v = beside(order, beside_second, b, x, p7, xn, hn, delta, dn)
    gu_send, sx, sz, t7, far_got = lax.optimization_barrier((gu_send, sx, sz, t7, far_got))
    grad_u = (gu_keep + swap(gu_send, "dp", 2).astype(F32)).astype(BF16)
    grad_x, grad_w = last(
        info, mask, back, [sx, sz, t7], bc, low_u, far_keep, far_near, far_got, grad_w
    )
    return out, grad_x, grad_w, grad_u, grad_v


def solution(mesh):
    return jax.shard_map(
        per_device,
        mesh=mesh,
        in_specs=(
            P("dp", "feat"),
            P(None, "feat", None, None),
            P(),
            P(None, "feat"),
            P("feat", None),
            P(None, "feat"),
            P("dp", "feat"),
        ),
        out_specs=(
            P("dp", "feat"),
            P("dp", "feat"),
            P(None, "feat", "dp", None),
            P(("feat", "dp"), None),
            P(None, ("feat", "dp")),
        ),
        check_vma=False,
    )
```

```python
import jax
import jax.numpy as jnp
from jax import lax
from jax.experimental import pallas as pl
from jax.experimental.pallas import tpu as pltpu
from jax.sharding import PartitionSpec as P

F32 = jnp.float32
BF16 = jnp.bfloat16
T = 256
D = 2048
B = 256
R = 128
NB = 8
STEPS = 4
W2 = 2 * B
MID, FAR, SEC = 4, 4, 4
YLO, CORE, DP = 8, 9, 10
LIMIT, LESS = 60 << 20, 52 << 20


def nn(a, b):
    return jnp.dot(a, b, preferred_element_type=F32)


def nt(a, b):
    return lax.dot_general(a, b, (((1,), (1,)), ((), ())), preferred_element_type=F32)


def tn(a, b):
    return lax.dot_general(a, b, (((0,), (0,)), ((), ())), preferred_element_type=F32)


def gelu_parts(value):
    cdf = 0.5 * (1.0 + lax.erf(value * 0.7071067811865476))
    slope = cdf + value * jnp.exp(-0.5 * value * value) * 0.3989422804014327
    return (value * cdf, slope)


def gate(info, mask, bit, block):
    return mask[info[bit] - 1, block].astype(F32)


def call(body, in_specs, out_specs, out_shape, flops, data, name, grid=STEPS, aliases=None, limit=LIMIT):
    return pl.pallas_call(
        body,
        grid_spec=pltpu.PrefetchScalarGridSpec(
            num_scalar_prefetch=2, grid=(grid,), in_specs=in_specs, out_specs=out_specs
        ),
        out_shape=out_shape,
        input_output_aliases=aliases or {},
        compiler_params=pltpu.CompilerParams(
            dimension_semantics=("arbitrary",), vmem_limit_bytes=limit
        ),
        cost_estimate=pl.CostEstimate(flops=flops, bytes_accessed=data, transcendentals=0),
        name=name,
    )


def sds(shape, dtype):
    return jax.ShapeDtypeStruct(shape, dtype)


def col(width=W2, at=lambda i, info: i):
    return pl.BlockSpec((T, width), lambda i, info, mask: (0, at(i, info)))


def whole(shape):
    return pl.BlockSpec(shape, lambda i, info, mask: (0,) * len(shape))


def weight(bit, blocks=2):
    if bit is None:
        return pl.BlockSpec((1, blocks, B, B), lambda i, info, mask: (0, i, 0, 0))
    return pl.BlockSpec((1, blocks, B, B), lambda i, info, mask: (info[bit], i, 0, 0))


def blk(ref, j):
    return ref[:, j * B : (j + 1) * B]


OWN = [col(), col(at=lambda i, info: i ^ 1), col(at=lambda i, info: i ^ 2)]


def slices_body(info, mask, x, xs):
    for j in range(NB):
        b = blk(x, j)
        xs[:, j * 128 : (j + 1) * 128] = jnp.where(info[YLO] == 0, b[:, 128:], b[:, :128])


def slices(info, mask, x):
    return call(
        slices_body,
        [whole((T, D))],
        whole((T, D // 2)),
        sds((T, D // 2), BF16),
        0,
        2 << 20,
        "slices",
        1,
    )(info, mask, x)


def near_mix_body(info, mask, xa, xb, xc, p3, p5, p7, w, w0, w1, w2, w3, w5, w7, mixed):
    i = pl.program_id(0)
    for j in range(2):
        total = nn(blk(xa, j), w[0, j])
        for x, k, v, bit in (
            (xa, 1 - j, w0, 0),
            (xb, j, w1, 1),
            (xc, j, w2, 2),
            (p3, j, w3, 3),
            (p5, j, w5, 5),
            (p7, j, w7, 7),
        ):
            total += nn(blk(x, k), v[0, j]) * gate(info, mask, bit, 2 * i + j)
        mixed[:, j * B : (j + 1) * B] = total


def near_mix(info, mask, x, p3, p5, p7, weights):
    return call(
        near_mix_body,
        OWN + [col()] * 3 + [weight(b) for b in (None, 0, 1, 2, 3, 5, 7)],
        col(),
        sds((T, D), F32),
        14 * T * D * B,
        14 << 20,
        "near_mix",
    )(info, mask, x, x, x, p3, p5, p7, *([weights] * 7))


def middle_body(info, mask, mixed, p4, p6, w3, w4, w5, w6, *refs):
    coeff, low_v, cot, out, delta, t3, t4, t5, t6, bpart = refs
    i = pl.program_id(0)

    @pl.when(i == 0)
    def _():
        bpart[...] = jnp.zeros_like(bpart)
        delta[:, D:] = coeff[...]

    for j in range(MID):
        cols = slice(j * B, (j + 1) * B)
        pre = mixed[:, cols] + nn(coeff[...], low_v[:, cols])
        pre += nn(p4[:, cols], w4[0, j]) * gate(info, mask, 4, MID * i + j)
        pre += nn(p6[:, cols], w6[0, j]) * gate(info, mask, 6, MID * i + j)
        act, slope = gelu_parts(pre)
        out[:, cols] = act.astype(BF16)
        d = (cot[:, cols].astype(F32) * slope).astype(BF16)
        delta[:, pl.ds(pl.multiple_of((MID * i + j) * B, B), B)] = d
        bpart[...] += nt(d, low_v[:, cols])
        for bit, t, w in ((4, t4, w4), (6, t6, w6), (3, t3, w3), (5, t5, w5)):
            t[:, cols] = (nt(d, w[0, j]) * gate(info, mask, bit, MID * i + j)).astype(BF16)


def middle(info, mask, mixed, p4, p6, weights, coeff, low_v, cot):
    return call(
        middle_body,
        [col(MID * B)] * 3
        + [weight(b, MID) for b in range(3, 7)]
        + [whole((T, R)), pl.BlockSpec((R, MID * B), lambda i, info, mask: (0, i)), col(MID * B)],
        [col(MID * B), whole((T, D + R))] + [col(MID * B)] * 4 + [whole((T, R))],
        [sds((T, D), BF16), sds((T, D + R), BF16)]
        + [sds((T, D), BF16)] * 4
        + [sds((T, R), F32)],
        12 * T * D * B,
        18 << 20,
        "middle",
        NB // MID,
    )(info, mask, mixed, p4, p6, *([weights] * 4), coeff, low_v, cot)


def far_grads_body(info, mask, p3, p4, p5, p6, delta, keep, send):
    i = pl.program_id(0)
    first = info[CORE] == 0
    for j in range(FAR):
        d = blk(delta, j)
        for k, p in enumerate((p3, p4, p5, p6)):
            g = tn(blk(p, j), d) * gate(info, mask, 3 + k, FAR * i + j)
            for half in range(2):
                lo, hi = g[128 * half : 128 * half + 64], g[128 * half + 64 : 128 * half + 128]
                keep[half, k, j] = jnp.where(first, lo, hi)
                send[half, k, j] = jnp.where(first, hi, lo).astype(BF16)


def far_grads(info, mask, partners, delta):
    spec = pl.BlockSpec((2, 4, FAR, 64, B), lambda i, info, mask: (0, 0, i, 0, 0))
    return call(
        far_grads_body,
        [col(FAR * B)] * 5,
        [spec, spec],
        [sds((2, 4, NB, 64, B), F32), sds((2, 4, NB, 64, B), BF16)],
        8 * T * D * B,
        12 << 20,
        "far_grads",
        NB // FAR,
    )(info, mask, *partners, delta)


def hi_term_body(info, mask, dn, w, hi):
    for j in range(SEC):
        g = gate(info, mask, 7, SEC * pl.program_id(0) + j)
        hi[:, j * B : (j + 1) * B] = (nt(blk(dn, j), w[0, j]) * g).astype(BF16)


def hi_term(info, mask, dn, weights):
    return call(
        hi_term_body,
        [col(SEC * B), weight(7, SEC)],
        col(SEC * B),
        sds((T, D), BF16),
        2 * T * D * B,
        3 << 20,
        "hi_term",
        NB // SEC,
    )(info, mask, dn, weights)


def merge_body(info, mask, t3, r4, t5, r6, sx, sz):
    sx[...] = t3[...] + r4[...]
    sz[...] = t5[...] + r6[...]


def merge(info, mask, t3, r4, t5, r6):
    return call(
        merge_body,
        [col(SEC * B)] * 4,
        [col(SEC * B)] * 2,
        [sds((T, D), BF16)] * 2,
        2 * T * D,
        6 << 20,
        "merge",
        NB // SEC,
    )(info, mask, t3, r4, t5, r6)


def local_back_body(info, mask, delta, w, w0, w1, w2, back):
    i = pl.program_id(0)

    @pl.when(i == 0)
    def _():
        back[...] = jnp.zeros_like(back)

    def place(step, j):
        return pl.ds(pl.multiple_of(step * W2 + j * B, B), B)

    for j in range(2):
        d, e = blk(delta, j), blk(delta, 1 - j)
        back[:, place(i, j)] += (
            nt(d, w[0, j]) + nt(e, w0[0, 1 - j]) * gate(info, mask, 0, 2 * i + 1 - j)
        )
        back[:, place(i ^ 1, j)] += nt(d, w1[0, j]) * gate(info, mask, 1, 2 * i + j)
        back[:, place(i ^ 2, j)] += nt(d, w2[0, j]) * gate(info, mask, 2, 2 * i + j)


def local_back(info, mask, delta, weights):
    return call(
        local_back_body,
        [col()] + [weight(b) for b in (None, 0, 1, 2)],
        whole((T, D)),
        sds((T, D), F32),
        8 * T * D * B,
        8 << 20,
        "local_back",
    )(info, mask, delta, *([weights] * 4))


def near_grads_body(info, mask, xa, xb, xc, p7, na, nb, nc, n7, delta, dn, co, cn, *outs):
    keep, send, vkeep, vsend = outs
    i = pl.program_id(0)
    first = info[CORE] == 0

    def half(ref, j):
        return ref[:, pl.ds(pl.multiple_of(j * B + info[YLO] * 128, 128), 128)]

    def part(ref, j):
        return ref[:, j * 128 : (j + 1) * 128]

    for j in range(2):
        own = [half(xa, j), half(xa, 1 - j), half(xb, j), half(xc, j), half(p7, j)]
        got = [part(na, j), part(na, 1 - j), part(nb, j), part(nc, j), part(n7, j)]
        g = tn(jnp.concatenate(own, 1), blk(delta, j)) + tn(jnp.concatenate(got, 1), blk(dn, j))
        for k, bit in enumerate((None, 0, 1, 2, 7)):
            h = g[128 * k : 128 * (k + 1)]
            if bit is not None:
                h = h * gate(info, mask, bit, 2 * i + j)
            keep[k, j] = jnp.where(first, h[:64], h[64:])
            send[k, j] = jnp.where(first, h[64:], h[:64]).astype(BF16)

    @pl.when(i // 2 == info[YLO])
    def _():
        v = tn(co[...], delta[...]) + tn(cn[...], dn[...])

        @pl.when(i == info[DP])
        def _():
            vkeep[...] = v

        @pl.when(i != info[DP])
        def _():
            for k in range(W2 // R):
                vsend[k * R : (k + 1) * R] = v[:, k * R : (k + 1) * R].astype(BF16)


def near_grads(info, mask, x, p7, xn, hn, delta, dn):
    got = [col(B), col(B, lambda i, info: i ^ 1), col(B, lambda i, info: i ^ 2), col(B)]
    spec = pl.BlockSpec((5, 2, 64, B), lambda i, info, mask: (0, i, 0, 0))
    last = col(R, lambda i, info: D // R)
    return call(
        near_grads_body,
        OWN + [col()] + got + [col(), col(), last, last],
        [spec, spec, whole((R, W2)), whole((W2, R))],
        [
            sds((5, NB, 64, B), F32),
            sds((5, NB, 64, B), BF16),
            sds((R, W2), F32),
            sds((W2, R), BF16),
        ],
        10 * T * D * B,
        12 << 20,
        "near_grads",
        limit=LESS,
    )(info, mask, x, x, x, p7, xn, xn, xn, hn, delta, dn, delta, dn)


def grad_u_body(info, mask, x, bc, v, keep, send):
    i = pl.program_id(0)
    g = tn(x[...], bc[...])

    @pl.when(i % 2 == info[CORE])
    def _():
        keep[i // 2] = g

    @pl.when(i % 2 != info[CORE])
    def _():
        send[i // 2] = g.astype(BF16)

    @pl.when(i == 0)
    def _():
        send[2] = v[...]


def grad_u_parts(info, mask, x, bc, v_send):
    return call(
        grad_u_body,
        [col(), whole((T, R)), whole((W2, R))],
        [whole((2, W2, R)), whole((3, W2, R))],
        [sds((2, W2, R), F32), sds((3, W2, R), BF16)],
        2 * T * D * R,
        2 << 20,
        "grad_u",
        limit=LESS,
    )(info, mask, x, bc, v_send)


def grad_u_halves_body(info, mask, keep, got, v_keep, mine, other, grad_v):
    y = info[YLO]
    mine[...] = keep[y] + got[y].astype(F32)
    other[...] = (keep[1 - y] + got[1 - y].astype(F32)).astype(BF16)
    for k in range(W2 // R):
        at = slice(k * R, (k + 1) * R)
        grad_v[:, at] = (v_keep[:, at] + got[2, at].astype(F32)).astype(BF16)


def grad_u_halves(info, mask, keep, got, v_keep):
    return call(
        grad_u_halves_body,
        [whole((2, W2, R)), whole((3, W2, R)), whole((R, W2))],
        [whole((W2, R)), whole((W2, R)), whole((R, W2))],
        [sds((W2, R), F32), sds((W2, R), BF16), sds((R, W2), BF16)],
        0,
        1 << 20,
        "grad_u_halves",
        1,
        limit=LESS,
    )(info, mask, keep, got, v_keep)


def last_body(info, mask, back, sx, sz, t7, bc, u, keep, near, got, before, out, grad_w):
    total = back[...] + nt(bc[...], u[...])
    for t in (sx, sz, t7):
        total += t[...].astype(F32)
    out[...] = total.astype(BF16)
    grad_w[...] = (keep[0] + near[0].astype(F32) + got[...].astype(F32)).astype(BF16)


def last(info, mask, back, terms, bc, low_u, keep, near, got, grad_w):
    half = pl.BlockSpec((1, 1, NB, 64, B), lambda i, info, mask: (info[YLO], i, 0, 0, 0))
    part = (1, NB, 64, B)
    return call(
        last_body,
        [col()] * 4
        + [whole((T, R)), pl.BlockSpec((W2, R), lambda i, info, mask: (i, 0)), half, half]
        + [pl.BlockSpec(part, lambda i, info, mask: (i, 0, 0, 0)), pl.BlockSpec(memory_space=pl.ANY)],
        [col(), pl.BlockSpec(part, lambda i, info, mask: (info[3 + i], 0, 0, 0))],
        [sds((T, D), BF16), sds((9, NB, 64, B), BF16)],
        2 * T * D * R,
        12 << 20,
        "last",
        aliases={11: 1},
    )(info, mask, back, *terms, bc, low_u, keep, near, got, grad_w)


def assemble_body(info, mask, keep, got, out):
    out[...] = (keep[...] + got[...].astype(F32)).astype(BF16)


def assemble(info, mask, keep, got):
    shape = (1, NB, 64, B)

    def place(k, info, mask):
        at = jnp.where(k == 4, info[7], info[jnp.clip(k - 1, 0, 2)])
        return (jnp.where(k == 0, 0, at), 0, 0, 0)

    return call(
        assemble_body,
        [pl.BlockSpec(shape, lambda k, info, mask: (k, 0, 0, 0))] * 2,
        pl.BlockSpec(shape, place),
        sds((9, NB, 64, B), BF16),
        0,
        6 << 20,
        "assemble",
        5,
        limit=LESS,
    )(info, mask, keep, got)


def swap(value, axis, offset):
    sizes = 1
    for name in axis if isinstance(axis, tuple) else (axis,):
        sizes *= lax.axis_size(name)
    return lax.ppermute(value, axis, [(i, i ^ offset) for i in range(sizes)])


def sum_feat(value, offsets):
    for offset in offsets:
        value = value + swap(value, "feat", offset)
    return value


def beside(order, part, *args):
    shapes = jax.eval_shape(part, *args)

    def nothing(*args):
        return jax.tree.map(lambda s: jnp.zeros(s.shape, s.dtype), shapes)

    return lax.cond(order[0] >= 0, part, nothing, *args)


def pick(arr, index, axis=0):
    return lax.dynamic_index_in_dim(arr, index, axis, keepdims=False)


def per_device(x, weights, order, mask, low_u, low_v, cot):
    dp = lax.axis_index("dp").astype(jnp.int32)
    ylo, core = dp // 2, dp % 2
    both = ("feat", "dp")
    levels = jnp.arange(8, dtype=jnp.int32)
    slots = 1 + jnp.sum(jnp.where(order[None, :] == levels[:, None], levels[None, :], 0), 1)
    info = jnp.concatenate([slots, jnp.stack([ylo, core, dp])]).astype(jnp.int32)

    cpart, xs = nn(x, low_u), slices(info, mask, x)
    p3, p5, p7 = swap(x, "feat", 1), swap(x, "feat", 4), swap(x, "feat", 16)
    c = sum_feat(cpart, (16, 3, 12))
    c, p3, p5, xs = lax.optimization_barrier((c, p3, p5, xs))
    p4, p6 = swap(p3, "feat", 3), swap(p5, "feat", 12)
    xn = swap(xs, "dp", 2)
    hn = swap(xs, both, 66)
    coeff = sum_feat(c, (1, 4)).astype(BF16)
    mixed = near_mix(info, mask, x, p3, p5, p7, weights)
    coeff, xn, hn, mixed = lax.optimization_barrier((coeff, xn, hn, mixed))
    out, delta, t3, t4, t5, t6, bpart = middle(
        info, mask, mixed, p4, p6, weights, coeff, low_v, cot
    )

    dn = swap(delta, "dp", 2)
    r4, r6 = swap(t4, "feat", 3), swap(t6, "feat", 12)

    far_keep, far_send = far_grads(info, mask, (p3, p4, p5, p6), delta)
    b = sum_feat(bpart, (1,))

    def beside_first(keep, send, delta, b, weights):
        got = swap(send, "dp", 1)
        back = local_back(info, mask, delta, weights)
        away = pick(keep, 1 - ylo) + pick(got, 1 - ylo).astype(F32)
        return sum_feat(b, (4,)), back, got, away.astype(BF16)

    b, back, far_near, far_send = beside(
        order, beside_first, far_keep, far_send, delta, b, weights
    )
    hi = hi_term(info, mask, dn, weights)
    r4, r6, b, far_send, hi = lax.optimization_barrier((r4, r6, b, far_send, hi))

    sx, sz = merge(info, mask, t3, r4, t5, r6)
    b = sum_feat(b, (16,))
    sx, sz, hi, b, far_send = lax.optimization_barrier((sx, sz, hi, b, far_send))
    sx, sz, t7 = swap(sx, "feat", 1), swap(sz, "feat", 4), swap(hi, both, 66)
    far_got = swap(far_send, "dp", 2)

    def beside_second(b, x, p7, xn, hn, delta, dn):
        b, dn = lax.optimization_barrier((b, dn))
        b = sum_feat(b, (3,))
        keep, send, v_keep, v_send = near_grads(info, mask, x, p7, xn, hn, delta, dn)
        b, send, v_send = lax.optimization_barrier((b, send, v_send))
        bc = sum_feat(b, (12,)).astype(BF16)
        bc, send, v_send = lax.optimization_barrier((bc, send, v_send))
        got = swap(send, "dp", 1)
        gu_keep, gu_send = grad_u_parts(info, mask, x, bc, v_send)
        gu_send, got = lax.optimization_barrier((gu_send, got))
        gu_got = swap(gu_send, "dp", 1)
        grad_w = assemble(info, mask, keep, got)
        return bc, grad_w, *grad_u_halves(info, mask, gu_keep, gu_got, v_keep)

    bc, grad_w, gu_keep, gu_send, grad_v = beside(order, beside_second, b, x, p7, xn, hn, delta, dn)
    gu_send, sx, sz, t7, far_got = lax.optimization_barrier((gu_send, sx, sz, t7, far_got))
    grad_u = (gu_keep + swap(gu_send, "dp", 2).astype(F32)).astype(BF16)
    grad_x, grad_w = last(
        info, mask, back, [sx, sz, t7], bc, low_u, far_keep, far_near, far_got, grad_w
    )
    return out, grad_x, grad_w, grad_u, grad_v


def solution(mesh):
    return jax.shard_map(
        per_device,
        mesh=mesh,
        in_specs=(
            P("dp", "feat"),
            P(None, "feat", None, None),
            P(),
            P(None, "feat"),
            P("feat", None),
            P(None, "feat"),
            P("dp", "feat"),
        ),
        out_specs=(
            P("dp", "feat"),
            P("dp", "feat"),
            P(None, "feat", "dp", None),
            P(("feat", "dp"), None),
            P(None, ("feat", "dp")),
        ),
        check_vma=False,
    )
```

```python
import jax
import jax.numpy as jnp
from jax import lax
from jax.experimental import pallas as pl
from jax.experimental.pallas import tpu as pltpu
from jax.sharding import PartitionSpec as P

F32 = jnp.float32
BF16 = jnp.bfloat16
T = 256
D = 2048
B = 256
R = 128
NB = 8
STEPS = 4
W2 = 2 * B
MID, FAR, SEC = 4, 4, 4
YLO, CORE, DP = 8, 9, 10
LIMIT, LESS = 60 << 20, 52 << 20


def nn(a, b):
    return jnp.dot(a, b, preferred_element_type=F32)


def nt(a, b):
    return lax.dot_general(a, b, (((1,), (1,)), ((), ())), preferred_element_type=F32)


def tn(a, b):
    return lax.dot_general(a, b, (((0,), (0,)), ((), ())), preferred_element_type=F32)


def gelu_parts(value):
    cdf = 0.5 * (1.0 + lax.erf(value * 0.7071067811865476))
    slope = cdf + value * jnp.exp(-0.5 * value * value) * 0.3989422804014327
    return (value * cdf, slope)


def gate(info, mask, bit, block):
    return mask[info[bit] - 1, block].astype(F32)


def call(body, in_specs, out_specs, out_shape, flops, data, name, grid=STEPS, aliases=None, limit=LIMIT, scratch=()):
    return pl.pallas_call(
        body,
        grid_spec=pltpu.PrefetchScalarGridSpec(
            num_scalar_prefetch=2,
            grid=(grid,),
            in_specs=in_specs,
            out_specs=out_specs,
            scratch_shapes=list(scratch),
        ),
        out_shape=out_shape,
        input_output_aliases=aliases or {},
        compiler_params=pltpu.CompilerParams(
            dimension_semantics=("arbitrary",), vmem_limit_bytes=limit
        ),
        cost_estimate=pl.CostEstimate(flops=flops, bytes_accessed=data, transcendentals=0),
        name=name,
    )


def sds(shape, dtype):
    return jax.ShapeDtypeStruct(shape, dtype)


def col(width=W2, at=lambda i, info: i):
    return pl.BlockSpec((T, width), lambda i, info, mask: (0, at(i, info)))


def whole(shape):
    return pl.BlockSpec(shape, lambda i, info, mask: (0,) * len(shape))


def weight(bit, blocks=2):
    if bit is None:
        return pl.BlockSpec((1, blocks, B, B), lambda i, info, mask: (0, i, 0, 0))
    return pl.BlockSpec((1, blocks, B, B), lambda i, info, mask: (info[bit], i, 0, 0))


def blk(ref, j):
    return ref[:, j * B : (j + 1) * B]


OWN = [col(), col(at=lambda i, info: i ^ 1), col(at=lambda i, info: i ^ 2)]


def slices_body(info, mask, x, xs):
    for j in range(NB):
        b = blk(x, j)
        xs[:, j * 128 : (j + 1) * 128] = jnp.where(info[YLO] == 0, b[:, 128:], b[:, :128])


def slices(info, mask, x):
    return call(
        slices_body,
        [whole((T, D))],
        whole((T, D // 2)),
        sds((T, D // 2), BF16),
        0,
        2 << 20,
        "slices",
        1,
    )(info, mask, x)


def near_mix_body(info, mask, xa, xb, xc, p3, p5, p7, w, w0, w1, w2, w3, w5, w7, mixed):
    i = pl.program_id(0)
    for j in range(2):
        total = nn(blk(xa, j), w[0, j])
        for x, k, v, bit in (
            (xa, 1 - j, w0, 0),
            (xb, j, w1, 1),
            (xc, j, w2, 2),
            (p3, j, w3, 3),
            (p5, j, w5, 5),
            (p7, j, w7, 7),
        ):
            total += nn(blk(x, k), v[0, j]) * gate(info, mask, bit, 2 * i + j)
        mixed[:, j * B : (j + 1) * B] = total


def near_mix(info, mask, x, p3, p5, p7, weights):
    return call(
        near_mix_body,
        OWN + [col()] * 3 + [weight(b) for b in (None, 0, 1, 2, 3, 5, 7)],
        col(),
        sds((T, D), F32),
        14 * T * D * B,
        14 << 20,
        "near_mix",
    )(info, mask, x, x, x, p3, p5, p7, *([weights] * 7))


def middle_body(info, mask, mixed, p4, p6, w3, w4, w5, w6, *refs):
    coeff, low_v, cot, out, delta, t3, t4, t5, t6, bpart = refs
    i = pl.program_id(0)

    @pl.when(i == 0)
    def _():
        bpart[...] = jnp.zeros_like(bpart)
        delta[:, D:] = coeff[...]

    for j in range(MID):
        cols = slice(j * B, (j + 1) * B)
        pre = mixed[:, cols] + nn(coeff[...], low_v[:, cols])
        pre += nn(p4[:, cols], w4[0, j]) * gate(info, mask, 4, MID * i + j)
        pre += nn(p6[:, cols], w6[0, j]) * gate(info, mask, 6, MID * i + j)
        act, slope = gelu_parts(pre)
        out[:, cols] = act.astype(BF16)
        d = (cot[:, cols].astype(F32) * slope).astype(BF16)
        delta[:, pl.ds(pl.multiple_of((MID * i + j) * B, B), B)] = d
        bpart[...] += nt(d, low_v[:, cols])
        for bit, t, w in ((4, t4, w4), (6, t6, w6), (3, t3, w3), (5, t5, w5)):
            t[:, cols] = (nt(d, w[0, j]) * gate(info, mask, bit, MID * i + j)).astype(BF16)


def middle(info, mask, mixed, p4, p6, weights, coeff, low_v, cot):
    return call(
        middle_body,
        [col(MID * B)] * 3
        + [weight(b, MID) for b in range(3, 7)]
        + [whole((T, R)), pl.BlockSpec((R, MID * B), lambda i, info, mask: (0, i)), col(MID * B)],
        [col(MID * B), whole((T, D + R))] + [col(MID * B)] * 4 + [whole((T, R))],
        [sds((T, D), BF16), sds((T, D + R), BF16)]
        + [sds((T, D), BF16)] * 4
        + [sds((T, R), F32)],
        12 * T * D * B,
        18 << 20,
        "middle",
        NB // MID,
    )(info, mask, mixed, p4, p6, *([weights] * 4), coeff, low_v, cot)


def far_grads_body(info, mask, p3, p4, p5, p6, delta, keep, send):
    i = pl.program_id(0)
    first = info[CORE] == 0
    for j in range(FAR):
        d = blk(delta, j)
        for k, p in enumerate((p3, p4, p5, p6)):
            g = tn(blk(p, j), d) * gate(info, mask, 3 + k, FAR * i + j)
            for half in range(2):
                lo, hi = g[128 * half : 128 * half + 64], g[128 * half + 64 : 128 * half + 128]
                keep[half, k, j] = jnp.where(first, lo, hi)
                send[half, k, j] = jnp.where(first, hi, lo).astype(BF16)


def far_grads(info, mask, partners, delta):
    spec = pl.BlockSpec((2, 4, FAR, 64, B), lambda i, info, mask: (0, 0, i, 0, 0))
    return call(
        far_grads_body,
        [col(FAR * B)] * 5,
        [spec, spec],
        [sds((2, 4, NB, 64, B), F32), sds((2, 4, NB, 64, B), BF16)],
        T * D * B << 7,
        12 << 20,
        "far_grads",
        NB // FAR,
    )(info, mask, *partners, delta)


def second_body(info, mask, t3, r4, t5, r6, dn, w, sx, sz, hi):
    sx[...] = t3[...] + r4[...]
    sz[...] = t5[...] + r6[...]
    for j in range(SEC):
        g = gate(info, mask, 7, SEC * pl.program_id(0) + j)
        hi[:, j * B : (j + 1) * B] = (nt(blk(dn, j), w[0, j]) * g).astype(BF16)


def second(info, mask, t3, r4, t5, r6, dn, weights):
    return call(
        second_body,
        [col(SEC * B)] * 5 + [weight(7, SEC)],
        [col(SEC * B)] * 3,
        [sds((T, D), BF16)] * 3,
        2 * T * D * B,
        9 << 20,
        "second",
        NB // SEC,
    )(info, mask, t3, r4, t5, r6, dn, weights)


def local_back_body(info, mask, delta, w, w0, w1, w2, back):
    i = pl.program_id(0)

    @pl.when(i == 0)
    def _():
        back[...] = jnp.zeros_like(back)

    def place(step, j):
        return pl.ds(pl.multiple_of(step * W2 + j * B, B), B)

    for j in range(2):
        d, e = blk(delta, j), blk(delta, 1 - j)
        back[:, place(i, j)] += (
            nt(d, w[0, j]) + nt(e, w0[0, 1 - j]) * gate(info, mask, 0, 2 * i + 1 - j)
        )
        back[:, place(i ^ 1, j)] += nt(d, w1[0, j]) * gate(info, mask, 1, 2 * i + j)
        back[:, place(i ^ 2, j)] += nt(d, w2[0, j]) * gate(info, mask, 2, 2 * i + j)


def local_back(info, mask, delta, weights):
    return call(
        local_back_body,
        [col()] + [weight(b) for b in (None, 0, 1, 2)],
        whole((T, D)),
        sds((T, D), F32),
        8 * T * D * B,
        8 << 20,
        "local_back",
    )(info, mask, delta, *([weights] * 4))


def near_grads_body(info, mask, xa, xb, xc, p7, na, nb, nc, n7, delta, dn, co, cn, *outs):
    keep, send, vkeep, vsend = outs
    i = pl.program_id(0)
    first = info[CORE] == 0

    def half(ref, j):
        return ref[:, pl.ds(pl.multiple_of(j * B + info[YLO] * 128, 128), 128)]

    def part(ref, j):
        return ref[:, j * 128 : (j + 1) * 128]

    for j in range(2):
        own = [half(xa, j), half(xa, 1 - j), half(xb, j), half(xc, j), half(p7, j)]
        got = [part(na, j), part(na, 1 - j), part(nb, j), part(nc, j), part(n7, j)]
        g = tn(jnp.concatenate(own, 1), blk(delta, j)) + tn(jnp.concatenate(got, 1), blk(dn, j))
        for k, bit in enumerate((None, 0, 1, 2, 7)):
            h = g[128 * k : 128 * (k + 1)]
            if bit is not None:
                h = h * gate(info, mask, bit, 2 * i + j)
            keep[k, j] = jnp.where(first, h[:64], h[64:])
            send[k, j] = jnp.where(first, h[64:], h[:64]).astype(BF16)

    @pl.when(i // 2 == info[YLO])
    def _():
        v = tn(co[...], delta[...]) + tn(cn[...], dn[...])

        @pl.when(i == info[DP])
        def _():
            vkeep[...] = v

        @pl.when(i != info[DP])
        def _():
            for k in range(W2 // R):
                vsend[k * R : (k + 1) * R] = v[:, k * R : (k + 1) * R].astype(BF16)


def near_grads(info, mask, x, p7, xn, hn, delta, dn):
    got = [col(B), col(B, lambda i, info: i ^ 1), col(B, lambda i, info: i ^ 2), col(B)]
    spec = pl.BlockSpec((5, 2, 64, B), lambda i, info, mask: (0, i, 0, 0))
    last = col(R, lambda i, info: D // R)
    return call(
        near_grads_body,
        OWN + [col()] + got + [col(), col(), last, last],
        [spec, spec, whole((R, W2)), whole((W2, R))],
        [
            sds((5, NB, 64, B), F32),
            sds((5, NB, 64, B), BF16),
            sds((R, W2), F32),
            sds((W2, R), BF16),
        ],
        10 * T * D * B,
        12 << 20,
        "near_grads",
        limit=LESS,
    )(info, mask, x, x, x, p7, xn, xn, xn, hn, delta, dn, delta, dn)


def grad_u_body(info, mask, x, bc, v, keep, send):
    i = pl.program_id(0)
    g = tn(x[...], bc[...])

    @pl.when(i % 2 == info[CORE])
    def _():
        keep[i // 2] = g

    @pl.when(i % 2 != info[CORE])
    def _():
        send[i // 2] = g.astype(BF16)

    @pl.when(i == 0)
    def _():
        send[2] = v[...]


def grad_u_parts(info, mask, x, bc, v_send):
    return call(
        grad_u_body,
        [col(), whole((T, R)), whole((W2, R))],
        [whole((2, W2, R)), whole((3, W2, R))],
        [sds((2, W2, R), F32), sds((3, W2, R), BF16)],
        2 * T * D * R,
        2 << 20,
        "grad_u",
        limit=LESS,
    )(info, mask, x, bc, v_send)


def grad_u_halves_body(info, mask, keep, got, v_keep, mine, other, grad_v):
    y = info[YLO]
    mine[...] = keep[y] + got[y].astype(F32)
    other[...] = (keep[1 - y] + got[1 - y].astype(F32)).astype(BF16)
    for k in range(W2 // R):
        at = slice(k * R, (k + 1) * R)
        grad_v[:, at] = (v_keep[:, at] + got[2, at].astype(F32)).astype(BF16)


def grad_u_halves(info, mask, keep, got, v_keep):
    return call(
        grad_u_halves_body,
        [whole((2, W2, R)), whole((3, W2, R)), whole((R, W2))],
        [whole((W2, R)), whole((W2, R)), whole((R, W2))],
        [sds((W2, R), F32), sds((W2, R), BF16), sds((R, W2), BF16)],
        0,
        1 << 20,
        "grad_u_halves",
        1,
        limit=LESS,
    )(info, mask, keep, got, v_keep)


def slot_copy(held, grad_w, sems, k, slot):
    return pltpu.make_async_copy(held.at[k], grad_w.at[slot], sems.at[k])


def last_body(info, mask, back, sx, sz, t7, bc, u, keep, near, got, before, out, grad_w, held, sems):
    i = pl.program_id(0)
    for j in range(2):
        held[2 * i + j] = (
            keep[0, j] + near[0, j].astype(F32) + got[j].astype(F32)
        ).astype(BF16)
        slot_copy(held, grad_w, sems, 2 * i + j, info[3 + 2 * i + j]).start()
    total = back[...] + nt(bc[...], u[...])
    for t in (sx, sz, t7):
        total += t[...].astype(F32)
    out[...] = total.astype(BF16)

    @pl.when(i == 1)
    def _():
        for k in range(4):
            slot_copy(held, grad_w, sems, k, info[3 + k]).wait()


def last(info, mask, back, terms, bc, low_u, keep, near, got, grad_w):
    half = pl.BlockSpec((1, 2, NB, 64, B), lambda i, info, mask: (info[YLO], i, 0, 0, 0))
    away = pl.BlockSpec(memory_space=pl.ANY)
    return call(
        last_body,
        [col(2 * W2)] * 4
        + [whole((T, R)), pl.BlockSpec((2 * W2, R), lambda i, info, mask: (i, 0)), half, half]
        + [pl.BlockSpec((2, NB, 64, B), lambda i, info, mask: (i, 0, 0, 0)), away],
        [col(2 * W2), away],
        [sds((T, D), BF16), sds((9, NB, 64, B), BF16)],
        2 * T * D * R,
        12 << 20,
        "last",
        2,
        aliases={11: 1},
        scratch=[pltpu.VMEM((4, NB, 64, B), BF16), pltpu.SemaphoreType.DMA((4,))],
    )(info, mask, back, *terms, bc, low_u, keep, near, got, grad_w)


def assemble_body(info, mask, keep, got, grad_w, held, sems):
    places = (0, info[0], info[1], info[2], info[7])
    for k, slot in enumerate(places):
        held[k] = (keep[k] + got[k].astype(F32)).astype(BF16)
        slot_copy(held, grad_w, sems, k, slot).start()
    for k, slot in enumerate(places):
        slot_copy(held, grad_w, sems, k, slot).wait()


def assemble(info, mask, keep, got):
    shape = (5, NB, 64, B)
    return call(
        assemble_body,
        [whole(shape)] * 2,
        pl.BlockSpec(memory_space=pl.ANY),
        sds((9, NB, 64, B), BF16),
        0,
        6 << 20,
        "assemble",
        1,
        limit=LESS,
        scratch=[pltpu.VMEM(shape, BF16), pltpu.SemaphoreType.DMA((5,))],
    )(info, mask, keep, got)


def swap(value, axis, offset):
    sizes = 1
    for name in axis if isinstance(axis, tuple) else (axis,):
        sizes *= lax.axis_size(name)
    return lax.ppermute(value, axis, [(i, i ^ offset) for i in range(sizes)])


def sum_feat(value, offsets):
    for offset in offsets:
        value = value + swap(value, "feat", offset)
    return value


def beside(order, part, *args):
    shapes = jax.eval_shape(part, *args)

    def nothing(*args):
        return jax.tree.map(lambda s: jnp.zeros(s.shape, s.dtype), shapes)

    return lax.cond(order[0] >= 0, part, nothing, *args)


def pick(arr, index, axis=0):
    return lax.dynamic_index_in_dim(arr, index, axis, keepdims=False)


def per_device(x, weights, order, mask, low_u, low_v, cot):
    dp = lax.axis_index("dp").astype(jnp.int32)
    ylo, core = dp // 2, dp % 2
    both = ("feat", "dp")
    levels = jnp.arange(8, dtype=jnp.int32)
    slots = 1 + jnp.sum(jnp.where(order[None, :] == levels[:, None], levels[None, :], 0), 1)
    info = jnp.concatenate([slots, jnp.stack([ylo, core, dp])]).astype(jnp.int32)

    cpart, xs = nn(x, low_u), slices(info, mask, x)
    p3, p5, p7 = swap(x, "feat", 1), swap(x, "feat", 4), swap(x, "feat", 16)
    c = sum_feat(cpart, (16, 3, 12))
    c, p3, p5, xs = lax.optimization_barrier((c, p3, p5, xs))
    p4, p6 = swap(p3, "feat", 3), swap(p5, "feat", 12)
    xn = swap(xs, "dp", 2)
    hn = swap(xs, both, 66)
    coeff = sum_feat(c, (1, 4)).astype(BF16)
    mixed = near_mix(info, mask, x, p3, p5, p7, weights)
    coeff, xn, hn, mixed = lax.optimization_barrier((coeff, xn, hn, mixed))
    out, delta, t3, t4, t5, t6, bpart = middle(
        info, mask, mixed, p4, p6, weights, coeff, low_v, cot
    )

    dn = swap(delta, "dp", 2)
    r4, r6 = swap(t4, "feat", 3), swap(t6, "feat", 12)

    far_keep, far_send = far_grads(info, mask, (p3, p4, p5, p6), delta)
    b = sum_feat(bpart, (16,))

    def beside_first(keep, send, delta, b, weights):
        got = swap(send, "dp", 1)
        back = local_back(info, mask, delta, weights)
        b, back, got = lax.optimization_barrier((sum_feat(b, (1,)), back, got))
        away = pick(keep, 1 - ylo) + pick(got, 1 - ylo).astype(F32)
        return sum_feat(b, (4,)), back, got, away.astype(BF16)

    b, back, far_near, far_send = beside(
        order, beside_first, far_keep, far_send, delta, b, weights
    )
    r4, r6, dn, b, far_send = lax.optimization_barrier((r4, r6, dn, b, far_send))

    sx, sz, hi = second(info, mask, t3, r4, t5, r6, dn, weights)
    sx, sz, hi, far_send = lax.optimization_barrier((sx, sz, hi, far_send))
    sx, sz, t7 = swap(sx, "feat", 1), swap(sz, "feat", 4), swap(hi, both, 66)
    far_got = swap(far_send, "dp", 2)

    def beside_second(b, x, p7, xn, hn, delta, dn):
        b, dn = lax.optimization_barrier((b, dn))
        b = sum_feat(b, (3,))
        keep, send, v_keep, v_send = near_grads(info, mask, x, p7, xn, hn, delta, dn)
        b, send, v_send = lax.optimization_barrier((b, send, v_send))
        bc = sum_feat(b, (12,)).astype(BF16)
        bc, send, v_send = lax.optimization_barrier((bc, send, v_send))
        got = swap(send, "dp", 1)
        gu_keep, gu_send = grad_u_parts(info, mask, x, bc, v_send)
        gu_send, got = lax.optimization_barrier((gu_send, got))
        gu_got = swap(gu_send, "dp", 1)
        grad_w = assemble(info, mask, keep, got)
        return bc, grad_w, *grad_u_halves(info, mask, gu_keep, gu_got, v_keep)

    bc, grad_w, gu_keep, gu_send, grad_v = beside(order, beside_second, b, x, p7, xn, hn, delta, dn)
    gu_send, sx, sz, t7, far_got = lax.optimization_barrier((gu_send, sx, sz, t7, far_got))
    grad_u = (gu_keep + swap(gu_send, "dp", 2).astype(F32)).astype(BF16)
    grad_x, grad_w = last(
        info, mask, back, [sx, sz, t7], bc, low_u, far_keep, far_near, far_got, grad_w
    )
    return out, grad_x, grad_w, grad_u, grad_v


def solution(mesh):
    return jax.shard_map(
        per_device,
        mesh=mesh,
        in_specs=(
            P("dp", "feat"),
            P(None, "feat", None, None),
            P(),
            P(None, "feat"),
            P("feat", None),
            P(None, "feat"),
            P("dp", "feat"),
        ),
        out_specs=(
            P("dp", "feat"),
            P("dp", "feat"),
            P(None, "feat", "dp", None),
            P(("feat", "dp"), None),
            P(None, ("feat", "dp")),
        ),
        check_vma=False,
    )
```

```python
import jax
import jax.numpy as jnp
from jax import lax
from jax.experimental import pallas as pl
from jax.experimental.pallas import tpu as pltpu
from jax.sharding import PartitionSpec as P

F32 = jnp.float32
BF16 = jnp.bfloat16
T = 256
D = 2048
B = 256
R = 128
NB = 8
STEPS = 4
W2 = 2 * B
MID, FAR, SEC = 4, 4, 4
YLO, CORE, DP = 8, 9, 10
LIMIT, LESS = 60 << 20, 52 << 20


def nn(a, b):
    return jnp.dot(a, b, preferred_element_type=F32)


def nt(a, b):
    return lax.dot_general(a, b, (((1,), (1,)), ((), ())), preferred_element_type=F32)


def tn(a, b):
    return lax.dot_general(a, b, (((0,), (0,)), ((), ())), preferred_element_type=F32)


def gelu_parts(value):
    cdf = 0.5 * (1.0 + lax.erf(value * 0.7071067811865476))
    slope = cdf + value * jnp.exp(-0.5 * value * value) * 0.3989422804014327
    return (value * cdf, slope)


def gate(info, mask, bit, block):
    return mask[info[bit] - 1, block].astype(F32)


def call(body, in_specs, out_specs, out_shape, flops, data, name, grid=STEPS, aliases=None, limit=LIMIT, scratch=()):
    return pl.pallas_call(
        body,
        grid_spec=pltpu.PrefetchScalarGridSpec(
            num_scalar_prefetch=2,
            grid=(grid,),
            in_specs=in_specs,
            out_specs=out_specs,
            scratch_shapes=list(scratch),
        ),
        out_shape=out_shape,
        input_output_aliases=aliases or {},
        compiler_params=pltpu.CompilerParams(
            dimension_semantics=("arbitrary",), vmem_limit_bytes=limit
        ),
        cost_estimate=pl.CostEstimate(flops=flops, bytes_accessed=data, transcendentals=0),
        name=name,
    )


def sds(shape, dtype):
    return jax.ShapeDtypeStruct(shape, dtype)


def col(width=W2, at=lambda i, info: i):
    return pl.BlockSpec((T, width), lambda i, info, mask: (0, at(i, info)))


def whole(shape):
    return pl.BlockSpec(shape, lambda i, info, mask: (0,) * len(shape))


def weight(bit, blocks=2):
    if bit is None:
        return pl.BlockSpec((1, blocks, B, B), lambda i, info, mask: (0, i, 0, 0))
    return pl.BlockSpec((1, blocks, B, B), lambda i, info, mask: (info[bit], i, 0, 0))


def blk(ref, j):
    return ref[:, j * B : (j + 1) * B]


OWN = [col(), col(at=lambda i, info: i ^ 1), col(at=lambda i, info: i ^ 2)]


def slices_body(info, mask, x, xs):
    for j in range(NB):
        b = blk(x, j)
        xs[:, j * 128 : (j + 1) * 128] = jnp.where(info[YLO] == 0, b[:, 128:], b[:, :128])


def slices(info, mask, x):
    return call(
        slices_body,
        [whole((T, D))],
        whole((T, D // 2)),
        sds((T, D // 2), BF16),
        0,
        2 << 20,
        "slices",
        1,
    )(info, mask, x)


def near_mix_body(info, mask, xa, xb, xc, p3, p5, p7, w, w0, w1, w2, w3, w5, w7, mixed):
    i = pl.program_id(0)
    for j in range(2):
        total = nn(blk(xa, j), w[0, j])
        for x, k, v, bit in (
            (xa, 1 - j, w0, 0),
            (xb, j, w1, 1),
            (xc, j, w2, 2),
            (p3, j, w3, 3),
            (p5, j, w5, 5),
            (p7, j, w7, 7),
        ):
            total += nn(blk(x, k), v[0, j]) * gate(info, mask, bit, 2 * i + j)
        mixed[:, j * B : (j + 1) * B] = total


def near_mix(info, mask, x, p3, p5, p7, weights):
    return call(
        near_mix_body,
        OWN + [col()] * 3 + [weight(b) for b in (None, 0, 1, 2, 3, 5, 7)],
        col(),
        sds((T, D), F32),
        14 * T * D * B,
        14 << 20,
        "near_mix",
    )(info, mask, x, x, x, p3, p5, p7, *([weights] * 7))


def middle_body(info, mask, mixed, p4, p6, w3, w4, w5, w6, *refs):
    coeff, low_v, cot, out, delta, t3, t4, t5, t6, bpart = refs
    i = pl.program_id(0)

    @pl.when(i == 0)
    def _():
        bpart[...] = jnp.zeros_like(bpart)
        delta[:, D:] = coeff[...]

    for j in range(MID):
        cols = slice(j * B, (j + 1) * B)
        pre = mixed[:, cols] + nn(coeff[...], low_v[:, cols])
        pre += nn(p4[:, cols], w4[0, j]) * gate(info, mask, 4, MID * i + j)
        pre += nn(p6[:, cols], w6[0, j]) * gate(info, mask, 6, MID * i + j)
        act, slope = gelu_parts(pre)
        out[:, cols] = act.astype(BF16)
        d = (cot[:, cols].astype(F32) * slope).astype(BF16)
        delta[:, pl.ds(pl.multiple_of((MID * i + j) * B, B), B)] = d
        bpart[...] += nt(d, low_v[:, cols])
        for bit, t, w in ((4, t4, w4), (6, t6, w6), (3, t3, w3), (5, t5, w5)):
            t[:, cols] = (nt(d, w[0, j]) * gate(info, mask, bit, MID * i + j)).astype(BF16)


def middle(info, mask, mixed, p4, p6, weights, coeff, low_v, cot):
    return call(
        middle_body,
        [col(MID * B)] * 3
        + [weight(b, MID) for b in range(3, 7)]
        + [whole((T, R)), pl.BlockSpec((R, MID * B), lambda i, info, mask: (0, i)), col(MID * B)],
        [col(MID * B), whole((T, D + R))] + [col(MID * B)] * 4 + [whole((T, R))],
        [sds((T, D), BF16), sds((T, D + R), BF16)]
        + [sds((T, D), BF16)] * 4
        + [sds((T, R), F32)],
        12 * T * D * B,
        18 << 20,
        "middle",
        NB // MID,
    )(info, mask, mixed, p4, p6, *([weights] * 4), coeff, low_v, cot)


def far_grads_body(info, mask, p3, p4, p5, p6, delta, keep, send):
    i = pl.program_id(0)
    first = info[CORE] == 0
    for j in range(FAR):
        d = blk(delta, j)
        for k, p in enumerate((p3, p4, p5, p6)):
            g = tn(blk(p, j), d) * gate(info, mask, 3 + k, FAR * i + j)
            for half in range(2):
                lo, hi = g[128 * half : 128 * half + 64], g[128 * half + 64 : 128 * half + 128]
                keep[half, k, j] = jnp.where(first, lo, hi)
                send[half, k, j] = jnp.where(first, hi, lo).astype(BF16)


def far_grads(info, mask, partners, delta):
    spec = pl.BlockSpec((2, 4, FAR, 64, B), lambda i, info, mask: (0, 0, i, 0, 0))
    return call(
        far_grads_body,
        [col(FAR * B)] * 5,
        [spec, spec],
        [sds((2, 4, NB, 64, B), F32), sds((2, 4, NB, 64, B), BF16)],
        T * D * B << 7,
        12 << 20,
        "far_grads",
        NB // FAR,
    )(info, mask, *partners, delta)


def second_body(info, mask, t3, r4, t5, r6, dn, w, sx, sz, hi):
    sx[...] = t3[...] + r4[...]
    sz[...] = t5[...] + r6[...]
    for j in range(SEC):
        g = gate(info, mask, 7, SEC * pl.program_id(0) + j)
        hi[:, j * B : (j + 1) * B] = (nt(blk(dn, j), w[0, j]) * g).astype(BF16)


def second(info, mask, t3, r4, t5, r6, dn, weights):
    return call(
        second_body,
        [col(SEC * B)] * 5 + [weight(7, SEC)],
        [col(SEC * B)] * 3,
        [sds((T, D), BF16)] * 3,
        2 * T * D * B,
        9 << 20,
        "second",
        NB // SEC,
    )(info, mask, t3, r4, t5, r6, dn, weights)


def local_back_body(info, mask, delta, w, w0, w1, w2, back):
    i = pl.program_id(0)

    @pl.when(i == 0)
    def _():
        back[...] = jnp.zeros_like(back)

    def place(step, j):
        return pl.ds(pl.multiple_of(step * W2 + j * B, B), B)

    for j in range(2):
        d, e = blk(delta, j), blk(delta, 1 - j)
        back[:, place(i, j)] += (
            nt(d, w[0, j]) + nt(e, w0[0, 1 - j]) * gate(info, mask, 0, 2 * i + 1 - j)
        )
        back[:, place(i ^ 1, j)] += nt(d, w1[0, j]) * gate(info, mask, 1, 2 * i + j)
        back[:, place(i ^ 2, j)] += nt(d, w2[0, j]) * gate(info, mask, 2, 2 * i + j)


def local_back(info, mask, delta, weights):
    return call(
        local_back_body,
        [col()] + [weight(b) for b in (None, 0, 1, 2)],
        whole((T, D)),
        sds((T, D), F32),
        8 * T * D * B,
        8 << 20,
        "local_back",
    )(info, mask, delta, *([weights] * 4))


def near_grads_body(info, mask, xa, xb, xc, p7, na, nb, nc, n7, delta, dn, co, cn, *outs):
    keep, send, vkeep, vsend = outs
    i = pl.program_id(0)
    first = info[CORE] == 0

    def half(ref, j):
        return ref[:, pl.ds(pl.multiple_of(j * B + info[YLO] * 128, 128), 128)]

    def part(ref, j):
        return ref[:, j * 128 : (j + 1) * 128]

    for j in range(2):
        own = [half(xa, j), half(xa, 1 - j), half(xb, j), half(xc, j), half(p7, j)]
        got = [part(na, j), part(na, 1 - j), part(nb, j), part(nc, j), part(n7, j)]
        g = tn(jnp.concatenate(own, 1), blk(delta, j)) + tn(jnp.concatenate(got, 1), blk(dn, j))
        for k, bit in enumerate((None, 0, 1, 2, 7)):
            h = g[128 * k : 128 * (k + 1)]
            if bit is not None:
                h = h * gate(info, mask, bit, 2 * i + j)
            keep[k, j] = jnp.where(first, h[:64], h[64:])
            send[k, j] = jnp.where(first, h[64:], h[:64]).astype(BF16)

    @pl.when(i // 2 == info[YLO])
    def _():
        v = tn(co[...], delta[...]) + tn(cn[...], dn[...])

        @pl.when(i == info[DP])
        def _():
            vkeep[...] = v

        @pl.when(i != info[DP])
        def _():
            for k in range(W2 // R):
                vsend[k * R : (k + 1) * R] = v[:, k * R : (k + 1) * R].astype(BF16)


def near_grads(info, mask, x, p7, xn, hn, delta, dn):
    got = [col(B), col(B, lambda i, info: i ^ 1), col(B, lambda i, info: i ^ 2), col(B)]
    spec = pl.BlockSpec((5, 2, 64, B), lambda i, info, mask: (0, i, 0, 0))
    last = col(R, lambda i, info: D // R)
    return call(
        near_grads_body,
        OWN + [col()] + got + [col(), col(), last, last],
        [spec, spec, whole((R, W2)), whole((W2, R))],
        [
            sds((5, NB, 64, B), F32),
            sds((5, NB, 64, B), BF16),
            sds((R, W2), F32),
            sds((W2, R), BF16),
        ],
        10 * T * D * B,
        12 << 20,
        "near_grads",
        limit=LESS,
    )(info, mask, x, x, x, p7, xn, xn, xn, hn, delta, dn, delta, dn)


def grad_u_body(info, mask, x, bc, v, keep, send):
    i = pl.program_id(0)
    g = tn(x[...], bc[...])

    @pl.when(i % 2 == info[CORE])
    def _():
        keep[i // 2] = g

    @pl.when(i % 2 != info[CORE])
    def _():
        send[i // 2] = g.astype(BF16)

    @pl.when(i == 0)
    def _():
        send[2] = v[...]


def grad_u_parts(info, mask, x, bc, v_send):
    return call(
        grad_u_body,
        [col(), whole((T, R)), whole((W2, R))],
        [whole((2, W2, R)), whole((3, W2, R))],
        [sds((2, W2, R), F32), sds((3, W2, R), BF16)],
        2 * T * D * R,
        2 << 20,
        "grad_u",
        limit=LESS,
    )(info, mask, x, bc, v_send)


def grad_u_halves_body(info, mask, keep, got, v_keep, mine, other, grad_v):
    y = info[YLO]
    mine[...] = keep[y] + got[y].astype(F32)
    other[...] = (keep[1 - y] + got[1 - y].astype(F32)).astype(BF16)
    for k in range(W2 // R):
        at = slice(k * R, (k + 1) * R)
        grad_v[:, at] = (v_keep[:, at] + got[2, at].astype(F32)).astype(BF16)


def grad_u_halves(info, mask, keep, got, v_keep):
    return call(
        grad_u_halves_body,
        [whole((2, W2, R)), whole((3, W2, R)), whole((R, W2))],
        [whole((W2, R)), whole((W2, R)), whole((R, W2))],
        [sds((W2, R), F32), sds((W2, R), BF16), sds((R, W2), BF16)],
        0,
        1 << 20,
        "grad_u_halves",
        1,
        limit=LESS,
    )(info, mask, keep, got, v_keep)


def slot_copy(held, grad_w, sems, k, slot):
    return pltpu.make_async_copy(held.at[k], grad_w.at[slot], sems.at[k])


def last_body(info, mask, back, sx, sz, t7, bc, u, keep, got, before, out, grad_w, held, sems):
    i = pl.program_id(0)
    for j in range(2):
        held[2 * i + j] = (keep[j] + got[j].astype(F32)).astype(BF16)
        slot_copy(held, grad_w, sems, 2 * i + j, info[3 + 2 * i + j]).start()
    total = back[...] + nt(bc[...], u[...])
    for t in (sx, sz, t7):
        total += t[...].astype(F32)
    out[...] = total.astype(BF16)

    @pl.when(i == 1)
    def _():
        for k in range(4):
            slot_copy(held, grad_w, sems, k, info[3 + k]).wait()


def last(info, mask, back, terms, bc, low_u, keep, got, grad_w):
    part = pl.BlockSpec((2, NB, 64, B), lambda i, info, mask: (i, 0, 0, 0))
    away = pl.BlockSpec(memory_space=pl.ANY)
    return call(
        last_body,
        [col(2 * W2)] * 4
        + [whole((T, R)), pl.BlockSpec((2 * W2, R), lambda i, info, mask: (i, 0)), part, part, away],
        [col(2 * W2), away],
        [sds((T, D), BF16), sds((9, NB, 64, B), BF16)],
        2 * T * D * R,
        12 << 20,
        "last",
        2,
        aliases={10: 1},
        scratch=[pltpu.VMEM((4, NB, 64, B), BF16), pltpu.SemaphoreType.DMA((4,))],
    )(info, mask, back, *terms, bc, low_u, keep, got, grad_w)


def assemble_body(info, mask, keep, got, grad_w, held, sems):
    places = (0, info[0], info[1], info[2], info[7])
    for k, slot in enumerate(places):
        held[k] = (keep[k] + got[k].astype(F32)).astype(BF16)
        slot_copy(held, grad_w, sems, k, slot).start()
    for k, slot in enumerate(places):
        slot_copy(held, grad_w, sems, k, slot).wait()


def assemble(info, mask, keep, got):
    shape = (5, NB, 64, B)
    return call(
        assemble_body,
        [whole(shape)] * 2,
        pl.BlockSpec(memory_space=pl.ANY),
        sds((9, NB, 64, B), BF16),
        0,
        6 << 20,
        "assemble",
        1,
        limit=LESS,
        scratch=[pltpu.VMEM(shape, BF16), pltpu.SemaphoreType.DMA((5,))],
    )(info, mask, keep, got)


def swap(value, axis, offset):
    sizes = 1
    for name in axis if isinstance(axis, tuple) else (axis,):
        sizes *= lax.axis_size(name)
    return lax.ppermute(value, axis, [(i, i ^ offset) for i in range(sizes)])


def sum_feat(value, offsets):
    for offset in offsets:
        value = value + swap(value, "feat", offset)
    return value


def beside(order, part, *args):
    shapes = jax.eval_shape(part, *args)

    def nothing(*args):
        return jax.tree.map(lambda s: jnp.zeros(s.shape, s.dtype), shapes)

    return lax.cond(order[0] >= 0, part, nothing, *args)


def pick(arr, index, axis=0):
    return lax.dynamic_index_in_dim(arr, index, axis, keepdims=False)


def per_device(x, weights, order, mask, low_u, low_v, cot):
    dp = lax.axis_index("dp").astype(jnp.int32)
    ylo, core = dp // 2, dp % 2
    both = ("feat", "dp")
    levels = jnp.arange(8, dtype=jnp.int32)
    slots = 1 + jnp.sum(jnp.where(order[None, :] == levels[:, None], levels[None, :], 0), 1)
    info = jnp.concatenate([slots, jnp.stack([ylo, core, dp])]).astype(jnp.int32)

    cpart, xs = nn(x, low_u), slices(info, mask, x)
    p3, p5, p7 = swap(x, "feat", 1), swap(x, "feat", 4), swap(x, "feat", 16)
    c = sum_feat(cpart, (16, 3, 12))
    c, p3, xs = lax.optimization_barrier((c, p3, xs))
    p4, p6 = swap(p3, "feat", 3), swap(p5, "feat", 12)
    xn = swap(xs, "dp", 2)
    hn = swap(xs, both, 66)
    coeff = sum_feat(c, (1, 4)).astype(BF16)
    mixed = near_mix(info, mask, x, p3, p5, p7, weights)
    coeff, xn, hn, mixed = lax.optimization_barrier((coeff, xn, hn, mixed))
    out, delta, t3, t4, t5, t6, bpart = middle(
        info, mask, mixed, p4, p6, weights, coeff, low_v, cot
    )

    dn = swap(delta, "dp", 2)
    r4, r6 = swap(t4, "feat", 3), swap(t6, "feat", 12)

    far_keep, far_send = far_grads(info, mask, (p3, p4, p5, p6), delta)
    b = sum_feat(bpart, (16,))

    def beside_first(keep, send, delta, b, weights):
        got = swap(send, "dp", 1)
        back = local_back(info, mask, delta, weights)
        b, back, got = lax.optimization_barrier((sum_feat(b, (1,)), back, got))
        away = pick(keep, 1 - ylo) + pick(got, 1 - ylo).astype(F32)
        return sum_feat(b, (4,)), back, got, away.astype(BF16)

    b, back, far_near, far_send = beside(
        order, beside_first, far_keep, far_send, delta, b, weights
    )
    r4, r6, dn, b, far_send = lax.optimization_barrier((r4, r6, dn, b, far_send))

    sx, sz, hi = second(info, mask, t3, r4, t5, r6, dn, weights)
    sx, sz, hi, far_send = lax.optimization_barrier((sx, sz, hi, far_send))
    sx, sz, t7 = swap(sx, "feat", 1), swap(sz, "feat", 4), swap(hi, both, 66)
    far_got = swap(far_send, "dp", 2)

    def beside_second(b, x, p7, xn, hn, delta, dn, far_keep, far_near):
        b, dn = lax.optimization_barrier((b, dn))
        b = sum_feat(b, (3,))
        keep, send, v_keep, v_send = near_grads(info, mask, x, p7, xn, hn, delta, dn)
        b, send, v_send, far_keep, far_near = lax.optimization_barrier(
            (b, send, v_send, far_keep, far_near)
        )
        far = pick(far_keep, ylo) + pick(far_near, ylo).astype(F32)
        bc = sum_feat(b, (12,)).astype(BF16)
        bc, send, v_send, far = lax.optimization_barrier((bc, send, v_send, far))
        got = swap(send, "dp", 1)
        gu_keep, gu_send = grad_u_parts(info, mask, x, bc, v_send)
        gu_send, got = lax.optimization_barrier((gu_send, got))
        gu_got = swap(gu_send, "dp", 1)
        grad_w = assemble(info, mask, keep, got)
        return far, bc, grad_w, *grad_u_halves(info, mask, gu_keep, gu_got, v_keep)

    far, bc, grad_w, gu_keep, gu_send, grad_v = beside(
        order, beside_second, b, x, p7, xn, hn, delta, dn, far_keep, far_near
    )
    gu_send, sx, sz, t7, far_got = lax.optimization_barrier((gu_send, sx, sz, t7, far_got))
    grad_u = (gu_keep + swap(gu_send, "dp", 2).astype(F32)).astype(BF16)
    grad_x, grad_w = last(
        info, mask, back, [sx, sz, t7], bc, low_u, far, far_got, grad_w
    )
    return out, grad_x, grad_w, grad_u, grad_v


def solution(mesh):
    return jax.shard_map(
        per_device,
        mesh=mesh,
        in_specs=(
            P("dp", "feat"),
            P(None, "feat", None, None),
            P(),
            P(None, "feat"),
            P("feat", None),
            P(None, "feat"),
            P("dp", "feat"),
        ),
        out_specs=(
            P("dp", "feat"),
            P("dp", "feat"),
            P(None, "feat", "dp", None),
            P(("feat", "dp"), None),
            P(None, ("feat", "dp")),
        ),
        check_vma=False,
    )
```

```python
import jax
import jax.numpy as jnp
from jax import lax
from jax.experimental import pallas as pl
from jax.experimental.pallas import tpu as pltpu
from jax.sharding import PartitionSpec as P

F32 = jnp.float32
BF16 = jnp.bfloat16
T = 256
D = 2048
B = 256
R = 128
NB = 8
STEPS = 4
W2 = 2 * B
MID, FAR, SEC = 4, 4, 4
YLO, CORE, DP = 8, 9, 10
LIMIT, LESS = 60 << 20, 52 << 20


def nn(a, b):
    return jnp.dot(a, b, preferred_element_type=F32)


def nt(a, b):
    return lax.dot_general(a, b, (((1,), (1,)), ((), ())), preferred_element_type=F32)


def tn(a, b):
    return lax.dot_general(a, b, (((0,), (0,)), ((), ())), preferred_element_type=F32)


def gelu_parts(value):
    cdf = 0.5 * (1.0 + lax.erf(value * 0.7071067811865476))
    slope = cdf + value * jnp.exp(-0.5 * value * value) * 0.3989422804014327
    return (value * cdf, slope)


def gate(info, mask, bit, block):
    return mask[info[bit] - 1, block].astype(F32)


def call(body, in_specs, out_specs, out_shape, flops, data, name, grid=STEPS, aliases=None, limit=LIMIT, scratch=()):
    return pl.pallas_call(
        body,
        grid_spec=pltpu.PrefetchScalarGridSpec(
            num_scalar_prefetch=2,
            grid=(grid,),
            in_specs=in_specs,
            out_specs=out_specs,
            scratch_shapes=list(scratch),
        ),
        out_shape=out_shape,
        input_output_aliases=aliases or {},
        compiler_params=pltpu.CompilerParams(
            dimension_semantics=("arbitrary",), vmem_limit_bytes=limit
        ),
        cost_estimate=pl.CostEstimate(flops=flops, bytes_accessed=data, transcendentals=0),
        name=name,
    )


def sds(shape, dtype):
    return jax.ShapeDtypeStruct(shape, dtype)


def col(width=W2, at=lambda i, info: i):
    return pl.BlockSpec((T, width), lambda i, info, mask: (0, at(i, info)))


def whole(shape):
    return pl.BlockSpec(shape, lambda i, info, mask: (0,) * len(shape))


def weight(bit, blocks=2):
    if bit is None:
        return pl.BlockSpec((1, blocks, B, B), lambda i, info, mask: (0, i, 0, 0))
    return pl.BlockSpec((1, blocks, B, B), lambda i, info, mask: (info[bit], i, 0, 0))


def blk(ref, j):
    return ref[:, j * B : (j + 1) * B]


OWN = [col(), col(at=lambda i, info: i ^ 1), col(at=lambda i, info: i ^ 2)]


def slices_body(info, mask, x, xs):
    for j in range(NB):
        b = blk(x, j)
        xs[:, j * 128 : (j + 1) * 128] = jnp.where(info[YLO] == 0, b[:, 128:], b[:, :128])


def slices(info, mask, x):
    return call(
        slices_body,
        [whole((T, D))],
        whole((T, D // 2)),
        sds((T, D // 2), BF16),
        0,
        2 << 20,
        "slices",
        1,
    )(info, mask, x)


def near_mix_body(info, mask, xa, xb, xc, p3, p5, p7, w, w0, w1, w2, w3, w5, w7, mixed):
    i = pl.program_id(0)
    for j in range(2):
        total = nn(blk(xa, j), w[0, j])
        for x, k, v, bit in (
            (xa, 1 - j, w0, 0),
            (xb, j, w1, 1),
            (xc, j, w2, 2),
            (p3, j, w3, 3),
            (p5, j, w5, 5),
            (p7, j, w7, 7),
        ):
            total += nn(blk(x, k), v[0, j]) * gate(info, mask, bit, 2 * i + j)
        mixed[:, j * B : (j + 1) * B] = total


def near_mix(info, mask, x, p3, p5, p7, weights):
    return call(
        near_mix_body,
        OWN + [col()] * 3 + [weight(b) for b in (None, 0, 1, 2, 3, 5, 7)],
        col(),
        sds((T, D), F32),
        14 * T * D * B,
        14 << 20,
        "near_mix",
    )(info, mask, x, x, x, p3, p5, p7, *([weights] * 7))


def middle_body(info, mask, mixed, p4, p6, w3, w4, w5, w6, *refs):
    coeff, low_v, cot, out, delta, t3, t4, t5, t6, bpart = refs
    i = pl.program_id(0)

    @pl.when(i == 0)
    def _():
        bpart[...] = jnp.zeros_like(bpart)
        delta[:, D:] = coeff[...]

    for j in range(MID):
        cols = slice(j * B, (j + 1) * B)
        pre = mixed[:, cols] + nn(coeff[...], low_v[:, cols])
        pre += nn(p4[:, cols], w4[0, j]) * gate(info, mask, 4, MID * i + j)
        pre += nn(p6[:, cols], w6[0, j]) * gate(info, mask, 6, MID * i + j)
        act, slope = gelu_parts(pre)
        out[:, cols] = act.astype(BF16)
        d = (cot[:, cols].astype(F32) * slope).astype(BF16)
        delta[:, pl.ds(pl.multiple_of((MID * i + j) * B, B), B)] = d
        bpart[...] += nt(d, low_v[:, cols])
        for bit, t, w in ((4, t4, w4), (6, t6, w6), (3, t3, w3), (5, t5, w5)):
            t[:, cols] = (nt(d, w[0, j]) * gate(info, mask, bit, MID * i + j)).astype(BF16)


def middle(info, mask, mixed, p4, p6, weights, coeff, low_v, cot):
    return call(
        middle_body,
        [col(MID * B)] * 3
        + [weight(b, MID) for b in range(3, 7)]
        + [whole((T, R)), pl.BlockSpec((R, MID * B), lambda i, info, mask: (0, i)), col(MID * B)],
        [col(MID * B), whole((T, D + R))] + [col(MID * B)] * 4 + [whole((T, R))],
        [sds((T, D), BF16), sds((T, D + R), BF16)]
        + [sds((T, D), BF16)] * 4
        + [sds((T, R), F32)],
        12 * T * D * B,
        18 << 20,
        "middle",
        NB // MID,
    )(info, mask, mixed, p4, p6, *([weights] * 4), coeff, low_v, cot)


def far_grads_body(info, mask, p3, p4, p5, p6, delta, keep, send):
    i = pl.program_id(0)
    first = info[CORE] == 0
    for j in range(FAR):
        d = blk(delta, j)
        for k, p in enumerate((p3, p4, p5, p6)):
            g = tn(blk(p, j), d) * gate(info, mask, 3 + k, FAR * i + j)
            for half in range(2):
                lo, hi = g[128 * half : 128 * half + 64], g[128 * half + 64 : 128 * half + 128]
                keep[half, k, j] = jnp.where(first, lo, hi)
                send[half, k, j] = jnp.where(first, hi, lo).astype(BF16)


def far_grads(info, mask, partners, delta):
    spec = pl.BlockSpec((2, 4, FAR, 64, B), lambda i, info, mask: (0, 0, i, 0, 0))
    return call(
        far_grads_body,
        [col(FAR * B)] * 5,
        [spec, spec],
        [sds((2, 4, NB, 64, B), F32), sds((2, 4, NB, 64, B), BF16)],
        T * D * B << 7,
        12 << 20,
        "far_grads",
        NB // FAR,
    )(info, mask, *partners, delta)


def second_body(info, mask, t3, r4, t5, r6, dn, w, sx, sz, hi):
    sx[...] = t3[...] + r4[...]
    sz[...] = t5[...] + r6[...]
    for j in range(SEC):
        g = gate(info, mask, 7, SEC * pl.program_id(0) + j)
        hi[:, j * B : (j + 1) * B] = (nt(blk(dn, j), w[0, j]) * g).astype(BF16)


def second(info, mask, t3, r4, t5, r6, dn, weights):
    return call(
        second_body,
        [col(SEC * B)] * 5 + [weight(7, SEC)],
        [col(SEC * B)] * 3,
        [sds((T, D), BF16)] * 3,
        2 * T * D * B,
        9 << 20,
        "second",
        NB // SEC,
    )(info, mask, t3, r4, t5, r6, dn, weights)


def local_back_body(info, mask, delta, w, w0, w1, w2, back):
    i = pl.program_id(0)

    @pl.when(i == 0)
    def _():
        back[...] = jnp.zeros_like(back)

    def place(step, j):
        return pl.ds(pl.multiple_of(step * W2 + j * B, B), B)

    for j in range(2):
        d, e = blk(delta, j), blk(delta, 1 - j)
        back[:, place(i, j)] += (
            nt(d, w[0, j]) + nt(e, w0[0, 1 - j]) * gate(info, mask, 0, 2 * i + 1 - j)
        )
        back[:, place(i ^ 1, j)] += nt(d, w1[0, j]) * gate(info, mask, 1, 2 * i + j)
        back[:, place(i ^ 2, j)] += nt(d, w2[0, j]) * gate(info, mask, 2, 2 * i + j)


def local_back(info, mask, delta, weights):
    return call(
        local_back_body,
        [col()] + [weight(b) for b in (None, 0, 1, 2)],
        whole((T, D)),
        sds((T, D), F32),
        8 * T * D * B,
        8 << 20,
        "local_back",
    )(info, mask, delta, *([weights] * 4))


def near_grads_body(info, mask, xa, xb, xc, p7, na, nb, nc, n7, delta, dn, co, cn, *outs):
    keep, send, vkeep, vsend = outs
    i = pl.program_id(0)
    first = info[CORE] == 0

    def half(ref, j):
        return ref[:, pl.ds(pl.multiple_of(j * B + info[YLO] * 128, 128), 128)]

    def part(ref, j):
        return ref[:, j * 128 : (j + 1) * 128]

    for j in range(2):
        own = [half(xa, j), half(xa, 1 - j), half(xb, j), half(xc, j), half(p7, j)]
        got = [part(na, j), part(na, 1 - j), part(nb, j), part(nc, j), part(n7, j)]
        g = tn(jnp.concatenate(own, 1), blk(delta, j)) + tn(jnp.concatenate(got, 1), blk(dn, j))
        for k, bit in enumerate((None, 0, 1, 2, 7)):
            h = g[128 * k : 128 * (k + 1)]
            if bit is not None:
                h = h * gate(info, mask, bit, 2 * i + j)
            keep[k, j] = jnp.where(first, h[:64], h[64:])
            send[k, j] = jnp.where(first, h[64:], h[:64]).astype(BF16)

    @pl.when(i // 2 == info[YLO])
    def _():
        v = tn(co[...], delta[...]) + tn(cn[...], dn[...])

        @pl.when(i == info[DP])
        def _():
            vkeep[...] = v

        @pl.when(i != info[DP])
        def _():
            for k in range(W2 // R):
                vsend[k * R : (k + 1) * R] = v[:, k * R : (k + 1) * R].astype(BF16)


def near_grads(info, mask, x, p7, xn, hn, delta, dn):
    got = [col(B), col(B, lambda i, info: i ^ 1), col(B, lambda i, info: i ^ 2), col(B)]
    spec = pl.BlockSpec((5, 2, 64, B), lambda i, info, mask: (0, i, 0, 0))
    last = col(R, lambda i, info: D // R)
    return call(
        near_grads_body,
        OWN + [col()] + got + [col(), col(), last, last],
        [spec, spec, whole((R, W2)), whole((W2, R))],
        [
            sds((5, NB, 64, B), F32),
            sds((5, NB, 64, B), BF16),
            sds((R, W2), F32),
            sds((W2, R), BF16),
        ],
        10 * T * D * B,
        12 << 20,
        "near_grads",
        limit=LESS,
    )(info, mask, x, x, x, p7, xn, xn, xn, hn, delta, dn, delta, dn)


def grad_u_body(info, mask, x, bc, v, keep, send):
    i = pl.program_id(0)
    g = tn(x[...], bc[...])

    @pl.when(i % 2 == info[CORE])
    def _():
        keep[i // 2] = g

    @pl.when(i % 2 != info[CORE])
    def _():
        send[i // 2] = g.astype(BF16)

    @pl.when(i == 0)
    def _():
        send[2] = v[...]


def grad_u_parts(info, mask, x, bc, v_send):
    return call(
        grad_u_body,
        [col(), whole((T, R)), whole((W2, R))],
        [whole((2, W2, R)), whole((3, W2, R))],
        [sds((2, W2, R), F32), sds((3, W2, R), BF16)],
        2 * T * D * R,
        2 << 20,
        "grad_u",
        limit=LESS,
    )(info, mask, x, bc, v_send)


def grad_u_halves_body(info, mask, keep, got, v_keep, mine, other, grad_v):
    y = info[YLO]
    mine[...] = keep[y] + got[y].astype(F32)
    other[...] = (keep[1 - y] + got[1 - y].astype(F32)).astype(BF16)
    for k in range(W2 // R):
        at = slice(k * R, (k + 1) * R)
        grad_v[:, at] = (v_keep[:, at] + got[2, at].astype(F32)).astype(BF16)


def grad_u_halves(info, mask, keep, got, v_keep):
    return call(
        grad_u_halves_body,
        [whole((2, W2, R)), whole((3, W2, R)), whole((R, W2))],
        [whole((W2, R)), whole((W2, R)), whole((R, W2))],
        [sds((W2, R), F32), sds((W2, R), BF16), sds((R, W2), BF16)],
        0,
        1 << 20,
        "grad_u_halves",
        1,
        limit=LESS,
    )(info, mask, keep, got, v_keep)


def slot_copy(held, grad_w, sems, k, slot):
    return pltpu.make_async_copy(held.at[k], grad_w.at[slot], sems.at[k])


def last_body(info, mask, back, sx, sz, t7, bc, u, keep, near, got, before, out, grad_w, held, sems):
    i = pl.program_id(0)
    for j in range(2):
        held[2 * i + j] = (
            keep[0, j] + near[0, j].astype(F32) + got[j].astype(F32)
        ).astype(BF16)
        slot_copy(held, grad_w, sems, 2 * i + j, info[3 + 2 * i + j]).start()
    total = back[...] + nt(bc[...], u[...])
    for t in (sx, sz, t7):
        total += t[...].astype(F32)
    out[...] = total.astype(BF16)

    @pl.when(i == 1)
    def _():
        for k in range(4):
            slot_copy(held, grad_w, sems, k, info[3 + k]).wait()


def last(info, mask, back, terms, bc, low_u, keep, near, got, grad_w):
    half = pl.BlockSpec((1, 2, NB, 64, B), lambda i, info, mask: (info[YLO], i, 0, 0, 0))
    away = pl.BlockSpec(memory_space=pl.ANY)
    return call(
        last_body,
        [col(2 * W2)] * 4
        + [whole((T, R)), pl.BlockSpec((2 * W2, R), lambda i, info, mask: (i, 0)), half, half]
        + [pl.BlockSpec((2, NB, 64, B), lambda i, info, mask: (i, 0, 0, 0)), away],
        [col(2 * W2), away],
        [sds((T, D), BF16), sds((9, NB, 64, B), BF16)],
        2 * T * D * R,
        12 << 20,
        "last",
        2,
        limit=40 << 20,
        aliases={11: 1},
        scratch=[pltpu.VMEM((4, NB, 64, B), BF16), pltpu.SemaphoreType.DMA((4,))],
    )(info, mask, back, *terms, bc, low_u, keep, near, got, grad_w)


def assemble_body(info, mask, keep, got, grad_w, held, sems):
    places = (0, info[0], info[1], info[2], info[7])
    for k, slot in enumerate(places):
        held[k] = (keep[k] + got[k].astype(F32)).astype(BF16)
        slot_copy(held, grad_w, sems, k, slot).start()
    for k, slot in enumerate(places):
        slot_copy(held, grad_w, sems, k, slot).wait()


def assemble(info, mask, keep, got):
    shape = (5, NB, 64, B)
    return call(
        assemble_body,
        [whole(shape)] * 2,
        pl.BlockSpec(memory_space=pl.ANY),
        sds((9, NB, 64, B), BF16),
        0,
        6 << 20,
        "assemble",
        1,
        limit=LESS,
        scratch=[pltpu.VMEM(shape, BF16), pltpu.SemaphoreType.DMA((5,))],
    )(info, mask, keep, got)


def swap(value, axis, offset):
    sizes = 1
    for name in axis if isinstance(axis, tuple) else (axis,):
        sizes *= lax.axis_size(name)
    return lax.ppermute(value, axis, [(i, i ^ offset) for i in range(sizes)])


def sum_feat(value, offsets):
    for offset in offsets:
        value = value + swap(value, "feat", offset)
    return value


def beside(order, part, *args):
    shapes = jax.eval_shape(part, *args)

    def nothing(*args):
        return jax.tree.map(lambda s: jnp.zeros(s.shape, s.dtype), shapes)

    return lax.cond(order[0] >= 0, part, nothing, *args)


def pick(arr, index, axis=0):
    return lax.dynamic_index_in_dim(arr, index, axis, keepdims=False)


def per_device(x, weights, order, mask, low_u, low_v, cot):
    dp = lax.axis_index("dp").astype(jnp.int32)
    ylo, core = dp // 2, dp % 2
    both = ("feat", "dp")
    levels = jnp.arange(8, dtype=jnp.int32)
    slots = 1 + jnp.sum(jnp.where(order[None, :] == levels[:, None], levels[None, :], 0), 1)
    info = jnp.concatenate([slots, jnp.stack([ylo, core, dp])]).astype(jnp.int32)

    cpart, xs = nn(x, low_u), slices(info, mask, x)
    p3, p5, p7 = swap(x, "feat", 1), swap(x, "feat", 4), swap(x, "feat", 16)
    c = sum_feat(cpart, (16, 3, 12))
    c, p3, p5, xs = lax.optimization_barrier((c, p3, p5, xs))
    p4, p6 = swap(p3, "feat", 3), swap(p5, "feat", 12)
    xn = swap(xs, "dp", 2)
    hn = swap(xs, both, 66)
    coeff = sum_feat(c, (1, 4)).astype(BF16)
    mixed = near_mix(info, mask, x, p3, p5, p7, weights)
    coeff, xn, hn, mixed = lax.optimization_barrier((coeff, xn, hn, mixed))
    out, delta, t3, t4, t5, t6, bpart = middle(
        info, mask, mixed, p4, p6, weights, coeff, low_v, cot
    )

    dn = swap(delta, "dp", 2)
    r4, r6 = swap(t4, "feat", 3), swap(t6, "feat", 12)

    far_keep, far_send = far_grads(info, mask, (p3, p4, p5, p6), delta)
    b = sum_feat(bpart, (16,))

    def beside_first(keep, send, delta, b, weights):
        got = swap(send, "dp", 1)
        back = local_back(info, mask, delta, weights)
        b, back, got = lax.optimization_barrier((sum_feat(b, (1,)), back, got))
        away = pick(keep, 1 - ylo) + pick(got, 1 - ylo).astype(F32)
        return sum_feat(b, (4,)), back, got, away.astype(BF16)

    b, back, far_near, far_send = beside(
        order, beside_first, far_keep, far_send, delta, b, weights
    )
    r4, r6, dn, b, far_send = lax.optimization_barrier((r4, r6, dn, b, far_send))

    sx, sz, hi = second(info, mask, t3, r4, t5, r6, dn, weights)
    sx, sz, hi, far_send = lax.optimization_barrier((sx, sz, hi, far_send))
    sx, sz, t7 = swap(sx, "feat", 1), swap(sz, "feat", 4), swap(hi, both, 66)
    far_got = swap(far_send, "dp", 2)

    def beside_second(b, x, p7, xn, hn, delta, dn):
        b, dn = lax.optimization_barrier((b, dn))
        b = sum_feat(b, (3,))
        keep, send, v_keep, v_send = near_grads(info, mask, x, p7, xn, hn, delta, dn)
        b, send, v_send = lax.optimization_barrier((b, send, v_send))
        bc = sum_feat(b, (12,)).astype(BF16)
        bc, send, v_send = lax.optimization_barrier((bc, send, v_send))
        got = swap(send, "dp", 1)
        gu_keep, gu_send = grad_u_parts(info, mask, x, bc, v_send)
        gu_send, got = lax.optimization_barrier((gu_send, got))
        gu_got = swap(gu_send, "dp", 1)
        grad_w = assemble(info, mask, keep, got)
        return bc, grad_w, *grad_u_halves(info, mask, gu_keep, gu_got, v_keep)

    bc, grad_w, gu_keep, gu_send, grad_v = beside(order, beside_second, b, x, p7, xn, hn, delta, dn)
    gu_send, sx, sz, t7, far_got = lax.optimization_barrier((gu_send, sx, sz, t7, far_got))
    grad_u = (gu_keep + swap(gu_send, "dp", 2).astype(F32)).astype(BF16)
    grad_x, grad_w = last(
        info, mask, back, [sx, sz, t7], bc, low_u, far_keep, far_near, far_got, grad_w
    )
    return out, grad_x, grad_w, grad_u, grad_v


def solution(mesh):
    return jax.shard_map(
        per_device,
        mesh=mesh,
        in_specs=(
            P("dp", "feat"),
            P(None, "feat", None, None),
            P(),
            P(None, "feat"),
            P("feat", None),
            P(None, "feat"),
            P("dp", "feat"),
        ),
        out_specs=(
            P("dp", "feat"),
            P("dp", "feat"),
            P(None, "feat", "dp", None),
            P(("feat", "dp"), None),
            P(None, ("feat", "dp")),
        ),
        check_vma=False,
    )
```
